512 devices in a mesh: pair: 64 (over x, z), tensor: 8 (over y, core).
Axes of the slice: x: 4, y: 4, z: 16, core: 2. Of those that a mesh axis runs over, the one named last changes fastest.
Arguments:
- rollout: bfloat16 [6144, 4608], P('pair', 'tensor'), may hold values from -6 to 6
- counts: int32 [64, 64], P('pair'), may hold values from 0 to 3, as said below
- lengths: int32 [192], replicated, may hold values from 1 to 32, 3840 in all
- partner_slot: int32 [64, 3], P('pair'), may hold values from 0 to 2, as said below
- pre_gain: float32 [4608], replicated, may hold values from 0.5 to 6
- post_gain: float32 [4608], P('tensor'), may hold values from 0.1 to 1.9
- query_weight: bfloat16 [4608, 2048], P('pair', 'tensor'), may hold values from -0.09375 to 0.09375
- key_weight: bfloat16 [4608, 1024], P('pair', 'tensor'), may hold values from -0.09375 to 0.09375
- value_weight: bfloat16 [4608, 1024], P('pair', 'tensor'), may hold values from -0.09375 to 0.09375
- out_weight: bfloat16 [4608, 2048], P('pair', 'tensor'), may hold values from -0.125 to 0.125
Outputs:
- layer_out: bfloat16 [6144, 4608], P('pair', 'tensor')
The draws below stay inside these ranges and needn't reach their ends.
Inputs may be any that keep to these rules, and one draw needn't show every extreme that they name: `counts`: every source shard sends 96 rows in all and every judge shard receives 96 rows in all. The matching pairs shard d with the shard half the pair axis away; partner_slot on the two shards are inverse permutations, so the partner of a partner is the response itself.
All inputs are finite; a program needn't handle non-finite values.
Results may differ from the reference program's by a relative error of at most 0.013.
Values may be sent and summed in bfloat16 or wider, within the bound.
A program may use at most 64 MiB of HBM per device.

```python
import math
import jax
import jax.numpy as jnp
import numpy as np
from jax import lax

D = 4608
HEADS = 16
KV_HEADS = 8
HD = 128
LEN = 32
RESP_DEV = 3
ROWS_DEV = 96
RESPONSES = 192
TOKENS = 6144
MOST = 3
N_PAIR = 64
N_TENSOR = 8


def draw_counts(key, part):
    key = jax.random.fold_in(key, 11)
    half_pairs = N_PAIR // 2
    key_corner, key_rows, key_columns = jax.random.split(key, 3)
    corner = jax.random.randint(key_corner, (half_pairs, half_pairs), 0, MOST + 1).astype(jnp.int32)
    corner = corner.at[0, 0].set(MOST)
    upper_half = jnp.concatenate((corner, MOST - corner), axis=1)
    lower_half = jnp.concatenate((MOST - corner, corner), axis=1)
    layout = jnp.concatenate((upper_half, lower_half), axis=0)
    layout = layout[jax.random.permutation(key_rows, N_PAIR)]
    layout = layout[:, jax.random.permutation(key_columns, N_PAIR)]
    return layout.astype(jnp.int32)


def draw_partner_slot(key, part):
    key = jax.random.fold_in(key, 12)
    half_pairs = N_PAIR // 2
    orders = jax.vmap(lambda single: jax.random.permutation(single, RESP_DEV))(jax.random.split(key, half_pairs))
    inverse = jnp.argsort(orders, axis=1)
    return jnp.concatenate((orders, inverse), axis=0).astype(jnp.int32)


def draw_pre_gain(key, part):
    key = jax.random.fold_in(key, 13)
    return jnp.exp(jax.random.uniform(key, (D,), jnp.float32, math.log(0.5), math.log(2.0)))


def block_scale(own_key, extent, cuts, least, high):
    def one(axis_at, shards_of):
        steps = jax.random.uniform(jax.random.fold_in(jax.random.fold_in(own_key, 6), axis_at), (shards_of,), jnp.float32, least / len(cuts), high / len(cuts))
        return jnp.repeat(jnp.exp(steps), extent[axis_at] // shards_of).reshape((-1,) + (1,) * (len(extent) - axis_at - 1))

    factor_of = one(*cuts[0])
    for cut in cuts[1:]:
        factor_of = factor_of * one(*cut)
    return factor_of


def split_up(number_of, total, most, lean):
    loads = [(1 << 20) // math.isqrt(standing ** lean) + 1 for standing in range(2, number_of + 1)]
    rest, holding = total - most - (number_of - 1), [1] * (number_of - 1)
    while rest > 0:
        movable = [i for i in range(number_of - 1) if holding[i] < most]
        pool, remaining = sum([loads[i] for i in movable]), rest
        for i in movable:
            addition = min(most - holding[i], max(1, remaining * loads[i] // pool), rest)
            holding[i] = holding[i] + addition
            rest = rest - addition
    return np.array([most] + holding)


def uneven_parts(rng, amount, total, reach, lean):
    if amount == 2:
        one = jax.random.randint(rng, (), max(1, total - reach), min(reach, total - 1) + 1)
        return jnp.stack([one, total - one])
    sizes = jnp.asarray(split_up(amount, total, reach, lean), jnp.int32)
    pairs = (amount - 1) // 2
    donor, sink = sizes[1:1 + 2 * pairs:2], sizes[2:2 + 2 * pairs:2]
    room = jnp.minimum(donor - 1, reach - sink)
    shifted = jax.random.randint(jax.random.fold_in(rng, 1), (pairs,), 0, 1 << 20) % (room + 1)
    sizes = sizes.at[1:1 + 2 * pairs:2].set(donor - shifted).at[2:2 + 2 * pairs:2].set(sink + shifted)
    return sizes[jax.random.permutation(jax.random.fold_in(rng, 2), amount)]


def gaussian(key, dims, deviation, reach, shards=(), kind=jnp.bfloat16):
    drawn = jax.random.normal(key, dims, jnp.float32) * deviation
    if len(shards) > 0:
        drawn = block_scale(key, dims, shards, -0.22, 0.18) * drawn
    return jnp.clip(drawn, min=-reach, max=reach).astype(kind)


def setup_inputs(seed: int = 0) -> dict:
    arg_keys = jax.random.split(jax.random.key(seed), 11)
    return {
        "rollout": gaussian(arg_keys[0], (TOKENS, D), 1.0, 6.0, ((0, 64), (1, 8))),
        "counts": draw_counts(jax.random.fold_in(arg_keys[10], 71), 0),
        "lengths": uneven_parts(arg_keys[2], RESPONSES, RESPONSES * LEN * 5 // 8, LEN, 2).astype(jnp.int32),
        "partner_slot": draw_partner_slot(jax.random.fold_in(arg_keys[10], 71), 0),
        "pre_gain": draw_pre_gain(jax.random.fold_in(arg_keys[10], 71), 0),
        "post_gain": jnp.clip(1.0 + 0.18 * jax.random.normal(arg_keys[5], (D,), jnp.float32), 0.1, 1.9),
        "query_weight": gaussian(arg_keys[6], (D, HEADS * HD), D ** -0.5, 0.09375, ((0, 64), (1, 8))),
        "key_weight": gaussian(arg_keys[7], (D, KV_HEADS * HD), D ** -0.5, 0.09375, ((0, 64), (1, 8))),
        "value_weight": gaussian(arg_keys[8], (D, KV_HEADS * HD), D ** -0.5, 0.09375, ((0, 64), (1, 8))),
        "out_weight": gaussian(arg_keys[9], (D, HEADS * HD), (HEADS * HD) ** -0.5, 0.125, ((0, 64), (1, 8))),
    }


score_scale = 144.0 ** (-0.5)
soft_cap = 50.0
epsilon = 1e-06
negative = -1e+30

def judge_sources(counts):
    counts = counts.astype(jnp.int32)
    offsets = (jnp.cumsum(counts, axis=1) - counts).astype(jnp.int32)
    through = jnp.cumsum(counts, axis=0).astype(jnp.int32)
    before = (through - counts).astype(jnp.int32)
    row_ids = jnp.arange(ROWS_DEV, dtype=jnp.int32)
    source = lax.optimization_barrier(jnp.sum((through[:, :, None] <= row_ids[None, None, :]).astype(jnp.int32), axis=0)).astype(jnp.int32)
    onehot = (jnp.arange(N_PAIR, dtype=jnp.int32)[:, None, None] == source[None, :, :]).astype(jnp.int32)
    shift_rows = lax.optimization_barrier(jnp.sum(onehot * (offsets - before)[:, :, None], axis=0)).astype(jnp.int32)
    return (source * ROWS_DEV + shift_rows + row_ids[None, :]).astype(jnp.int32)

def row_scale(wide):
    return lax.rsqrt(lax.optimization_barrier(jnp.mean(wide * wide, axis=-1, keepdims=True)) + epsilon)

def attend(queries, key_rows, values, partner_keys, partner_values, own_len, far_len):
    responses, length_rows = (queries.shape[0], queries.shape[1])
    keys_all = jnp.concatenate((key_rows, partner_keys), axis=1).astype(jnp.float32)
    values_all = jnp.concatenate((values, partner_values), axis=1).astype(jnp.float32)
    scores = jnp.einsum('rqkgd,rskd->rkgqs', queries.astype(jnp.float32), keys_all) * score_scale
    scores = soft_cap * jnp.tanh(scores / soft_cap)
    key_spot = jnp.arange(2 * length_rows, dtype=jnp.int32)
    query_spot = jnp.arange(length_rows, dtype=jnp.int32)
    own_ok = (key_spot[None, None, :] <= query_spot[None, :, None]) & (key_spot[None, None, :] < own_len[:, None, None])
    far_ok = (key_spot[None, None, :] >= length_rows) & (key_spot[None, None, :] - length_rows < far_len[:, None, None])
    allowed = own_ok | far_ok
    scores = jnp.where(allowed[:, None, None, :, :], scores, negative)
    powers = jnp.exp(scores)
    probs = (powers / lax.optimization_barrier(jnp.sum(powers, axis=-1, keepdims=True))).astype(jnp.bfloat16)
    context = jnp.einsum('rkgqs,rskd->rqkgd', probs.astype(jnp.float32), values_all)
    filled = query_spot[None, :] < own_len[:, None]
    context = jnp.where(filled[:, :, None, None, None], context, 0.0)
    return context.astype(jnp.bfloat16).reshape(responses * length_rows, -1)

def reference(rollout, counts, lengths, partner_slot, pre_gain, post_gain, query_weight, key_weight, value_weight, out_weight):
    judged = jnp.take(rollout, judge_sources(counts).reshape(-1), axis=0)
    x_wide = judged.astype(jnp.float32)
    normed = (x_wide * row_scale(x_wide) * pre_gain).astype(jnp.bfloat16)
    grouped = HEADS // KV_HEADS
    queries = jnp.dot(normed, query_weight, preferred_element_type=jnp.float32).astype(jnp.bfloat16)
    queries = queries.reshape(N_PAIR, RESP_DEV, LEN, KV_HEADS, grouped, HD)
    key_rows = jnp.dot(normed, key_weight, preferred_element_type=jnp.float32).astype(jnp.bfloat16)
    key_rows = key_rows.reshape(N_PAIR, RESP_DEV, LEN, KV_HEADS, HD)
    values = jnp.dot(normed, value_weight, preferred_element_type=jnp.float32).astype(jnp.bfloat16)
    values = values.reshape(N_PAIR, RESP_DEV, LEN, KV_HEADS, HD)
    facing = ((jnp.arange(N_PAIR, dtype=jnp.int32) + N_PAIR // 2) % N_PAIR).astype(jnp.int32)
    chosen = jax.vmap(lambda layout_table, slot_ids: jnp.take(layout_table, slot_ids, axis=0))
    slots = partner_slot.astype(jnp.int32)
    partner_keys = chosen(key_rows[facing], slots)
    partner_values = chosen(values[facing], slots)
    own_len = lengths.astype(jnp.int32).reshape(N_PAIR, RESP_DEV)
    far_len = chosen(own_len[facing], slots)

    def attend_shard(packed):
        return attend(*packed)
    context = lax.map(attend_shard, (queries, key_rows, values, partner_keys, partner_values, own_len, far_len))
    context = context.reshape(TOKENS, HEADS * HD)
    block_width = HEADS * HD // N_TENSOR
    attended = jnp.zeros((TOKENS, D), jnp.float32)
    for tensor_part in range(N_TENSOR):
        low = tensor_part * block_width
        partial_term = jnp.dot(context[:, low:low + block_width], out_weight[:, low:low + block_width].T, preferred_element_type=jnp.float32)
        rounded = lax.optimization_barrier(partial_term.astype(jnp.bfloat16))
        attended = attended + rounded.astype(jnp.float32)
    return (x_wide + attended * row_scale(attended) * post_gain).astype(jnp.bfloat16)
```

```python
import jax
import jax.numpy as jnp
from jax import lax
from jax.experimental import pallas as pl
from jax.experimental.pallas import tpu as pltpu
from jax.sharding import PartitionSpec as P

NX, NY, NZ, NC = 4, 4, 16, 2
NT = NY * NC
HD = 128
LEN = 32
RESP = 3
ROWS = RESP * LEN
FEAT = 576
WIDE = 640
WROWS = 72
BLOCK = NZ * WROWS
CAP = 3
SLOTS = NX * 4
KEPT = NZ * CAP
ALL_SLOTS = NX * KEPT
HALF = ALL_SLOTS // 2

score_scale = 144.0 ** (-0.5)
soft_cap = 50.0
epsilon = 1e-06
negative = -1e30

F32 = jnp.float32
BF16 = jnp.bfloat16
I32 = jnp.int32
MESH = pl.DeviceIdType.MESH
NN = (((1,), (0,)), ((), ()))
NTR = (((1,), (1,)), ((), ()))


def dot(a, b, dims=NN):
    return lax.dot_general(a, b, dims, preferred_element_type=F32)


def iota(shape, dim):
    return lax.broadcasted_iota(I32, shape, dim)


def ones_where(cond):
    return jnp.where(cond, 1.0, 0.0).astype(BF16)


def column_to_row(col):
    rows = col.shape[0]
    same = iota((rows, 128), 0) == iota((rows, 128), 1)
    return jnp.sum(jnp.where(same, col, 0.0), axis=0, keepdims=True)


def row_to_column(row, rows):
    same = iota((rows, 128), 0) == iota((rows, 128), 1)
    return jnp.sum(jnp.where(same, row, 0.0), axis=1, keepdims=True)


def kernel(
    roll, counts, lens, pslot, gain, post, wq, wk, wv, wo, out,
    xin, zsend, zrecv, wsend, wbuf, w32, slot_out, slot_in, xg, xs, judged, sq_in, fin_in,
    part, part_in, far_in, ctx, co_out, co_in, xo_out, xo_in,
    tr_s, tr_r, za_s, za_r, ring_s, ring_r, xg_s, xg_r, cs_s, cs_r, sq_s, sq_r,
    rs_s, rs_r, far_s, far_r, cx_s, cx_r, co_s, co_r, xo_s, xo_r, fn_s, fn_r,
):
    pair = lax.axis_index("pair")
    ten = lax.axis_index("tensor")
    x, z = pair // NZ, pair % NZ
    y, c = ten // NC, ten % NC

    def dev(xx, zz, yy, cc):
        return {"pair": xx * NZ + zz, "tensor": yy * NC + cc}

    def remote(src, dst, send, recv, where):
        return pltpu.make_async_remote_copy(
            src_ref=src, dst_ref=dst, send_sem=send, recv_sem=recv,
            device_id=where, device_id_type=MESH,
        )

    off_diagonal = x != y

    barrier = pltpu.get_barrier_semaphore()

    def greet(where):
        pl.semaphore_signal(barrier, inc=1, device_id=where, device_id_type=MESH)

    @pl.loop(1, NZ)
    def _(k):
        greet(dev(x, (z + k) % NZ, y, c))

    @pl.loop(1, NX)
    def _(k):
        greet(dev((x + k) % NX, z, y, c))

    @pl.loop(1, NT)
    def _(k):
        greet({"pair": pair, "tensor": (ten + k) % NT})

    @pl.when(off_diagonal)
    def _():
        greet(dev(y, z, x, c))

    def pack(p, first, second):
        wsend[p] = jnp.concatenate(
            (first.astype(F32), second.astype(F32)), axis=0
        ).astype(BF16)

    pack(0, wq[:, :HD], wq[:, HD:])
    pack(1, wk[...], wv[...])
    pack(2, wo[:, :HD], wo[:, HD:])
    lane = iota((8, 128), 1)
    spread = jnp.zeros((8, 128), I32)
    for k in range(RESP):
        spread = jnp.where(lane == k, pslot[0:1, k:k + 1], spread)
    slot_out[...] = spread

    xin[...] = jnp.ones((ROWS, WIDE), BF16)
    xin[:, :FEAT] = roll[...]
    slots = NZ * SLOTS
    j = iota((slots, NX * NZ), 0)
    dest = ((j >> 2) & (NX - 1)) * NZ + (j >> 4)
    other = iota((slots, NX * NZ), 1)
    sending = counts[...].astype(F32)
    start = jnp.sum(jnp.where(other < dest, sending, 0.0), axis=1, keepdims=True)
    amount = jnp.sum(jnp.where(other == dest, sending, 0.0), axis=1, keepdims=True)
    k_slot = (iota((slots, 1), 0) & 3).astype(F32)
    wanted = jnp.where((k_slot < amount) & (k_slot < CAP), start + k_slot, -1.0)
    pick = ones_where(wanted == iota((slots, ROWS), 1).astype(F32))
    zsend[...] = dot(pick, xin[...]).astype(BF16).reshape(NZ, SLOTS, WIDE)
    zrecv[z] = zsend[z]

    greeted = NZ - 1 + NX - 1 + NT - 1

    @pl.when(off_diagonal)
    def _():
        pl.semaphore_wait(barrier, greeted + 1)

    @pl.when(jnp.logical_not(off_diagonal))
    def _():
        pl.semaphore_wait(barrier, greeted)

    def z_out(k):
        t = (z + k) % NZ
        return remote(zsend.at[t], zrecv.at[z], za_s.at[k], za_r.at[k], dev(x, t, y, c))

    def z_in(k):
        f = (z + NZ - k) % NZ
        return remote(zsend.at[f], zrecv.at[f], za_s.at[k], za_r.at[k], dev(x, f, y, c))

    def turned(first):
        if first:
            return remote(wsend, wbuf.at[z], tr_s.at[0], tr_r.at[0], dev(y, z, x, c))
        return remote(slot_out, slot_in, tr_s.at[1], tr_r.at[1], dev(y, z, x, c))

    @pl.when(off_diagonal)
    def _():
        turned(True).start()
        turned(False).start()

    @pl.loop(1, NZ)
    def _(k):
        z_out(k).start()

    @pl.when(jnp.logical_not(off_diagonal))
    def _():
        wbuf[z] = wsend[...]
        slot_in[...] = slot_out[...]

    up, down = (z + 1) % NZ, (z + NZ - 1) % NZ

    def ring_block(d, s):
        return (z + NZ - s) % NZ if d == 0 else (z + s) % NZ

    def ring(p, d, s, distance):
        block = wbuf.at[ring_block(d, distance), p]
        return remote(
            block, block, ring_s.at[p, d, s], ring_r.at[p, d, s],
            dev(x, up if d == 0 else down, y, c),
        )

    def unpack(p, block):
        v = wbuf[block, p].astype(F32)
        at = pl.ds(pl.multiple_of(block * WROWS, 8), WROWS)
        w32[p, at, 0:HD] = v[:WROWS]
        w32[p, at, HD:2 * HD] = v[WROWS:]

    def ring_open(p):
        ring(p, 0, 0, 0).start()
        ring(p, 1, 0, 0).start()
        unpack(p, z)

    def ring_steps(pieces, low, high):
        @pl.loop(low, high)
        def _(s):
            for p in pieces:
                for d in (0, 1):
                    ring(p, d, s - 1, s).wait_recv()
                    ring(p, d, s, s).start()
            for p in pieces:
                for d in (0, 1):
                    unpack(p, ring_block(d, s))

    def ring_close(pieces):
        last = NZ // 2
        for p in pieces:
            for d in (0, 1):
                ring(p, d, last - 2, last - 1).wait_recv()
            ring(p, 0, last - 1, last - 1).start()
        for p in pieces:
            for d in (0, 1):
                unpack(p, ring_block(d, last - 1))
        for p in pieces:
            ring(p, 0, last - 1, last).wait_recv()
            unpack(p, ring_block(0, last))

    @pl.when(off_diagonal)
    def _():
        turned(True).wait_recv()
        turned(False).wait_recv()

    ring_open(0)
    ring_open(1)
    ring_steps((0, 1), 1, 3)

    @pl.loop(1, NZ)
    def _(k):
        z_in(k).wait_recv()

    i = iota((ALL_SLOTS, slots), 0)
    q = (i * 171) >> 9
    held_at = (q & (NZ - 1)) * SLOTS + (q >> 4) * 4 + (i - 3 * q)
    squeeze = ones_where(held_at == iota((ALL_SLOTS, slots), 1))
    xg[x] = dot(squeeze, zrecv[...].reshape(slots, WIDE)).astype(BF16)

    right, left = (x + 1) % NX, (x + NX - 1) % NX
    parts = (pl.ds(0, HALF), pl.ds(HALF, HALF))
    plan = (
        (0, 0, 1), (0, 1, 1), (1, 1, 1), (1, 0, 1), (0, 0, 2), (1, 1, 2),
    )

    def x_block(d, distance):
        return (x + NX - distance) % NX if d == 0 else (x + distance) % NX

    def x_out(n):
        d, half, distance = plan[n]
        block = xg.at[x_block(d, distance - 1), parts[half]]
        return remote(
            block, block, xg_s.at[n], xg_r.at[n],
            dev(right if d == 0 else left, z, y, c),
        )

    def x_in(n):
        d, half, distance = plan[n]
        block = xg.at[x_block(d, distance), parts[half]]
        return remote(
            block, block, xg_s.at[n], xg_r.at[n],
            dev(right if d == 0 else left, z, y, c),
        )

    for n in (0, 2, 1, 3):
        x_out(n).start()
    x_in(0).wait_recv()
    x_out(4).start()
    x_in(2).wait_recv()
    x_out(5).start()
    ring_steps((0, 1), 3, 5)
    for n in (1, 3, 4, 5):
        x_in(n).wait_recv()

    before = ones_where(iota((ALL_SLOTS, ALL_SLOTS), 0) < iota((ALL_SLOTS, ALL_SLOTS), 1))
    flag_lane = ones_where(iota((16, 128), 1) == FEAT - 512)
    my_gain = gain[pl.ds(ten, 1), :]
    table = jnp.zeros((8, 128), F32)
    sub = iota((8, 128), 0)

    def share(dx):
        return remote(
            xs.at[c, dx], xs.at[c, dx], cs_s.at[dx], cs_r.at[dx], dev(x, z, y, 1 - c)
        )

    def share_in(dx):
        return remote(
            xs.at[1 - c, dx], xs.at[1 - c, dx], cs_s.at[dx], cs_r.at[dx], dev(x, z, y, 1 - c)
        )

    for dx in range(NX):
        s = xg[:, dx * KEPT:(dx + 1) * KEPT, :].reshape(ALL_SLOTS, WIDE)
        filled = dot(flag_lane, s[:, 512:WIDE], NTR)
        rank = dot(filled.astype(BF16), before)
        key = jnp.where(filled > 0.5, rank, -1.0)[0:1]
        place = ones_where(iota((ROWS, ALL_SLOTS), 0).astype(F32) == key)
        rows = dot(place, s)[:, :FEAT]
        judged[dx] = rows.astype(BF16)
        xs[c, dx] = (rows * my_gain).astype(BF16)
        share(dx).start()
        squares = column_to_row(jnp.sum(rows * rows, axis=1, keepdims=True))
        table = jnp.where(sub == dx, squares, table)

    sq_in[0] = table

    def squares_out(k):
        return remote(
            sq_in.at[0], sq_in.at[k], sq_s.at[k], sq_r.at[k],
            {"pair": pair, "tensor": (ten + k) % NT},
        )

    @pl.loop(1, NT)
    def _(k):
        squares_out(k).start()

    ring_steps((0, 1), 5, NZ // 2 - 1)
    ring_close((0, 1))
    ring_open(2)
    for dx in range(NX):
        share_in(dx).wait_recv()

    first = xs[0].reshape(NX * ROWS, FEAT)
    second = xs[1].reshape(NX * ROWS, FEAT)
    for p in (0, 1):
        w = w32[p].astype(BF16)
        t = dot(first, w[:FEAT]) + dot(second, w[FEAT:])
        part[:, :, p * 256:(p + 1) * 256] = t.astype(BF16).reshape(NX, ROWS, 256)

    def sum_out(k):
        t = (y + k) % NY
        return remote(part.at[t], part_in.at[k], rs_s.at[k], rs_r.at[k], dev(x, z, t, c))

    def far_out(k):
        t = (y + k) % NY
        return remote(
            part.at[(t + NY // 2) % NY, :, pl.ds(256, 256)], far_in.at[k],
            far_s.at[k], far_r.at[k], dev(x, z, t, c),
        )

    for k in (2, 1, 3):
        sum_out(k).start()
        far_out(k).start()

    ring_steps((2,), 1, 4)

    @pl.loop(1, NT)
    def _(k):
        squares_out(k).wait_recv()

    total = sq_in[0]
    for k in range(1, NT):
        total = total + sq_in[k]
    far_y = (y + NY // 2) % NY
    width = float(NT * FEAT)

    def row_scale(which):
        row = jnp.sum(jnp.where(sub == which, total, 0.0), axis=0, keepdims=True)
        return lax.rsqrt(row_to_column(row, ROWS) / width + epsilon)

    scale_own, scale_far = row_scale(y), row_scale(far_y)
    for k in range(1, NY):
        sum_out(k).wait_recv()
        far_out(k).wait_recv()
    own = part[y].astype(F32)
    far = part[far_y, :, 256:512].astype(F32)
    for k in range(1, NY):
        own = own + part_in[k].astype(F32)
        far = far + far_in[k].astype(F32)
    own = (own * scale_own).astype(BF16)
    far = (far * scale_far).astype(BF16)

    queries = jnp.concatenate((own[:, 0:HD], own[:, HD:2 * HD]), axis=0)
    col = iota((2 * ROWS, ROWS), 1)
    row = iota((2 * ROWS, ROWS), 0)
    row = jnp.where(row >= ROWS, row - ROWS, row)
    resp_q, resp_k = row >> 5, col >> 5
    spot_q, spot_k = row & (LEN - 1), col & (LEN - 1)

    def by_response(resp, values):
        return jnp.where(resp == 0, values[0], jnp.where(resp == 1, values[1], values[2]))

    own_lens = [lens[(y * NZ + z) * RESP + k] for k in range(RESP)]
    far_lens = [lens[(far_y * NZ + z) * RESP + k] for k in range(RESP)]
    partner = by_response(resp_q, [slot_in[0:1, k:k + 1] for k in range(RESP)])
    own_ok = (resp_q == resp_k) & (spot_k <= spot_q) & (spot_k < by_response(resp_k, own_lens))
    far_ok = (partner == resp_k) & (spot_k < by_response(resp_k, far_lens))

    def powers(keys, ok):
        scores = dot(queries, keys, NTR) * score_scale
        scores = soft_cap * jnp.tanh(scores / soft_cap)
        return jnp.exp(jnp.where(ok, scores, negative))

    p_own = powers(own[:, 256:384], own_ok)
    p_far = powers(far[:, 0:HD], far_ok)
    whole = jnp.sum(p_own, axis=1, keepdims=True) + jnp.sum(p_far, axis=1, keepdims=True)
    mixed = dot((p_own / whole).astype(BF16), own[:, 384:512])
    mixed = mixed + dot((p_far / whole).astype(BF16), far[:, HD:2 * HD])
    row = iota((2 * ROWS, HD), 0)
    row = jnp.where(row >= ROWS, row - ROWS, row)
    present = (row & (LEN - 1)) < by_response(row >> 5, own_lens)
    mixed = jnp.where(present, mixed, 0.0).astype(BF16)
    ctx[y] = jnp.concatenate((mixed[:ROWS], mixed[ROWS:]), axis=1)

    def ctx_out(k):
        return remote(ctx.at[y], ctx.at[y], cx_s.at[k], cx_r.at[k], dev(x, z, (y + k) % NY, c))

    def ctx_in(k):
        f = (y + NY - k) % NY
        return remote(ctx.at[f], ctx.at[f], cx_s.at[k], cx_r.at[k], dev(x, z, f, c))

    for k in (2, 1, 3):
        ctx_out(k).start()
    ring_steps((2,), 4, NZ // 2 - 1)
    ring_close((2,))
    for k in range(1, NY):
        ctx_in(k).wait_recv()

    context = ctx[...].reshape(NX * ROWS, 2 * HD)

    def project(half):
        w = w32[2, pl.ds(pl.multiple_of(half * FEAT, 8), FEAT), :].astype(BF16)
        return dot(context, w, NTR).astype(BF16).reshape(NX, ROWS, FEAT)

    co_out[...] = project(1 - c)
    swap = remote(co_out, co_in, co_s.at[0], co_r.at[0], dev(x, z, y, 1 - c))
    swap.start()
    mine = project(c).astype(F32)
    swap.wait_recv()
    xo_out[...] = (mine + co_in[...].astype(F32)).astype(BF16)

    def xsum_out(k):
        t = (x + k) % NX
        return remote(xo_out.at[t], xo_in.at[k], xo_s.at[k], xo_r.at[k], dev(t, z, y, c))

    for k in (2, 1, 3):
        xsum_out(k).start()
    attended = xo_out[x].astype(F32)
    for k in (1, 3, 2):
        xsum_out(k).wait_recv()
        attended = attended + xo_in[k].astype(F32)

    squares = column_to_row(jnp.sum(attended * attended, axis=1, keepdims=True))
    fin_in[0] = jnp.where(sub == 0, squares, 0.0)

    def fin_out(k):
        return remote(
            fin_in.at[0], fin_in.at[k], fn_s.at[k], fn_r.at[k],
            {"pair": pair, "tensor": (ten + k) % NT},
        )

    @pl.loop(1, NT)
    def _(k):
        fin_out(k).start()

    @pl.when(off_diagonal)
    def _():
        turned(True).wait_send()
        turned(False).wait_send()

    @pl.loop(1, NZ)
    def _(k):
        z_out(k).wait_send()

    for p in range(3):
        @pl.loop(0, NZ // 2 - 1)
        def _(s):
            ring(p, 0, s, s).wait_send()
            ring(p, 1, s, s).wait_send()

        ring(p, 0, NZ // 2 - 1, NZ // 2 - 1).wait_send()
    for n in range(6):
        x_out(n).wait_send()
    for dx in range(NX):
        share(dx).wait_send()

    @pl.loop(1, NT)
    def _(k):
        squares_out(k).wait_send()

    for k in range(1, NY):
        sum_out(k).wait_send()
        far_out(k).wait_send()
        ctx_out(k).wait_send()
        xsum_out(k).wait_send()
    swap.wait_send()

    residual = judged[x].astype(F32)
    gained = attended * post[...]

    @pl.loop(1, NT)
    def _(k):
        fin_out(k).wait_recv()

    total = fin_in[0]
    for k in range(1, NT):
        total = total + fin_in[k]
    scale = lax.rsqrt(row_to_column(total[0:1], ROWS) / width + epsilon)
    out[...] = (residual + gained * scale).astype(BF16)

    @pl.loop(1, NT)
    def _(k):
        fin_out(k).wait_send()


def shards(
    rollout, counts, lengths, partner_slot, pre_gain, post_gain,
    query_weight, key_weight, value_weight, out_weight,
):
    vmem = pl.BlockSpec(memory_space=pltpu.VMEM)
    smem = pl.BlockSpec(memory_space=pltpu.SMEM)
    dma = pltpu.SemaphoreType.DMA
    scratch = [
        pltpu.VMEM((ROWS, WIDE), BF16),
        pltpu.VMEM((NZ, SLOTS, WIDE), BF16),
        pltpu.VMEM((NZ, SLOTS, WIDE), BF16),
        pltpu.VMEM((3, 2 * WROWS, HD), BF16),
        pltpu.VMEM((NZ, 3, 2 * WROWS, HD), BF16),
        pltpu.VMEM((3, BLOCK, 2 * HD), F32),
        pltpu.VMEM((8, 128), I32),
        pltpu.VMEM((8, 128), I32),
        pltpu.VMEM((NX, ALL_SLOTS, WIDE), BF16),
        pltpu.VMEM((NC, NX, ROWS, FEAT), BF16),
        pltpu.VMEM((NX, ROWS, FEAT), BF16),
        pltpu.VMEM((NT, 8, 128), F32),
        pltpu.VMEM((NT, 8, 128), F32),
        pltpu.VMEM((NX, ROWS, 512), BF16),
        pltpu.VMEM((NY, ROWS, 512), BF16),
        pltpu.VMEM((NY, ROWS, 256), BF16),
        pltpu.VMEM((NY, ROWS, 256), BF16),
        pltpu.VMEM((NX, ROWS, FEAT), BF16),
        pltpu.VMEM((NX, ROWS, FEAT), BF16),
        pltpu.VMEM((NX, ROWS, FEAT), BF16),
        pltpu.VMEM((NX, ROWS, FEAT), BF16),
        dma((2,)), dma((2,)),
        dma((NZ,)), dma((NZ,)),
        dma((3, 2, NZ // 2)), dma((3, 2, NZ // 2)),
        dma((6,)), dma((6,)),
        dma((NX,)), dma((NX,)),
        dma((NT,)), dma((NT,)),
        dma((NY,)), dma((NY,)),
        dma((NY,)), dma((NY,)),
        dma((NY,)), dma((NY,)),
        dma((1,)), dma((1,)),
        dma((NX,)), dma((NX,)),
        dma((NT,)), dma((NT,)),
    ]
    return pl.pallas_call(
        kernel,
        out_shape=jax.ShapeDtypeStruct((ROWS, FEAT), BF16),
        in_specs=[vmem, vmem, smem] + [vmem] * 7,
        out_specs=vmem,
        scratch_shapes=scratch,
        compiler_params=pltpu.CompilerParams(
            collective_id=0, has_side_effects=True, vmem_limit_bytes=40 * 1024 * 1024
        ),
    )(
        rollout, counts, lengths, partner_slot, pre_gain.reshape(NT, FEAT),
        post_gain.reshape(1, FEAT), query_weight, key_weight, value_weight, out_weight,
    )


def solution(mesh):
    placed = (
        P("pair", "tensor"),
        P("pair", None),
        P(),
        P("pair", None),
        P(),
        P("tensor"),
        P("pair", "tensor"),
        P("pair", "tensor"),
        P("pair", "tensor"),
        P("pair", "tensor"),
    )
    return jax.shard_map(
        shards, mesh=mesh, in_specs=placed, out_specs=P("pair", "tensor"), check_vma=False
    )
```

```python
import jax
import jax.numpy as jnp
from jax import lax
from jax.experimental import pallas as pl
from jax.experimental.pallas import tpu as pltpu
from jax.sharding import PartitionSpec as P

NX, NY, NZ, NC = 4, 4, 16, 2
NT = NY * NC
HD = 128
LEN = 32
RESP = 3
ROWS = RESP * LEN
FEAT = 576
WIDE = 640
WROWS = 72
BLOCK = NZ * WROWS
CAP = 3
SLOTS = NX * 4
KEPT = NZ * CAP
ALL_SLOTS = NX * KEPT
HALF = ALL_SLOTS // 2

score_scale = 144.0 ** (-0.5)
soft_cap = 50.0
epsilon = 1e-06
negative = -1e30

F32 = jnp.float32
BF16 = jnp.bfloat16
I32 = jnp.int32
MESH = pl.DeviceIdType.MESH
NN = (((1,), (0,)), ((), ()))
NTR = (((1,), (1,)), ((), ()))


def dot(a, b, dims=NN):
    return lax.dot_general(a, b, dims, preferred_element_type=F32)


def iota(shape, dim):
    return lax.broadcasted_iota(I32, shape, dim)


def ones_where(cond):
    return jnp.where(cond, 1.0, 0.0).astype(BF16)


def column_to_row(col):
    rows = col.shape[0]
    same = iota((rows, 128), 0) == iota((rows, 128), 1)
    return jnp.sum(jnp.where(same, col, 0.0), axis=0, keepdims=True)


def row_to_column(row, rows):
    same = iota((rows, 128), 0) == iota((rows, 128), 1)
    return jnp.sum(jnp.where(same, row, 0.0), axis=1, keepdims=True)


def kernel(
    roll_h, counts, lens, pslot, gain, post, wq_h, wk_h, wv_h, wo_h, out,
    roll, wq, wk, wv, wo, in_s, xin, zsend, zrecv, wsend, wbuf, w32, slot_out, slot_in, xg, xs, judged, sq_in, fin_in,
    part, part_in, far_in, ctx, co_out, co_in, xo_out, xo_in,
    tr_s, tr_r, za_s, za_r, ring_s, ring_r, xg_s, xg_r, cs_s, cs_r, sq_s, sq_r,
    rs_s, rs_r, far_s, far_r, cx_s, cx_r, co_s, co_r, xo_s, xo_r, fn_s, fn_r,
):
    pair = lax.axis_index("pair")
    ten = lax.axis_index("tensor")
    x, z = pair // NZ, pair % NZ
    y, c = ten // NC, ten % NC

    def dev(xx, zz, yy, cc):
        return {"pair": xx * NZ + zz, "tensor": yy * NC + cc}

    def remote(src, dst, send, recv, where):
        return pltpu.make_async_remote_copy(
            src_ref=src, dst_ref=dst, send_sem=send, recv_sem=recv,
            device_id=where, device_id_type=MESH,
        )

    off_diagonal = x != y

    loads = [
        pltpu.make_async_copy(a, b, in_s.at[n])
        for n, (a, b) in enumerate(
            ((roll_h, roll), (wq_h, wq), (wk_h, wk), (wv_h, wv), (wo_h, wo))
        )
    ]
    for load in loads:
        load.start()

    barrier = pltpu.get_barrier_semaphore()

    def greet(where):
        pl.semaphore_signal(barrier, inc=1, device_id=where, device_id_type=MESH)

    @pl.loop(1, NZ)
    def _(k):
        greet(dev(x, (z + k) % NZ, y, c))

    @pl.loop(1, NX)
    def _(k):
        greet(dev((x + k) % NX, z, y, c))

    @pl.loop(1, NT)
    def _(k):
        greet({"pair": pair, "tensor": (ten + k) % NT})

    @pl.when(off_diagonal)
    def _():
        greet(dev(y, z, x, c))

    for load in loads:
        load.wait()

    def pack(p, first, second):
        wsend[p] = jnp.concatenate(
            (first.astype(F32), second.astype(F32)), axis=0
        ).astype(BF16)

    pack(0, wq[:, :HD], wq[:, HD:])
    pack(1, wk[...], wv[...])
    pack(2, wo[:, :HD], wo[:, HD:])
    lane = iota((8, 128), 1)
    spread = jnp.zeros((8, 128), I32)
    for k in range(RESP):
        spread = jnp.where(lane == k, pslot[0:1, k:k + 1], spread)
    slot_out[...] = spread

    xin[...] = jnp.ones((ROWS, WIDE), BF16)
    xin[:, :FEAT] = roll[...]
    slots = NZ * SLOTS
    j = iota((slots, NX * NZ), 0)
    dest = ((j >> 2) & (NX - 1)) * NZ + (j >> 4)
    other = iota((slots, NX * NZ), 1)
    sending = counts[...].astype(F32)
    start = jnp.sum(jnp.where(other < dest, sending, 0.0), axis=1, keepdims=True)
    amount = jnp.sum(jnp.where(other == dest, sending, 0.0), axis=1, keepdims=True)
    k_slot = (iota((slots, 1), 0) & 3).astype(F32)
    wanted = jnp.where((k_slot < amount) & (k_slot < CAP), start + k_slot, -1.0)
    pick = ones_where(wanted == iota((slots, ROWS), 1).astype(F32))
    zsend[...] = dot(pick, xin[...]).astype(BF16).reshape(NZ, SLOTS, WIDE)
    zrecv[z] = zsend[z]

    greeted = NZ - 1 + NX - 1 + NT - 1

    @pl.when(off_diagonal)
    def _():
        pl.semaphore_wait(barrier, greeted + 1)

    @pl.when(jnp.logical_not(off_diagonal))
    def _():
        pl.semaphore_wait(barrier, greeted)

    def z_out(k):
        t = (z + k) % NZ
        return remote(zsend.at[t], zrecv.at[z], za_s.at[k], za_r.at[k], dev(x, t, y, c))

    def z_in(k):
        f = (z + NZ - k) % NZ
        return remote(zsend.at[f], zrecv.at[f], za_s.at[k], za_r.at[k], dev(x, f, y, c))

    def turned(first):
        if first:
            return remote(wsend, wbuf.at[z], tr_s.at[0], tr_r.at[0], dev(y, z, x, c))
        return remote(slot_out, slot_in, tr_s.at[1], tr_r.at[1], dev(y, z, x, c))

    @pl.when(off_diagonal)
    def _():
        turned(True).start()
        turned(False).start()

    z_out(NZ // 2).start()

    @pl.loop(1, NZ // 2)
    def _(k):
        z_out(NZ // 2 - k).start()
        z_out(NZ // 2 + k).start()

    @pl.when(jnp.logical_not(off_diagonal))
    def _():
        wbuf[z] = wsend[...]
        slot_in[...] = slot_out[...]

    up, down = (z + 1) % NZ, (z + NZ - 1) % NZ

    def ring_block(d, s):
        return (z + NZ - s) % NZ if d == 0 else (z + s) % NZ

    def ring(p, d, s, distance):
        block = wbuf.at[ring_block(d, distance), p]
        return remote(
            block, block, ring_s.at[p, d, s], ring_r.at[p, d, s],
            dev(x, up if d == 0 else down, y, c),
        )

    def unpack(p, block):
        v = wbuf[block, p].astype(F32)
        at = pl.ds(pl.multiple_of(block * WROWS, 8), WROWS)
        w32[p, at, 0:HD] = v[:WROWS]
        w32[p, at, HD:2 * HD] = v[WROWS:]

    def ring_open(p):
        ring(p, 0, 0, 0).start()
        ring(p, 1, 0, 0).start()
        unpack(p, z)

    def ring_steps(pieces, low, high):
        @pl.loop(low, high)
        def _(s):
            for p in pieces:
                for d in (0, 1):
                    ring(p, d, s - 1, s).wait_recv()
                    ring(p, d, s, s).start()
            for p in pieces:
                for d in (0, 1):
                    unpack(p, ring_block(d, s))

    last = NZ // 2

    def ring_last_sends(pieces):
        for p in pieces:
            for d in (0, 1):
                ring(p, d, last - 2, last - 1).wait_recv()
            ring(p, 0, last - 1, last - 1).start()
        for p in pieces:
            for d in (0, 1):
                unpack(p, ring_block(d, last - 1))

    def ring_close(pieces):
        for p in pieces:
            ring(p, 0, last - 1, last).wait_recv()
            unpack(p, ring_block(0, last))

    @pl.when(off_diagonal)
    def _():
        turned(True).wait_recv()
        turned(False).wait_recv()

    early, late = (0, 1), (2,)
    for p in early:
        ring_open(p)
    ring_steps(early, 1, 3)

    @pl.loop(1, NZ)
    def _(k):
        z_in(k).wait_recv()

    i = iota((ALL_SLOTS, slots), 0)
    q = (i * 171) >> 9
    held_at = (q & (NZ - 1)) * SLOTS + (q >> 4) * 4 + (i - 3 * q)
    squeeze = ones_where(held_at == iota((ALL_SLOTS, slots), 1))
    xg[x] = dot(squeeze, zrecv[...].reshape(slots, WIDE)).astype(BF16)

    right, left = (x + 1) % NX, (x + NX - 1) % NX
    parts = (pl.ds(0, HALF), pl.ds(HALF, HALF))
    plan = (
        (0, 0, 1), (0, 1, 1), (1, 1, 1), (1, 0, 1), (0, 0, 2), (1, 1, 2),
    )

    def x_block(d, distance):
        return (x + NX - distance) % NX if d == 0 else (x + distance) % NX

    def x_out(n):
        d, half, distance = plan[n]
        block = xg.at[x_block(d, distance - 1), parts[half]]
        return remote(
            block, block, xg_s.at[n], xg_r.at[n],
            dev(right if d == 0 else left, z, y, c),
        )

    def x_in(n):
        d, half, distance = plan[n]
        block = xg.at[x_block(d, distance), parts[half]]
        return remote(
            block, block, xg_s.at[n], xg_r.at[n],
            dev(right if d == 0 else left, z, y, c),
        )

    for n in (0, 2, 1, 3):
        x_out(n).start()
    ring_steps(early, 3, 4)
    x_in(0).wait_recv()
    x_out(4).start()
    x_in(2).wait_recv()
    x_out(5).start()
    ring_steps(early, 4, 6)
    ring_open(2)
    for n in (1, 3, 4, 5):
        x_in(n).wait_recv()

    before = ones_where(iota((ALL_SLOTS, ALL_SLOTS), 0) < iota((ALL_SLOTS, ALL_SLOTS), 1))
    flag_lane = ones_where(iota((16, 128), 1) == FEAT - 512)
    my_gain = gain[pl.ds(pl.multiple_of(y * NC * FEAT, 128), NC * FEAT)].reshape(1, NC * FEAT)
    my_gain = jnp.where(c == 0, my_gain[:, :FEAT], my_gain[:, FEAT:])
    table = jnp.zeros((8, 128), F32)
    sub = iota((8, 128), 0)

    def share(dx):
        return remote(
            xs.at[c, dx], xs.at[c, dx], cs_s.at[dx], cs_r.at[dx], dev(x, z, y, 1 - c)
        )

    def share_in(dx):
        return remote(
            xs.at[1 - c, dx], xs.at[1 - c, dx], cs_s.at[dx], cs_r.at[dx], dev(x, z, y, 1 - c)
        )

    for dx in range(NX):
        s = xg[:, dx * KEPT:(dx + 1) * KEPT, :].reshape(ALL_SLOTS, WIDE)
        filled = dot(flag_lane, s[:, 512:WIDE], NTR)
        rank = dot(filled.astype(BF16), before)
        key = jnp.where(filled > 0.5, rank, -1.0)[0:1]
        place = ones_where(iota((ROWS, ALL_SLOTS), 0).astype(F32) == key)
        rows = dot(place, s)[:, :FEAT]
        judged[dx] = rows.astype(BF16)
        xs[c, dx] = (rows * my_gain).astype(BF16)
        share(dx).start()
        squares = column_to_row(jnp.sum(rows * rows, axis=1, keepdims=True))
        table = jnp.where(sub == dx, squares, table)

    sq_in[0] = table

    def squares_out(k):
        return remote(
            sq_in.at[0], sq_in.at[k], sq_s.at[k], sq_r.at[k],
            {"pair": pair, "tensor": (ten + k) % NT},
        )

    @pl.loop(1, NT)
    def _(k):
        squares_out(k).start()

    ring_steps(early, 6, last - 1)
    ring_steps(late, 1, 2)
    ring_last_sends(early)
    ring_steps(late, 2, 3)
    ring_close(early)
    for dx in range(NX):
        share_in(dx).wait_recv()

    first = xs[0].reshape(NX * ROWS, FEAT)
    second = xs[1].reshape(NX * ROWS, FEAT)
    for p in (0, 1):
        w = w32[p].astype(BF16)
        t = dot(first, w[:FEAT]) + dot(second, w[FEAT:])
        part[:, :, p * 256:(p + 1) * 256] = t.astype(BF16).reshape(NX, ROWS, 256)

    def sum_out(k):
        t = (y + k) % NY
        return remote(part.at[t], part_in.at[k], rs_s.at[k], rs_r.at[k], dev(x, z, t, c))

    def far_out(k):
        t = (y + k) % NY
        return remote(
            part.at[(t + NY // 2) % NY, :, pl.ds(256, 256)], far_in.at[k],
            far_s.at[k], far_r.at[k], dev(x, z, t, c),
        )

    for k in (2, 1, 3):
        sum_out(k).start()
        far_out(k).start()

    ring_steps(late, 3, 6)

    @pl.loop(1, NT)
    def _(k):
        squares_out(k).wait_recv()

    total = sq_in[0]
    for k in range(1, NT):
        total = total + sq_in[k]
    far_y = (y + NY // 2) % NY
    width = float(NT * FEAT)

    def row_scale(which):
        row = jnp.sum(jnp.where(sub == which, total, 0.0), axis=0, keepdims=True)
        return lax.rsqrt(row_to_column(row, ROWS) / width + epsilon)

    scale_own, scale_far = row_scale(y), row_scale(far_y)
    for k in range(1, NY):
        sum_out(k).wait_recv()
        far_out(k).wait_recv()
    own = part[y].astype(F32)
    far = part[far_y, :, 256:512].astype(F32)
    for k in range(1, NY):
        own = own + part_in[k].astype(F32)
        far = far + far_in[k].astype(F32)
    own = (own * scale_own).astype(BF16)
    far = (far * scale_far).astype(BF16)

    queries = jnp.concatenate((own[:, 0:HD], own[:, HD:2 * HD]), axis=0)
    col = iota((2 * ROWS, ROWS), 1)
    row = iota((2 * ROWS, ROWS), 0)
    row = jnp.where(row >= ROWS, row - ROWS, row)
    resp_q, resp_k = row >> 5, col >> 5
    spot_q, spot_k = row & (LEN - 1), col & (LEN - 1)

    def by_response(resp, values):
        return jnp.where(resp == 0, values[0], jnp.where(resp == 1, values[1], values[2]))

    own_lens = [lens[(y * NZ + z) * RESP + k] for k in range(RESP)]
    far_lens = [lens[(far_y * NZ + z) * RESP + k] for k in range(RESP)]
    partner = by_response(resp_q, [slot_in[0:1, k:k + 1] for k in range(RESP)])
    own_ok = (resp_q == resp_k) & (spot_k <= spot_q) & (spot_k < by_response(resp_k, own_lens))
    far_ok = (partner == resp_k) & (spot_k < by_response(resp_k, far_lens))

    def powers(keys, ok):
        scores = dot(queries, keys, NTR) * score_scale
        scores = soft_cap * jnp.tanh(scores / soft_cap)
        return jnp.exp(jnp.where(ok, scores, negative))

    p_own = powers(own[:, 256:384], own_ok)
    p_far = powers(far[:, 0:HD], far_ok)
    whole = jnp.sum(p_own, axis=1, keepdims=True) + jnp.sum(p_far, axis=1, keepdims=True)
    mixed = dot((p_own / whole).astype(BF16), own[:, 384:512])
    mixed = mixed + dot((p_far / whole).astype(BF16), far[:, HD:2 * HD])
    row = iota((2 * ROWS, HD), 0)
    row = jnp.where(row >= ROWS, row - ROWS, row)
    present = (row & (LEN - 1)) < by_response(row >> 5, own_lens)
    mixed = jnp.where(present, mixed, 0.0).astype(BF16)
    ctx[y] = jnp.concatenate((mixed[:ROWS], mixed[ROWS:]), axis=1)

    def ctx_out(k):
        return remote(ctx.at[y], ctx.at[y], cx_s.at[k], cx_r.at[k], dev(x, z, (y + k) % NY, c))

    def ctx_in(k):
        f = (y + NY - k) % NY
        return remote(ctx.at[f], ctx.at[f], cx_s.at[k], cx_r.at[k], dev(x, z, f, c))

    for k in (2, 1, 3):
        ctx_out(k).start()
    ring_steps(late, 6, last - 1)
    ring_last_sends(late)
    ring_close(late)

    def out_rows(half):
        return w32[2, pl.ds(pl.multiple_of(half * FEAT, 8), FEAT), :].astype(BF16)

    w_other, w_mine = out_rows(1 - c), out_rows(c)

    def swap(k):
        t = (y + NY - k) % NY
        return remote(
            co_out.at[t], co_in.at[t], co_s.at[k], co_r.at[k], dev(x, z, y, 1 - c)
        )

    def xsum(k):
        t = (x + k) % NX
        return remote(xo_out.at[t], xo_in.at[k], xo_s.at[k], xo_r.at[k], dev(t, z, y, c))

    order = (0, 1, 3, 2)
    for k in order:
        t = (y + NY - k) % NY
        if k > 0:
            ctx_in(k).wait_recv()
        co_out[t] = dot(ctx[t], w_other, NTR).astype(BF16)
        swap(k).start()
        xo_out[t] = dot(ctx[t], w_mine, NTR).astype(BF16)
    for k in order:
        t = (y + NY - k) % NY
        swap(k).wait_recv()
        xo_out[t] = (xo_out[t].astype(F32) + co_in[t].astype(F32)).astype(BF16)

        @pl.when(t != x)
        def _():
            xsum((t + NX - x) % NX).start()

    attended = xo_out[x].astype(F32)
    for k in (1, 3, 2):
        xsum(k).wait_recv()
        attended = attended + xo_in[k].astype(F32)

    squares = column_to_row(jnp.sum(attended * attended, axis=1, keepdims=True))
    fin_in[0] = jnp.where(sub == 0, squares, 0.0)

    def fin_out(k):
        return remote(
            fin_in.at[0], fin_in.at[k], fn_s.at[k], fn_r.at[k],
            {"pair": pair, "tensor": (ten + k) % NT},
        )

    @pl.loop(1, NT)
    def _(k):
        fin_out(k).start()

    @pl.when(off_diagonal)
    def _():
        turned(True).wait_send()
        turned(False).wait_send()

    @pl.loop(1, NZ)
    def _(k):
        z_out(k).wait_send()

    for p in range(3):
        @pl.loop(0, NZ // 2 - 1)
        def _(s):
            ring(p, 0, s, s).wait_send()
            ring(p, 1, s, s).wait_send()

        ring(p, 0, NZ // 2 - 1, NZ // 2 - 1).wait_send()
    for n in range(6):
        x_out(n).wait_send()
    for dx in range(NX):
        share(dx).wait_send()

    @pl.loop(1, NT)
    def _(k):
        squares_out(k).wait_send()

    for k in range(1, NY):
        sum_out(k).wait_send()
        far_out(k).wait_send()
        ctx_out(k).wait_send()
        xsum(k).wait_send()
    for k in order:
        swap(k).wait_send()

    residual = judged[x].astype(F32)
    gained = attended * post[...].reshape(1, FEAT)

    @pl.loop(1, NT)
    def _(k):
        fin_out(k).wait_recv()

    total = fin_in[0]
    for k in range(1, NT):
        total = total + fin_in[k]
    scale = lax.rsqrt(row_to_column(total[0:1], ROWS) / width + epsilon)
    out[...] = (residual + gained * scale).astype(BF16)

    @pl.loop(1, NT)
    def _(k):
        fin_out(k).wait_send()


def shards(
    rollout, counts, lengths, partner_slot, pre_gain, post_gain,
    query_weight, key_weight, value_weight, out_weight,
):
    vmem = pl.BlockSpec(memory_space=pltpu.VMEM)
    hbm = pl.BlockSpec(memory_space=pltpu.HBM)
    smem = pl.BlockSpec(memory_space=pltpu.SMEM)
    dma = pltpu.SemaphoreType.DMA
    scratch = [
        pltpu.VMEM((ROWS, FEAT), BF16),
        pltpu.VMEM((WROWS, 256), BF16),
        pltpu.VMEM((WROWS, HD), BF16),
        pltpu.VMEM((WROWS, HD), BF16),
        pltpu.VMEM((WROWS, 256), BF16),
        dma((5,)),
        pltpu.VMEM((ROWS, WIDE), BF16),
        pltpu.VMEM((NZ, SLOTS, WIDE), BF16),
        pltpu.VMEM((NZ, SLOTS, WIDE), BF16),
        pltpu.VMEM((3, 2 * WROWS, HD), BF16),
        pltpu.VMEM((NZ, 3, 2 * WROWS, HD), BF16),
        pltpu.VMEM((3, BLOCK, 2 * HD), F32),
        pltpu.VMEM((8, 128), I32),
        pltpu.VMEM((8, 128), I32),
        pltpu.VMEM((NX, ALL_SLOTS, WIDE), BF16),
        pltpu.VMEM((NC, NX, ROWS, FEAT), BF16),
        pltpu.VMEM((NX, ROWS, FEAT), BF16),
        pltpu.VMEM((NT, 8, 128), F32),
        pltpu.VMEM((NT, 8, 128), F32),
        pltpu.VMEM((NX, ROWS, 512), BF16),
        pltpu.VMEM((NY, ROWS, 512), BF16),
        pltpu.VMEM((NY, ROWS, 256), BF16),
        pltpu.VMEM((NY, ROWS, 256), BF16),
        pltpu.VMEM((NX, ROWS, FEAT), BF16),
        pltpu.VMEM((NX, ROWS, FEAT), BF16),
        pltpu.VMEM((NX, ROWS, FEAT), BF16),
        pltpu.VMEM((NX, ROWS, FEAT), BF16),
        dma((2,)), dma((2,)),
        dma((NZ,)), dma((NZ,)),
        dma((3, 2, NZ // 2)), dma((3, 2, NZ // 2)),
        dma((6,)), dma((6,)),
        dma((NX,)), dma((NX,)),
        dma((NT,)), dma((NT,)),
        dma((NY,)), dma((NY,)),
        dma((NY,)), dma((NY,)),
        dma((NY,)), dma((NY,)),
        dma((NX,)), dma((NX,)),
        dma((NX,)), dma((NX,)),
        dma((NT,)), dma((NT,)),
    ]
    return pl.pallas_call(
        kernel,
        out_shape=jax.ShapeDtypeStruct((ROWS, FEAT), BF16),
        in_specs=[hbm, vmem, smem, vmem, vmem, vmem, hbm, hbm, hbm, hbm],
        out_specs=vmem,
        scratch_shapes=scratch,
        compiler_params=pltpu.CompilerParams(
            collective_id=0, has_side_effects=True, vmem_limit_bytes=62 * 1024 * 1024
        ),
    )(
        rollout, counts, lengths, partner_slot, pre_gain,
        post_gain, query_weight, key_weight, value_weight, out_weight,
    )


def solution(mesh):
    placed = (
        P("pair", "tensor"),
        P("pair", None),
        P(),
        P("pair", None),
        P(),
        P("tensor"),
        P("pair", "tensor"),
        P("pair", "tensor"),
        P("pair", "tensor"),
        P("pair", "tensor"),
    )
    return jax.shard_map(
        shards, mesh=mesh, in_specs=placed, out_specs=P("pair", "tensor"), check_vma=False
    )
```

```python
import jax
import jax.numpy as jnp
from jax import lax
from jax.experimental import pallas as pl
from jax.experimental.pallas import tpu as pltpu
from jax.sharding import PartitionSpec as P

NX, NY, NZ, NC = 4, 4, 16, 2
NT = NY * NC
HD = 128
LEN = 32
RESP = 3
ROWS = RESP * LEN
FEAT = 576
WIDE = 640
WROWS = 72
BLOCK = NZ * WROWS
CAP = 3
SLOTS = NX * 4
KEPT = NZ * CAP
ALL_SLOTS = NX * KEPT
HALF = ALL_SLOTS // 2

score_scale = 144.0 ** (-0.5)
soft_cap = 50.0
epsilon = 1e-06
negative = -1e30

F32 = jnp.float32
BF16 = jnp.bfloat16
I32 = jnp.int32
MESH = pl.DeviceIdType.MESH
NN = (((1,), (0,)), ((), ()))
NTR = (((1,), (1,)), ((), ()))


def dot(a, b, dims=NN):
    return lax.dot_general(a, b, dims, preferred_element_type=F32)


def iota(shape, dim):
    return lax.broadcasted_iota(I32, shape, dim)


def ones_where(cond):
    return jnp.where(cond, 1.0, 0.0).astype(BF16)


def column_to_row(col):
    rows = col.shape[0]
    same = iota((rows, 128), 0) == iota((rows, 128), 1)
    return jnp.sum(jnp.where(same, col, 0.0), axis=0, keepdims=True)


def row_to_column(row, rows):
    same = iota((rows, 128), 0) == iota((rows, 128), 1)
    return jnp.sum(jnp.where(same, row, 0.0), axis=1, keepdims=True)


def kernel(
    roll_h, counts, lens, pslot, gain, post, wq_h, wk_h, wv_h, wo_h, out,
    roll, wq, wk, wv, wo, in_s, xin, zsend, zrecv, wsend, wbuf, w32, slot_out, slot_in, xg, xs, judged, sq_in, fin_in,
    part, part_in, far_in, ctx, co_out, co_in, xo_out, xo_in,
    tr_s, tr_r, za_s, za_r, ring_s, ring_r, xg_s, xg_r, cs_s, cs_r, sq_s, sq_r,
    rs_s, rs_r, far_s, far_r, cx_s, cx_r, co_s, co_r, xo_s, xo_r, fn_s, fn_r,
):
    pair = lax.axis_index("pair")
    ten = lax.axis_index("tensor")
    x, z = pair // NZ, pair % NZ
    y, c = ten // NC, ten % NC

    def dev(xx, zz, yy, cc):
        return {"pair": xx * NZ + zz, "tensor": yy * NC + cc}

    def remote(src, dst, send, recv, where):
        return pltpu.make_async_remote_copy(
            src_ref=src, dst_ref=dst, send_sem=send, recv_sem=recv,
            device_id=where, device_id_type=MESH,
        )

    off_diagonal = x != y

    loads = [
        pltpu.make_async_copy(a, b, in_s.at[n])
        for n, (a, b) in enumerate(
            ((roll_h, roll), (wq_h, wq), (wk_h, wk), (wv_h, wv), (wo_h, wo))
        )
    ]
    for load in loads:
        load.start()

    barrier = pltpu.get_barrier_semaphore()

    def greet(where):
        pl.semaphore_signal(barrier, inc=1, device_id=where, device_id_type=MESH)

    @pl.loop(1, NZ)
    def _(k):
        greet(dev(x, (z + k) % NZ, y, c))

    @pl.loop(1, NX)
    def _(k):
        greet(dev((x + k) % NX, z, y, c))

    @pl.loop(1, NT)
    def _(k):
        greet({"pair": pair, "tensor": (ten + k) % NT})

    @pl.when(off_diagonal)
    def _():
        greet(dev(y, z, x, c))

    xin[...] = jnp.ones((ROWS, WIDE), BF16)
    slots = NZ * SLOTS
    j = iota((slots, NX * NZ), 0)
    dest = ((j >> 2) & (NX - 1)) * NZ + (j >> 4)
    other = iota((slots, NX * NZ), 1)
    sending = counts[...].astype(F32)
    start = jnp.sum(jnp.where(other < dest, sending, 0.0), axis=1, keepdims=True)
    amount = jnp.sum(jnp.where(other == dest, sending, 0.0), axis=1, keepdims=True)
    k_slot = (iota((slots, 1), 0) & 3).astype(F32)
    wanted = jnp.where((k_slot < amount) & (k_slot < CAP), start + k_slot, -1.0)
    pick = ones_where(wanted == iota((slots, ROWS), 1).astype(F32))
    loads[0].wait()
    xin[:, :FEAT] = roll[...]
    zsend[...] = dot(pick, xin[...]).astype(BF16).reshape(NZ, SLOTS, WIDE)
    zrecv[z] = zsend[z]

    for load in loads[1:]:
        load.wait()

    def pack(p, first, second):
        wsend[p] = jnp.concatenate(
            (first.astype(F32), second.astype(F32)), axis=0
        ).astype(BF16)

    pack(0, wq[:, :HD], wq[:, HD:])
    pack(1, wk[...], wv[...])
    pack(2, wo[:, :HD], wo[:, HD:])
    lane = iota((8, 128), 1)
    spread = jnp.zeros((8, 128), I32)
    for k in range(RESP):
        spread = jnp.where(lane == k, pslot[0:1, k:k + 1], spread)
    slot_out[...] = spread

    greeted = NZ - 1 + NX - 1 + NT - 1

    @pl.when(off_diagonal)
    def _():
        pl.semaphore_wait(barrier, greeted + 1)

    @pl.when(jnp.logical_not(off_diagonal))
    def _():
        pl.semaphore_wait(barrier, greeted)

    def z_out(k):
        t = (z + k) % NZ
        return remote(zsend.at[t], zrecv.at[z], za_s.at[k], za_r.at[k], dev(x, t, y, c))

    def z_in(k):
        f = (z + NZ - k) % NZ
        return remote(zsend.at[f], zrecv.at[f], za_s.at[k], za_r.at[k], dev(x, f, y, c))

    def turned(first):
        if first:
            return remote(wsend, wbuf.at[z], tr_s.at[0], tr_r.at[0], dev(y, z, x, c))
        return remote(slot_out, slot_in, tr_s.at[1], tr_r.at[1], dev(y, z, x, c))

    @pl.when(off_diagonal)
    def _():
        turned(True).start()
        turned(False).start()

    z_out(NZ // 2).start()

    @pl.loop(1, NZ // 2)
    def _(k):
        z_out(NZ // 2 - k).start()
        z_out(NZ // 2 + k).start()

    @pl.when(jnp.logical_not(off_diagonal))
    def _():
        wbuf[z] = wsend[...]
        slot_in[...] = slot_out[...]

    up, down = (z + 1) % NZ, (z + NZ - 1) % NZ

    def ring_block(d, s):
        return (z + NZ - s) % NZ if d == 0 else (z + s) % NZ

    def ring(p, d, s, distance):
        block = wbuf.at[ring_block(d, distance), p]
        return remote(
            block, block, ring_s.at[p, d, s], ring_r.at[p, d, s],
            dev(x, up if d == 0 else down, y, c),
        )

    def unpack(p, block):
        v = wbuf[block, p].astype(F32)
        at = pl.ds(pl.multiple_of(block * WROWS, 8), WROWS)
        w32[p, at, 0:HD] = v[:WROWS]
        w32[p, at, HD:2 * HD] = v[WROWS:]

    def ring_open(p):
        ring(p, 0, 0, 0).start()
        ring(p, 1, 0, 0).start()
        unpack(p, z)

    def ring_steps(pieces, low, high):
        @pl.loop(low, high)
        def _(s):
            for p in pieces:
                for d in (0, 1):
                    ring(p, d, s - 1, s).wait_recv()
                    ring(p, d, s, s).start()
            for p in pieces:
                for d in (0, 1):
                    unpack(p, ring_block(d, s))

    last = NZ // 2

    def ring_last_sends(pieces):
        for p in pieces:
            for d in (0, 1):
                ring(p, d, last - 2, last - 1).wait_recv()
            ring(p, 0, last - 1, last - 1).start()
        for p in pieces:
            for d in (0, 1):
                unpack(p, ring_block(d, last - 1))

    def ring_close(pieces):
        for p in pieces:
            ring(p, 0, last - 1, last).wait_recv()
            unpack(p, ring_block(0, last))

    @pl.when(off_diagonal)
    def _():
        turned(True).wait_recv()
        turned(False).wait_recv()

    pieces = (0, 1, 2)
    for p in pieces:
        ring_open(p)
    ring_steps(pieces, 1, 3)

    @pl.loop(1, NZ)
    def _(k):
        z_in(k).wait_recv()

    i = iota((ALL_SLOTS, slots), 0)
    q = (i * 171) >> 9
    held_at = (q & (NZ - 1)) * SLOTS + (q >> 4) * 4 + (i - 3 * q)
    squeeze = ones_where(held_at == iota((ALL_SLOTS, slots), 1))
    xg[x] = dot(squeeze, zrecv[...].reshape(slots, WIDE)).astype(BF16)

    right, left = (x + 1) % NX, (x + NX - 1) % NX
    parts = (pl.ds(0, HALF), pl.ds(HALF, HALF))
    plan = (
        (0, 0, 1), (0, 1, 1), (1, 1, 1), (1, 0, 1), (0, 0, 2), (1, 1, 2),
    )

    def x_block(d, distance):
        return (x + NX - distance) % NX if d == 0 else (x + distance) % NX

    def x_out(n):
        d, half, distance = plan[n]
        block = xg.at[x_block(d, distance - 1), parts[half]]
        return remote(
            block, block, xg_s.at[n], xg_r.at[n],
            dev(right if d == 0 else left, z, y, c),
        )

    def x_in(n):
        d, half, distance = plan[n]
        block = xg.at[x_block(d, distance), parts[half]]
        return remote(
            block, block, xg_s.at[n], xg_r.at[n],
            dev(right if d == 0 else left, z, y, c),
        )

    for n in (0, 2, 1, 3):
        x_out(n).start()
    ring_steps(pieces, 3, 4)
    x_in(0).wait_recv()
    x_out(4).start()
    x_in(2).wait_recv()
    x_out(5).start()
    ring_steps(pieces, 4, 6)
    for n in (1, 3, 4, 5):
        x_in(n).wait_recv()

    before = ones_where(iota((ALL_SLOTS, ALL_SLOTS), 0) < iota((ALL_SLOTS, ALL_SLOTS), 1))
    flag_lane = ones_where(iota((16, 128), 1) == FEAT - 512)
    my_gain = gain[pl.ds(pl.multiple_of(y * NC * FEAT, 128), NC * FEAT)].reshape(1, NC * FEAT)
    my_gain = jnp.where(c == 0, my_gain[:, :FEAT], my_gain[:, FEAT:])
    table = jnp.zeros((8, 128), F32)
    sub = iota((8, 128), 0)

    def share(dx):
        return remote(
            xs.at[c, dx], xs.at[c, dx], cs_s.at[dx], cs_r.at[dx], dev(x, z, y, 1 - c)
        )

    def share_in(dx):
        return remote(
            xs.at[1 - c, dx], xs.at[1 - c, dx], cs_s.at[dx], cs_r.at[dx], dev(x, z, y, 1 - c)
        )

    for dx in range(NX):
        s = xg[:, dx * KEPT:(dx + 1) * KEPT, :].reshape(ALL_SLOTS, WIDE)
        filled = dot(flag_lane, s[:, 512:WIDE], NTR)
        rank = dot(filled.astype(BF16), before)
        key = jnp.where(filled > 0.5, rank, -1.0)[0:1]
        place = ones_where(iota((ROWS, ALL_SLOTS), 0).astype(F32) == key)
        rows = dot(place, s)[:, :FEAT]
        judged[dx] = rows.astype(BF16)
        xs[c, dx] = (rows * my_gain).astype(BF16)
        share(dx).start()
        squares = column_to_row(jnp.sum(rows * rows, axis=1, keepdims=True))
        table = jnp.where(sub == dx, squares, table)

    sq_in[0] = table

    def squares_out(k):
        return remote(
            sq_in.at[0], sq_in.at[k], sq_s.at[k], sq_r.at[k],
            {"pair": pair, "tensor": (ten + k) % NT},
        )

    @pl.loop(1, NT)
    def _(k):
        squares_out(k).start()

    ring_steps(pieces, 6, last - 1)
    ring_last_sends(pieces)
    ring_close((0, 1))
    for dx in range(NX):
        share_in(dx).wait_recv()

    first = xs[0].reshape(NX * ROWS, FEAT)
    second = xs[1].reshape(NX * ROWS, FEAT)
    for p in (0, 1):
        w = w32[p].astype(BF16)
        t = dot(first, w[:FEAT]) + dot(second, w[FEAT:])
        part[:, :, p * 256:(p + 1) * 256] = t.astype(BF16).reshape(NX, ROWS, 256)

    def sum_out(k):
        t = (y + k) % NY
        return remote(part.at[t], part_in.at[k], rs_s.at[k], rs_r.at[k], dev(x, z, t, c))

    def far_out(k):
        t = (y + k) % NY
        return remote(
            part.at[(t + NY // 2) % NY, :, pl.ds(256, 256)], far_in.at[k],
            far_s.at[k], far_r.at[k], dev(x, z, t, c),
        )

    for k in (2, 1, 3):
        sum_out(k).start()
        far_out(k).start()

    ring_close((2,))

    @pl.loop(1, NT)
    def _(k):
        squares_out(k).wait_recv()

    total = sq_in[0]
    for k in range(1, NT):
        total = total + sq_in[k]
    far_y = (y + NY // 2) % NY
    width = float(NT * FEAT)

    def row_scale(which):
        row = jnp.sum(jnp.where(sub == which, total, 0.0), axis=0, keepdims=True)
        return lax.rsqrt(row_to_column(row, ROWS) / width + epsilon)

    scale_own, scale_far = row_scale(y), row_scale(far_y)
    for k in range(1, NY):
        sum_out(k).wait_recv()
        far_out(k).wait_recv()
    own = part[y].astype(F32)
    far = part[far_y, :, 256:512].astype(F32)
    for k in range(1, NY):
        own = own + part_in[k].astype(F32)
        far = far + far_in[k].astype(F32)
    own = (own * scale_own).astype(BF16)
    far = (far * scale_far).astype(BF16)

    queries = jnp.concatenate((own[:, 0:HD], own[:, HD:2 * HD]), axis=0)
    col = iota((2 * ROWS, ROWS), 1)
    row = iota((2 * ROWS, ROWS), 0)
    row = jnp.where(row >= ROWS, row - ROWS, row)
    resp_q, resp_k = row >> 5, col >> 5
    spot_q, spot_k = row & (LEN - 1), col & (LEN - 1)

    def by_response(resp, values):
        return jnp.where(resp == 0, values[0], jnp.where(resp == 1, values[1], values[2]))

    own_lens = [lens[(y * NZ + z) * RESP + k] for k in range(RESP)]
    far_lens = [lens[(far_y * NZ + z) * RESP + k] for k in range(RESP)]
    partner = by_response(resp_q, [slot_in[0:1, k:k + 1] for k in range(RESP)])
    own_ok = (resp_q == resp_k) & (spot_k <= spot_q) & (spot_k < by_response(resp_k, own_lens))
    far_ok = (partner == resp_k) & (spot_k < by_response(resp_k, far_lens))

    def powers(keys, ok):
        scores = dot(queries, keys, NTR) * score_scale
        scores = soft_cap * jnp.tanh(scores / soft_cap)
        return jnp.exp(jnp.where(ok, scores, negative))

    p_own = powers(own[:, 256:384], own_ok)
    p_far = powers(far[:, 0:HD], far_ok)
    whole = jnp.sum(p_own, axis=1, keepdims=True) + jnp.sum(p_far, axis=1, keepdims=True)
    mixed = dot((p_own / whole).astype(BF16), own[:, 384:512])
    mixed = mixed + dot((p_far / whole).astype(BF16), far[:, HD:2 * HD])
    row = iota((2 * ROWS, HD), 0)
    row = jnp.where(row >= ROWS, row - ROWS, row)
    present = (row & (LEN - 1)) < by_response(row >> 5, own_lens)
    mixed = jnp.where(present, mixed, 0.0).astype(BF16)
    ctx[y] = jnp.concatenate((mixed[:ROWS], mixed[ROWS:]), axis=1)

    def ctx_out(k):
        return remote(ctx.at[y], ctx.at[y], cx_s.at[k], cx_r.at[k], dev(x, z, (y + k) % NY, c))

    def ctx_in(k):
        f = (y + NY - k) % NY
        return remote(ctx.at[f], ctx.at[f], cx_s.at[k], cx_r.at[k], dev(x, z, f, c))

    for k in (2, 1, 3):
        ctx_out(k).start()

    def out_rows(half):
        return w32[2, pl.ds(pl.multiple_of(half * FEAT, 8), FEAT), :].astype(BF16)

    w_other, w_mine = out_rows(1 - c), out_rows(c)

    def swap(k):
        t = (y + NY - k) % NY
        return remote(
            co_out.at[t], co_in.at[t], co_s.at[k], co_r.at[k], dev(x, z, y, 1 - c)
        )

    def xsum(k):
        t = (x + k) % NX
        return remote(xo_out.at[t], xo_in.at[k], xo_s.at[k], xo_r.at[k], dev(t, z, y, c))

    order = (0, 1, 3, 2)
    for k in order:
        t = (y + NY - k) % NY
        if k > 0:
            ctx_in(k).wait_recv()
        co_out[t] = dot(ctx[t], w_other, NTR).astype(BF16)
        swap(k).start()
        xo_out[t] = dot(ctx[t], w_mine, NTR).astype(BF16)
    for k in order:
        t = (y + NY - k) % NY
        swap(k).wait_recv()
        xo_out[t] = (xo_out[t].astype(F32) + co_in[t].astype(F32)).astype(BF16)

        @pl.when(t != x)
        def _():
            xsum((t + NX - x) % NX).start()

    attended = xo_out[x].astype(F32)
    for k in (1, 3, 2):
        xsum(k).wait_recv()
        attended = attended + xo_in[k].astype(F32)

    squares = column_to_row(jnp.sum(attended * attended, axis=1, keepdims=True))
    fin_in[0] = jnp.where(sub == 0, squares, 0.0)

    def fin_out(k):
        return remote(
            fin_in.at[0], fin_in.at[k], fn_s.at[k], fn_r.at[k],
            {"pair": pair, "tensor": (ten + k) % NT},
        )

    @pl.loop(1, NT)
    def _(k):
        fin_out(k).start()

    @pl.when(off_diagonal)
    def _():
        turned(True).wait_send()
        turned(False).wait_send()

    @pl.loop(1, NZ)
    def _(k):
        z_out(k).wait_send()

    for p in range(3):
        @pl.loop(0, NZ // 2 - 1)
        def _(s):
            ring(p, 0, s, s).wait_send()
            ring(p, 1, s, s).wait_send()

        ring(p, 0, NZ // 2 - 1, NZ // 2 - 1).wait_send()
    for n in range(6):
        x_out(n).wait_send()
    for dx in range(NX):
        share(dx).wait_send()

    @pl.loop(1, NT)
    def _(k):
        squares_out(k).wait_send()

    for k in range(1, NY):
        sum_out(k).wait_send()
        far_out(k).wait_send()
        ctx_out(k).wait_send()
        xsum(k).wait_send()
    for k in order:
        swap(k).wait_send()

    residual = judged[x].astype(F32)
    gained = attended * post[...].reshape(1, FEAT)

    @pl.loop(1, NT)
    def _(k):
        fin_out(k).wait_recv()

    total = fin_in[0]
    for k in range(1, NT):
        total = total + fin_in[k]
    scale = lax.rsqrt(row_to_column(total[0:1], ROWS) / width + epsilon)
    out[...] = (residual + gained * scale).astype(BF16)

    @pl.loop(1, NT)
    def _(k):
        fin_out(k).wait_send()


def shards(
    rollout, counts, lengths, partner_slot, pre_gain, post_gain,
    query_weight, key_weight, value_weight, out_weight,
):
    vmem = pl.BlockSpec(memory_space=pltpu.VMEM)
    hbm = pl.BlockSpec(memory_space=pltpu.HBM)
    smem = pl.BlockSpec(memory_space=pltpu.SMEM)
    dma = pltpu.SemaphoreType.DMA
    scratch = [
        pltpu.VMEM((ROWS, FEAT), BF16),
        pltpu.VMEM((WROWS, 256), BF16),
        pltpu.VMEM((WROWS, HD), BF16),
        pltpu.VMEM((WROWS, HD), BF16),
        pltpu.VMEM((WROWS, 256), BF16),
        dma((5,)),
        pltpu.VMEM((ROWS, WIDE), BF16),
        pltpu.VMEM((NZ, SLOTS, WIDE), BF16),
        pltpu.VMEM((NZ, SLOTS, WIDE), BF16),
        pltpu.VMEM((3, 2 * WROWS, HD), BF16),
        pltpu.VMEM((NZ, 3, 2 * WROWS, HD), BF16),
        pltpu.VMEM((3, BLOCK, 2 * HD), F32),
        pltpu.VMEM((8, 128), I32),
        pltpu.VMEM((8, 128), I32),
        pltpu.VMEM((NX, ALL_SLOTS, WIDE), BF16),
        pltpu.VMEM((NC, NX, ROWS, FEAT), BF16),
        pltpu.VMEM((NX, ROWS, FEAT), BF16),
        pltpu.VMEM((NT, 8, 128), F32),
        pltpu.VMEM((NT, 8, 128), F32),
        pltpu.VMEM((NX, ROWS, 512), BF16),
        pltpu.VMEM((NY, ROWS, 512), BF16),
        pltpu.VMEM((NY, ROWS, 256), BF16),
        pltpu.VMEM((NY, ROWS, 256), BF16),
        pltpu.VMEM((NX, ROWS, FEAT), BF16),
        pltpu.VMEM((NX, ROWS, FEAT), BF16),
        pltpu.VMEM((NX, ROWS, FEAT), BF16),
        pltpu.VMEM((NX, ROWS, FEAT), BF16),
        dma((2,)), dma((2,)),
        dma((NZ,)), dma((NZ,)),
        dma((3, 2, NZ // 2)), dma((3, 2, NZ // 2)),
        dma((6,)), dma((6,)),
        dma((NX,)), dma((NX,)),
        dma((NT,)), dma((NT,)),
        dma((NY,)), dma((NY,)),
        dma((NY,)), dma((NY,)),
        dma((NY,)), dma((NY,)),
        dma((NX,)), dma((NX,)),
        dma((NX,)), dma((NX,)),
        dma((NT,)), dma((NT,)),
    ]
    return pl.pallas_call(
        kernel,
        out_shape=jax.ShapeDtypeStruct((ROWS, FEAT), BF16),
        in_specs=[hbm, vmem, smem, vmem, vmem, vmem, hbm, hbm, hbm, hbm],
        out_specs=vmem,
        scratch_shapes=scratch,
        compiler_params=pltpu.CompilerParams(
            collective_id=0, has_side_effects=True, vmem_limit_bytes=62 * 1024 * 1024
        ),
    )(
        rollout, counts, lengths, partner_slot, pre_gain,
        post_gain, query_weight, key_weight, value_weight, out_weight,
    )


def solution(mesh):
    placed = (
        P("pair", "tensor"),
        P("pair", None),
        P(),
        P("pair", None),
        P(),
        P("tensor"),
        P("pair", "tensor"),
        P("pair", "tensor"),
        P("pair", "tensor"),
        P("pair", "tensor"),
    )
    return jax.shard_map(
        shards, mesh=mesh, in_specs=placed, out_specs=P("pair", "tensor"), check_vma=False
    )
```

```python
import jax
import jax.numpy as jnp
from jax import lax
from jax.experimental import pallas as pl
from jax.experimental.pallas import tpu as pltpu
from jax.sharding import PartitionSpec as P

NX, NY, NZ, NC = 4, 4, 16, 2
NT = NY * NC
HD = 128
LEN = 32
RESP = 3
ROWS = RESP * LEN
FEAT = 576
WIDE = 640
WROWS = 72
BLOCK = NZ * WROWS
CAP = 3
SLOTS = NX * 4
KEPT = NZ * CAP
ALL_SLOTS = NX * KEPT
HALF = ALL_SLOTS // 2

score_scale = 144.0 ** (-0.5)
soft_cap = 50.0
epsilon = 1e-06
negative = -1e30

F32 = jnp.float32
BF16 = jnp.bfloat16
I32 = jnp.int32
MESH = pl.DeviceIdType.MESH
NN = (((1,), (0,)), ((), ()))
NTR = (((1,), (1,)), ((), ()))


def dot(a, b, dims=NN):
    return lax.dot_general(a, b, dims, preferred_element_type=F32)


def iota(shape, dim):
    return lax.broadcasted_iota(I32, shape, dim)


def ones_where(cond):
    return jnp.where(cond, 1.0, 0.0).astype(BF16)


def column_to_row(col):
    rows = col.shape[0]
    same = iota((rows, 128), 0) == iota((rows, 128), 1)
    return jnp.sum(jnp.where(same, col, 0.0), axis=0, keepdims=True)


def row_to_column(row, rows):
    same = iota((rows, 128), 0) == iota((rows, 128), 1)
    return jnp.sum(jnp.where(same, row, 0.0), axis=1, keepdims=True)


def kernel(
    roll_h, counts, lens, pslot, gain, post, wq_h, wk_h, wv_h, wo_h, out,
    roll, wq, wk, wv, wo, in_s, xin, zsend, zrecv, wsend, wbuf, w32, slot_out, slot_in, xg, xs, judged, sq_in, fin_in,
    part, part_in, ycomb, ctx, co_out, co_in, xo_out, xo_in, xcomb,
    tr_s, tr_r, za_s, za_r, ring_s, ring_r, xg_s, xg_r, cs_s, cs_r, sq_s, sq_r,
    rs_s, rs_r, cx_s, cx_r, co_s, co_r, xo_s, xo_r, fn_s, fn_r,
):
    pair = lax.axis_index("pair")
    ten = lax.axis_index("tensor")
    x, z = pair // NZ, pair % NZ
    y, c = ten // NC, ten % NC

    def dev(xx, zz, yy, cc):
        return {"pair": xx * NZ + zz, "tensor": yy * NC + cc}

    def remote(src, dst, send, recv, where):
        return pltpu.make_async_remote_copy(
            src_ref=src, dst_ref=dst, send_sem=send, recv_sem=recv,
            device_id=where, device_id_type=MESH,
        )

    off_diagonal = x != y

    loads = [
        pltpu.make_async_copy(a, b, in_s.at[n])
        for n, (a, b) in enumerate(
            ((roll_h, roll), (wq_h, wq), (wk_h, wk), (wv_h, wv), (wo_h, wo))
        )
    ]
    for load in loads:
        load.start()

    barrier = pltpu.get_barrier_semaphore()

    def greet(where):
        pl.semaphore_signal(barrier, inc=1, device_id=where, device_id_type=MESH)

    @pl.loop(1, NZ)
    def _(k):
        greet(dev(x, (z + k) % NZ, y, c))

    @pl.loop(1, NX)
    def _(k):
        greet(dev((x + k) % NX, z, y, c))

    @pl.loop(1, NT)
    def _(k):
        greet({"pair": pair, "tensor": (ten + k) % NT})

    @pl.when(off_diagonal)
    def _():
        greet(dev(y, z, x, c))

    xin[...] = jnp.ones((ROWS, WIDE), BF16)
    slots = NZ * SLOTS
    j = iota((slots, NX * NZ), 0)
    dest = ((j >> 2) & (NX - 1)) * NZ + (j >> 4)
    other = iota((slots, NX * NZ), 1)
    sending = counts[...].astype(F32)
    start = jnp.sum(jnp.where(other < dest, sending, 0.0), axis=1, keepdims=True)
    amount = jnp.sum(jnp.where(other == dest, sending, 0.0), axis=1, keepdims=True)
    k_slot = (iota((slots, 1), 0) & 3).astype(F32)
    wanted = jnp.where((k_slot < amount) & (k_slot < CAP), start + k_slot, -1.0)
    pick = ones_where(wanted == iota((slots, ROWS), 1).astype(F32))
    loads[0].wait()
    xin[:, :FEAT] = roll[...]
    zsend[...] = dot(pick, xin[...]).astype(BF16).reshape(NZ, SLOTS, WIDE)
    zrecv[z] = zsend[z]

    for load in loads[1:]:
        load.wait()

    def pack(p, first, second):
        wsend[p] = jnp.concatenate(
            (first.astype(F32), second.astype(F32)), axis=0
        ).astype(BF16)

    pack(0, wq[:, :HD], wq[:, HD:])
    pack(1, wk[...], wv[...])
    pack(2, wo[:, :HD], wo[:, HD:])
    lane = iota((8, 128), 1)
    spread = jnp.zeros((8, 128), I32)
    for k in range(RESP):
        spread = jnp.where(lane == k, pslot[0:1, k:k + 1], spread)
    slot_out[...] = spread

    greeted = NZ - 1 + NX - 1 + NT - 1

    @pl.when(off_diagonal)
    def _():
        pl.semaphore_wait(barrier, greeted + 1)

    @pl.when(jnp.logical_not(off_diagonal))
    def _():
        pl.semaphore_wait(barrier, greeted)

    def z_out(k):
        t = (z + k) % NZ
        return remote(zsend.at[t], zrecv.at[z], za_s.at[k], za_r.at[k], dev(x, t, y, c))

    def z_in(k):
        f = (z + NZ - k) % NZ
        return remote(zsend.at[f], zrecv.at[f], za_s.at[k], za_r.at[k], dev(x, f, y, c))

    def turned(first):
        if first:
            return remote(wsend, wbuf.at[z], tr_s.at[0], tr_r.at[0], dev(y, z, x, c))
        return remote(slot_out, slot_in, tr_s.at[1], tr_r.at[1], dev(y, z, x, c))

    @pl.when(off_diagonal)
    def _():
        turned(True).start()
        turned(False).start()

    z_out(NZ // 2).start()

    @pl.loop(1, NZ // 2)
    def _(k):
        z_out(NZ // 2 - k).start()
        z_out(NZ // 2 + k).start()

    @pl.when(jnp.logical_not(off_diagonal))
    def _():
        wbuf[z] = wsend[...]
        slot_in[...] = slot_out[...]

    up, down = (z + 1) % NZ, (z + NZ - 1) % NZ

    def ring_block(d, s):
        return (z + NZ - s) % NZ if d == 0 else (z + s) % NZ

    def ring(p, d, s, distance):
        block = wbuf.at[ring_block(d, distance), p]
        return remote(
            block, block, ring_s.at[p, d, s], ring_r.at[p, d, s],
            dev(x, up if d == 0 else down, y, c),
        )

    def unpack(p, block):
        v = wbuf[block, p].astype(F32)
        at = pl.ds(pl.multiple_of(block * WROWS, 8), WROWS)
        w32[p, at, 0:HD] = v[:WROWS]
        w32[p, at, HD:2 * HD] = v[WROWS:]

    def ring_open(p):
        ring(p, 0, 0, 0).start()
        ring(p, 1, 0, 0).start()
        unpack(p, z)

    def ring_steps(pieces, low, high):
        @pl.loop(low, high)
        def _(s):
            for p in pieces:
                for d in (0, 1):
                    ring(p, d, s - 1, s).wait_recv()
                    ring(p, d, s, s).start()
            for p in pieces:
                for d in (0, 1):
                    unpack(p, ring_block(d, s))

    last = NZ // 2

    def ring_last_sends(pieces):
        for p in pieces:
            for d in (0, 1):
                ring(p, d, last - 2, last - 1).wait_recv()
            ring(p, 0, last - 1, last - 1).start()
        for p in pieces:
            for d in (0, 1):
                unpack(p, ring_block(d, last - 1))

    def ring_close(pieces):
        for p in pieces:
            ring(p, 0, last - 1, last).wait_recv()
            unpack(p, ring_block(0, last))

    @pl.when(off_diagonal)
    def _():
        turned(True).wait_recv()
        turned(False).wait_recv()

    pieces = (0, 1, 2)
    for p in pieces:
        ring_open(p)
    ring_steps(pieces, 1, 3)

    @pl.loop(1, NZ)
    def _(k):
        z_in(k).wait_recv()

    i = iota((ALL_SLOTS, slots), 0)
    q = (i * 171) >> 9
    held_at = (q & (NZ - 1)) * SLOTS + (q >> 4) * 4 + (i - 3 * q)
    squeeze = ones_where(held_at == iota((ALL_SLOTS, slots), 1))
    xg[x] = dot(squeeze, zrecv[...].reshape(slots, WIDE)).astype(BF16)

    right, left = (x + 1) % NX, (x + NX - 1) % NX
    parts = (pl.ds(0, HALF), pl.ds(HALF, HALF))
    plan = (
        (0, 0, 1), (0, 1, 1), (1, 1, 1), (1, 0, 1), (0, 0, 2), (1, 1, 2),
    )

    def x_block(d, distance):
        return (x + NX - distance) % NX if d == 0 else (x + distance) % NX

    def x_out(n):
        d, half, distance = plan[n]
        block = xg.at[x_block(d, distance - 1), parts[half]]
        return remote(
            block, block, xg_s.at[n], xg_r.at[n],
            dev(right if d == 0 else left, z, y, c),
        )

    def x_in(n):
        d, half, distance = plan[n]
        block = xg.at[x_block(d, distance), parts[half]]
        return remote(
            block, block, xg_s.at[n], xg_r.at[n],
            dev(right if d == 0 else left, z, y, c),
        )

    for n in (0, 2, 1, 3):
        x_out(n).start()
    ring_steps(pieces, 3, 4)
    x_in(0).wait_recv()
    x_out(4).start()
    x_in(2).wait_recv()
    x_out(5).start()
    ring_steps(pieces, 4, 6)
    for n in (1, 3, 4, 5):
        x_in(n).wait_recv()

    before = ones_where(iota((ALL_SLOTS, ALL_SLOTS), 0) < iota((ALL_SLOTS, ALL_SLOTS), 1))
    flag_lane = ones_where(iota((16, 128), 1) == FEAT - 512)
    my_gain = gain[pl.ds(pl.multiple_of(y * NC * FEAT, 128), NC * FEAT)].reshape(1, NC * FEAT)
    my_gain = jnp.where(c == 0, my_gain[:, :FEAT], my_gain[:, FEAT:])
    table = jnp.zeros((8, 128), F32)
    sub = iota((8, 128), 0)

    def share(dx):
        return remote(
            xs.at[c, dx], xs.at[c, dx], cs_s.at[dx], cs_r.at[dx], dev(x, z, y, 1 - c)
        )

    def share_in(dx):
        return remote(
            xs.at[1 - c, dx], xs.at[1 - c, dx], cs_s.at[dx], cs_r.at[dx], dev(x, z, y, 1 - c)
        )

    for dx in range(NX):
        s = xg[:, dx * KEPT:(dx + 1) * KEPT, :].reshape(ALL_SLOTS, WIDE)
        filled = dot(flag_lane, s[:, 512:WIDE], NTR)
        rank = dot(filled.astype(BF16), before)
        key = jnp.where(filled > 0.5, rank, -1.0)[0:1]
        place = ones_where(iota((ROWS, ALL_SLOTS), 0).astype(F32) == key)
        rows = dot(place, s)[:, :FEAT]
        judged[dx] = rows.astype(BF16)
        xs[c, dx] = (rows * my_gain).astype(BF16)
        share(dx).start()
        squares = column_to_row(jnp.sum(rows * rows, axis=1, keepdims=True))
        table = jnp.where(sub == dx, squares, table)

    sq_in[0] = table

    def squares_out(k):
        return remote(
            sq_in.at[0], sq_in.at[k], sq_s.at[k], sq_r.at[k],
            {"pair": pair, "tensor": (ten + k) % NT},
        )

    @pl.loop(1, NT)
    def _(k):
        squares_out(k).start()

    ring_steps(pieces, 6, last - 1)
    ring_last_sends(pieces)
    ring_close((0, 1))
    for dx in range(NX):
        share_in(dx).wait_recv()

    first = xs[0].reshape(NX * ROWS, FEAT)
    second = xs[1].reshape(NX * ROWS, FEAT)

    def products(p):
        w = w32[p].astype(BF16)
        t = dot(first, w[:FEAT]) + dot(second, w[FEAT:])
        return t.astype(BF16).reshape(NX, ROWS, 256)

    key_values = products(1)
    part[:, :, 256:512] = key_values
    for dx in range(NX):
        part[dx, :, 512:768] = key_values[(dx + NX // 2) % NX]
    part[:, :, 0:256] = products(0)

    halves = (pl.ds(0, ROWS // 2), pl.ds(ROWS // 2, ROWS // 2))

    def y_near(d):
        return (y + 1) % NY if d == 0 else (y + NY - 1) % NY

    def ysum(stage, d):
        t = y_near(d)
        src = (
            part.at[(y + NY // 2) % NY, halves[d]], part.at[t, halves[1 - d]], ycomb.at[d]
        )[stage]
        return remote(
            src, part_in.at[stage, d], rs_s.at[stage, d], rs_r.at[stage, d], dev(x, z, t, c)
        )

    for stage in (0, 1):
        for d in (0, 1):
            ysum(stage, d).start()
    for d in (0, 1):
        ysum(0, d).wait_recv()
        mine = part[y_near(d), halves[d]].astype(F32)
        ycomb[d] = (mine + part_in[0, d].astype(F32)).astype(BF16)
        ysum(2, d).start()

    ring_close((2,))

    @pl.loop(1, NT)
    def _(k):
        squares_out(k).wait_recv()

    total = sq_in[0]
    for k in range(1, NT):
        total = total + sq_in[k]
    far_y = (y + NY // 2) % NY
    width = float(NT * FEAT)

    def row_scale(which):
        row = jnp.sum(jnp.where(sub == which, total, 0.0), axis=0, keepdims=True)
        return lax.rsqrt(row_to_column(row, ROWS) / width + epsilon)

    scale_own, scale_far = row_scale(y), row_scale(far_y)
    for stage in (1, 2):
        for d in (0, 1):
            ysum(stage, d).wait_recv()
    both = part[y].astype(F32) + jnp.concatenate(
        (
            part_in[2, 0].astype(F32) + part_in[1, 1].astype(F32),
            part_in[2, 1].astype(F32) + part_in[1, 0].astype(F32),
        ),
        axis=0,
    )
    own, far = both[:, 0:512], both[:, 512:768]
    own = (own * scale_own).astype(BF16)
    far = (far * scale_far).astype(BF16)

    queries = jnp.concatenate((own[:, 0:HD], own[:, HD:2 * HD]), axis=0)
    col = iota((2 * ROWS, ROWS), 1)
    row = iota((2 * ROWS, ROWS), 0)
    row = jnp.where(row >= ROWS, row - ROWS, row)
    resp_q, resp_k = row >> 5, col >> 5
    spot_q, spot_k = row & (LEN - 1), col & (LEN - 1)

    def by_response(resp, values):
        return jnp.where(resp == 0, values[0], jnp.where(resp == 1, values[1], values[2]))

    own_lens = [lens[(y * NZ + z) * RESP + k] for k in range(RESP)]
    far_lens = [lens[(far_y * NZ + z) * RESP + k] for k in range(RESP)]
    partner = by_response(resp_q, [slot_in[0:1, k:k + 1] for k in range(RESP)])
    own_ok = (resp_q == resp_k) & (spot_k <= spot_q) & (spot_k < by_response(resp_k, own_lens))
    far_ok = (partner == resp_k) & (spot_k < by_response(resp_k, far_lens))

    def powers(keys, ok):
        scores = dot(queries, keys, NTR) * score_scale
        scores = soft_cap * jnp.tanh(scores / soft_cap)
        return jnp.exp(jnp.where(ok, scores, negative))

    p_own = powers(own[:, 256:384], own_ok)
    p_far = powers(far[:, 0:HD], far_ok)
    whole = jnp.sum(p_own, axis=1, keepdims=True) + jnp.sum(p_far, axis=1, keepdims=True)
    mixed = dot((p_own / whole).astype(BF16), own[:, 384:512])
    mixed = mixed + dot((p_far / whole).astype(BF16), far[:, HD:2 * HD])
    row = iota((2 * ROWS, HD), 0)
    row = jnp.where(row >= ROWS, row - ROWS, row)
    present = (row & (LEN - 1)) < by_response(row >> 5, own_lens)
    mixed = jnp.where(present, mixed, 0.0).astype(BF16)
    ctx[y] = jnp.concatenate((mixed[:ROWS], mixed[ROWS:]), axis=1)

    def ctx_out(k):
        return remote(ctx.at[y], ctx.at[y], cx_s.at[k], cx_r.at[k], dev(x, z, (y + k) % NY, c))

    def ctx_in(k):
        f = (y + NY - k) % NY
        return remote(ctx.at[f], ctx.at[f], cx_s.at[k], cx_r.at[k], dev(x, z, f, c))

    for k in (2, 1, 3):
        ctx_out(k).start()

    def out_rows(half):
        return w32[2, pl.ds(pl.multiple_of(half * FEAT, 8), FEAT), :].astype(BF16)

    w_other, w_mine = out_rows(1 - c), out_rows(c)

    def swap(t):
        return remote(
            co_out.at[t], co_in.at[t], co_s.at[t], co_r.at[t], dev(x, z, y, 1 - c)
        )

    for k in (0, 1, 3, 2):
        t = (y + NY - k) % NY
        if k > 0:
            ctx_in(k).wait_recv()
        co_out[t] = dot(ctx[t], w_other, NTR).astype(BF16)
        swap(t).start()
        xo_out[t] = dot(ctx[t], w_mine, NTR).astype(BF16)

    def x_near(d):
        return right if d == 0 else left

    def xsum(stage, d):
        t = x_near(d)
        src = (
            xo_out.at[(x + NX // 2) % NX, halves[d]], xo_out.at[t, halves[1 - d]], xcomb.at[d]
        )[stage]
        return remote(
            src, xo_in.at[stage, d], xo_s.at[stage, d], xo_r.at[stage, d], dev(t, z, y, c)
        )

    def swapped(t):
        swap(t).wait_recv()
        xo_out[t] = (xo_out[t].astype(F32) + co_in[t].astype(F32)).astype(BF16)

    swapped((x + NX // 2) % NX)
    for d in (0, 1):
        xsum(0, d).start()
    for d in (0, 1):
        swapped(x_near(d))
        xsum(1, d).start()
    swapped(x)
    for d in (0, 1):
        xsum(0, d).wait_recv()
        mine = xo_out[x_near(d), halves[d]].astype(F32)
        xcomb[d] = (mine + xo_in[0, d].astype(F32)).astype(BF16)
        xsum(2, d).start()
    for stage in (1, 2):
        for d in (0, 1):
            xsum(stage, d).wait_recv()
    attended = xo_out[x].astype(F32) + jnp.concatenate(
        (
            xo_in[2, 0].astype(F32) + xo_in[1, 1].astype(F32),
            xo_in[2, 1].astype(F32) + xo_in[1, 0].astype(F32),
        ),
        axis=0,
    )

    squares = column_to_row(jnp.sum(attended * attended, axis=1, keepdims=True))
    fin_in[0] = jnp.where(sub == 0, squares, 0.0)

    def fin_out(k):
        return remote(
            fin_in.at[0], fin_in.at[k], fn_s.at[k], fn_r.at[k],
            {"pair": pair, "tensor": (ten + k) % NT},
        )

    @pl.loop(1, NT)
    def _(k):
        fin_out(k).start()

    @pl.when(off_diagonal)
    def _():
        turned(True).wait_send()
        turned(False).wait_send()

    @pl.loop(1, NZ)
    def _(k):
        z_out(k).wait_send()

    for p in range(3):
        @pl.loop(0, NZ // 2 - 1)
        def _(s):
            ring(p, 0, s, s).wait_send()
            ring(p, 1, s, s).wait_send()

        ring(p, 0, NZ // 2 - 1, NZ // 2 - 1).wait_send()
    for n in range(6):
        x_out(n).wait_send()
    for dx in range(NX):
        share(dx).wait_send()

    @pl.loop(1, NT)
    def _(k):
        squares_out(k).wait_send()

    for stage in range(3):
        for d in (0, 1):
            ysum(stage, d).wait_send()
            xsum(stage, d).wait_send()
    for k in range(1, NY):
        ctx_out(k).wait_send()
    for t in range(NX):
        swap(t).wait_send()

    residual = judged[x].astype(F32)
    gained = attended * post[...].reshape(1, FEAT)

    @pl.loop(1, NT)
    def _(k):
        fin_out(k).wait_recv()

    total = fin_in[0]
    for k in range(1, NT):
        total = total + fin_in[k]
    scale = lax.rsqrt(row_to_column(total[0:1], ROWS) / width + epsilon)
    out[...] = (residual + gained * scale).astype(BF16)

    @pl.loop(1, NT)
    def _(k):
        fin_out(k).wait_send()


def shards(
    rollout, counts, lengths, partner_slot, pre_gain, post_gain,
    query_weight, key_weight, value_weight, out_weight,
):
    vmem = pl.BlockSpec(memory_space=pltpu.VMEM)
    hbm = pl.BlockSpec(memory_space=pltpu.HBM)
    smem = pl.BlockSpec(memory_space=pltpu.SMEM)
    dma = pltpu.SemaphoreType.DMA
    scratch = [
        pltpu.VMEM((ROWS, FEAT), BF16),
        pltpu.VMEM((WROWS, 256), BF16),
        pltpu.VMEM((WROWS, HD), BF16),
        pltpu.VMEM((WROWS, HD), BF16),
        pltpu.VMEM((WROWS, 256), BF16),
        dma((5,)),
        pltpu.VMEM((ROWS, WIDE), BF16),
        pltpu.VMEM((NZ, SLOTS, WIDE), BF16),
        pltpu.VMEM((NZ, SLOTS, WIDE), BF16),
        pltpu.VMEM((3, 2 * WROWS, HD), BF16),
        pltpu.VMEM((NZ, 3, 2 * WROWS, HD), BF16),
        pltpu.VMEM((3, BLOCK, 2 * HD), F32),
        pltpu.VMEM((8, 128), I32),
        pltpu.VMEM((8, 128), I32),
        pltpu.VMEM((NX, ALL_SLOTS, WIDE), BF16),
        pltpu.VMEM((NC, NX, ROWS, FEAT), BF16),
        pltpu.VMEM((NX, ROWS, FEAT), BF16),
        pltpu.VMEM((NT, 8, 128), F32),
        pltpu.VMEM((NT, 8, 128), F32),
        pltpu.VMEM((NX, ROWS, 768), BF16),
        pltpu.VMEM((3, 2, ROWS // 2, 768), BF16),
        pltpu.VMEM((2, ROWS // 2, 768), BF16),
        pltpu.VMEM((NY, ROWS, 256), BF16),
        pltpu.VMEM((NX, ROWS, FEAT), BF16),
        pltpu.VMEM((NX, ROWS, FEAT), BF16),
        pltpu.VMEM((NX, ROWS, FEAT), BF16),
        pltpu.VMEM((3, 2, ROWS // 2, FEAT), BF16),
        pltpu.VMEM((2, ROWS // 2, FEAT), BF16),
        dma((2,)), dma((2,)),
        dma((NZ,)), dma((NZ,)),
        dma((3, 2, NZ // 2)), dma((3, 2, NZ // 2)),
        dma((6,)), dma((6,)),
        dma((NX,)), dma((NX,)),
        dma((NT,)), dma((NT,)),
        dma((3, 2)), dma((3, 2)),
        dma((NY,)), dma((NY,)),
        dma((NX,)), dma((NX,)),
        dma((3, 2)), dma((3, 2)),
        dma((NT,)), dma((NT,)),
    ]
    return pl.pallas_call(
        kernel,
        out_shape=jax.ShapeDtypeStruct((ROWS, FEAT), BF16),
        in_specs=[hbm, vmem, smem, vmem, vmem, vmem, hbm, hbm, hbm, hbm],
        out_specs=vmem,
        scratch_shapes=scratch,
        compiler_params=pltpu.CompilerParams(
            collective_id=0, has_side_effects=True, vmem_limit_bytes=62 * 1024 * 1024
        ),
    )(
        rollout, counts, lengths, partner_slot, pre_gain,
        post_gain, query_weight, key_weight, value_weight, out_weight,
    )


def solution(mesh):
    placed = (
        P("pair", "tensor"),
        P("pair", None),
        P(),
        P("pair", None),
        P(),
        P("tensor"),
        P("pair", "tensor"),
        P("pair", "tensor"),
        P("pair", "tensor"),
        P("pair", "tensor"),
    )
    return jax.shard_map(
        shards, mesh=mesh, in_specs=placed, out_specs=P("pair", "tensor"), check_vma=False
    )
```

```python
import jax
import jax.numpy as jnp
from jax import lax
from jax.experimental import pallas as pl
from jax.experimental.pallas import tpu as pltpu
from jax.sharding import PartitionSpec as P

NX, NY, NZ, NC = 4, 4, 16, 2
NT = NY * NC
HD = 128
LEN = 32
RESP = 3
ROWS = RESP * LEN
FEAT = 576
SIDE = 256
TAIL = FEAT - 2 * SIDE
WIDE = SIDE + 128
WROWS = 72
BLOCK = NZ * WROWS
CAP = 3
SLOTS = NX * 4
KEPT = NZ * CAP
ALL_SLOTS = NX * KEPT
HALF = ALL_SLOTS // 2

score_scale = 144.0 ** (-0.5)
soft_cap = 50.0
epsilon = 1e-06
negative = -1e30

F32 = jnp.float32
BF16 = jnp.bfloat16
I32 = jnp.int32
MESH = pl.DeviceIdType.MESH
NN = (((1,), (0,)), ((), ()))
NTR = (((1,), (1,)), ((), ()))


def dot(a, b, dims=NN):
    return lax.dot_general(a, b, dims, preferred_element_type=F32)


def iota(shape, dim):
    return lax.broadcasted_iota(I32, shape, dim)


def ones_where(cond):
    return jnp.where(cond, 1.0, 0.0).astype(BF16)


def column_to_row(col):
    rows = col.shape[0]
    same = iota((rows, 128), 0) == iota((rows, 128), 1)
    return jnp.sum(jnp.where(same, col, 0.0), axis=0, keepdims=True)


def row_to_column(row, rows):
    same = iota((rows, 128), 0) == iota((rows, 128), 1)
    return jnp.sum(jnp.where(same, row, 0.0), axis=1, keepdims=True)


def kernel(
    roll_h, counts, lens, pslot, gain, post, wq_h, wk_h, wv_h, wo_h, out,
    roll, wq, wk, wv, wo, in_s, low, zsend, zrecv, wsend, wbuf, w32, slot_out, slot_in, xg0, xg1, xs, judged, sq_in, fin_in,
    part, part_in, far_in, ctx, co_out, co_in, xo_out, xo_in,
    tr_s, tr_r, za_s, za_r, ring_s, ring_r, xg_s, xg_r, cs_s, cs_r, sq_s, sq_r,
    rs_s, rs_r, far_s, far_r, cx_s, cx_r, co_s, co_r, xo_s, xo_r, fn_s, fn_r,
):
    pair = lax.axis_index("pair")
    ten = lax.axis_index("tensor")
    x, z = pair // NZ, pair % NZ
    y, c = ten // NC, ten % NC

    def dev(xx, zz, yy, cc):
        return {"pair": xx * NZ + zz, "tensor": yy * NC + cc}

    def remote(src, dst, send, recv, where):
        return pltpu.make_async_remote_copy(
            src_ref=src, dst_ref=dst, send_sem=send, recv_sem=recv,
            device_id=where, device_id_type=MESH,
        )

    off_diagonal = x != y

    loads = [
        pltpu.make_async_copy(a, b, in_s.at[n])
        for n, (a, b) in enumerate(
            ((roll_h, roll), (wq_h, wq), (wk_h, wk), (wv_h, wv), (wo_h, wo))
        )
    ]
    for load in loads:
        load.start()

    barrier = pltpu.get_barrier_semaphore()

    def greet(where):
        pl.semaphore_signal(barrier, inc=1, device_id=where, device_id_type=MESH)

    @pl.loop(1, NZ)
    def _(k):
        greet(dev(x, (z + k) % NZ, y, c))

    @pl.loop(1, NX)
    def _(k):
        greet(dev((x + k) % NX, z, y, c))

    @pl.loop(1, NT)
    def _(k):
        greet({"pair": pair, "tensor": (ten + k) % NT})

    @pl.when(off_diagonal)
    def _():
        greet(dev(y, z, x, c))

    slots = NZ * SLOTS
    j = iota((slots, NX * NZ), 0)
    dest = ((j >> 2) & (NX - 1)) * NZ + (j >> 4)
    other = iota((slots, NX * NZ), 1)
    sending = counts[...].astype(F32)
    start = jnp.sum(jnp.where(other < dest, sending, 0.0), axis=1, keepdims=True)
    amount = jnp.sum(jnp.where(other == dest, sending, 0.0), axis=1, keepdims=True)
    k_slot = (iota((slots, 1), 0) & 3).astype(F32)
    spare = k_slot == CAP
    row_of = iota((slots, ROWS), 1).astype(F32)

    def picking(cond, k):
        return ones_where(jnp.where(cond & (amount > k), start + k, -1.0) == row_of)

    pick = picking(k_slot < CAP, k_slot)
    pick_tail = [picking(spare, float(k)) for k in range(CAP)]
    spot = iota((slots, 128), 1) - TAIL
    flags = jnp.where(
        spare & (spot >= 0) & (spot < CAP) & (spot.astype(F32) < amount), 1.0, 0.0
    )
    low[...] = jnp.zeros((ROWS, 128), BF16)
    loads[0].wait()
    low[:, 0:TAIL] = roll[:, 2 * SIDE:FEAT]
    low_tail = low[...]
    high_tail = pltpu.roll(low_tail.astype(F32), TAIL, 1).astype(BF16)
    base = dot(pick, roll[:, 0:2 * SIDE])
    tile0 = base[:, 0:128] + dot(pick_tail[0], low_tail) + dot(pick_tail[1], high_tail)
    tile1 = base[:, 128:256] + dot(pick_tail[2], low_tail) + flags
    zsend[0] = jnp.concatenate((tile0, tile1), axis=1).astype(BF16).reshape(NZ, SLOTS, SIDE)
    zsend[1] = base[:, SIDE:].astype(BF16).reshape(NZ, SLOTS, SIDE)
    for h in (0, 1):
        zrecv[h, z] = zsend[h, z]

    for load in loads[1:]:
        load.wait()

    def pack(p, first, second):
        wsend[p] = jnp.concatenate(
            (first.astype(F32), second.astype(F32)), axis=0
        ).astype(BF16)

    pack(0, wq[:, :HD], wq[:, HD:])
    pack(1, wk[...], wv[...])
    pack(2, wo[:, :HD], wo[:, HD:])
    lane = iota((8, 128), 1)
    spread = jnp.zeros((8, 128), I32)
    for k in range(RESP):
        spread = jnp.where(lane == k, pslot[0:1, k:k + 1], spread)
    slot_out[...] = spread

    greeted = NZ - 1 + NX - 1 + NT - 1

    @pl.when(off_diagonal)
    def _():
        pl.semaphore_wait(barrier, greeted + 1)

    @pl.when(jnp.logical_not(off_diagonal))
    def _():
        pl.semaphore_wait(barrier, greeted)

    def z_out(h, k):
        t = (z + k) % NZ
        return remote(
            zsend.at[h, t], zrecv.at[h, z], za_s.at[h, k], za_r.at[h, k], dev(x, t, y, c)
        )

    def z_in(h, k):
        f = (z + NZ - k) % NZ
        return remote(
            zsend.at[h, f], zrecv.at[h, f], za_s.at[h, k], za_r.at[h, k], dev(x, f, y, c)
        )

    def turned(first):
        if first:
            return remote(wsend, wbuf.at[z], tr_s.at[0], tr_r.at[0], dev(y, z, x, c))
        return remote(slot_out, slot_in, tr_s.at[1], tr_r.at[1], dev(y, z, x, c))

    @pl.when(off_diagonal)
    def _():
        turned(True).start()
        turned(False).start()

    for h in (0, 1):
        z_out(h, NZ // 2).start()

        @pl.loop(1, NZ // 2)
        def _(k):
            z_out(h, NZ // 2 - k).start()
            z_out(h, NZ // 2 + k).start()

    @pl.when(jnp.logical_not(off_diagonal))
    def _():
        wbuf[z] = wsend[...]
        slot_in[...] = slot_out[...]

    up, down = (z + 1) % NZ, (z + NZ - 1) % NZ

    def ring_block(d, s):
        return (z + NZ - s) % NZ if d == 0 else (z + s) % NZ

    def ring(p, d, s, distance):
        block = wbuf.at[ring_block(d, distance), p]
        return remote(
            block, block, ring_s.at[p, d, s], ring_r.at[p, d, s],
            dev(x, up if d == 0 else down, y, c),
        )

    def unpack(p, block):
        v = wbuf[block, p].astype(F32)
        at = pl.ds(pl.multiple_of(block * WROWS, 8), WROWS)
        w32[p, at, 0:HD] = v[:WROWS]
        w32[p, at, HD:2 * HD] = v[WROWS:]

    def ring_open(p):
        ring(p, 0, 0, 0).start()
        ring(p, 1, 0, 0).start()
        unpack(p, z)

    def ring_steps(pieces, low, high):
        @pl.loop(low, high)
        def _(s):
            for p in pieces:
                for d in (0, 1):
                    ring(p, d, s - 1, s).wait_recv()
                    ring(p, d, s, s).start()
            for p in pieces:
                for d in (0, 1):
                    unpack(p, ring_block(d, s))

    last = NZ // 2

    def ring_last_sends(pieces):
        for p in pieces:
            for d in (0, 1):
                ring(p, d, last - 2, last - 1).wait_recv()
            ring(p, 0, last - 1, last - 1).start()
        for p in pieces:
            for d in (0, 1):
                unpack(p, ring_block(d, last - 1))

    def ring_close(pieces):
        for p in pieces:
            ring(p, 0, last - 1, last).wait_recv()
            unpack(p, ring_block(0, last))

    @pl.when(off_diagonal)
    def _():
        turned(True).wait_recv()
        turned(False).wait_recv()

    pieces = (0, 1, 2)
    for p in pieces:
        ring_open(p)
    ring_steps(pieces, 1, 2)

    def z_wait(h):
        @pl.loop(1, NZ)
        def _(k):
            z_in(h, k).wait_recv()

    right, left = (x + 1) % NX, (x + NX - 1) % NX
    parts = (pl.ds(0, HALF), pl.ds(HALF, HALF))
    plan = (
        (0, 0, 1), (0, 1, 1), (1, 1, 1), (1, 0, 1), (0, 0, 2), (1, 1, 2),
    )
    held = (xg0, xg1)

    def x_block(d, distance):
        return (x + NX - distance) % NX if d == 0 else (x + distance) % NX

    def x_copy(h, n, distance):
        d, half, _ = plan[n]
        block = held[h].at[x_block(d, distance), parts[half]]
        return remote(
            block, block, xg_s.at[h, n], xg_r.at[h, n],
            dev(right if d == 0 else left, z, y, c),
        )

    def x_out(h, n):
        return x_copy(h, n, plan[n][2] - 1)

    def x_in(h, n):
        return x_copy(h, n, plan[n][2])

    def x_open(h):
        for n in (0, 2, 1, 3):
            x_out(h, n).start()

    def x_forward(h):
        x_in(h, 0).wait_recv()
        x_out(h, 4).start()
        x_in(h, 2).wait_recv()
        x_out(h, 5).start()

    def x_wait(h):
        for n in (1, 3, 4, 5):
            x_in(h, n).wait_recv()

    i = iota((ALL_SLOTS, slots), 0)
    q = (i * 171) >> 9
    at = iota((ALL_SLOTS, slots), 1) - (q & (NZ - 1)) * SLOTS - (q >> 4) * 4
    squeeze = ones_where(at == i - 3 * q)
    squeeze_spare = ones_where(at == CAP)
    i = iota((ALL_SLOTS, 128), 0)
    k_kept = i - 3 * ((i * 171) >> 9)
    lane = iota((ALL_SLOTS, 128), 1)

    z_wait(0)
    got = zrecv[0].reshape(slots, SIDE)
    spare_rows = dot(squeeze_spare, got)
    first, second = spare_rows[:, 0:128], spare_rows[:, 128:256]
    tail = jnp.where(
        k_kept == 0, first, jnp.where(k_kept == 1, pltpu.roll(first, TAIL, 1), second)
    )
    flag = jnp.sum(jnp.where(lane == TAIL + k_kept, second, 0.0), axis=1, keepdims=True)
    tail = jnp.where(lane < TAIL, tail, flag)
    xg0[x] = jnp.concatenate((dot(squeeze, got), tail), axis=1).astype(BF16)
    x_open(0)
    ring_steps(pieces, 2, 3)
    x_forward(0)
    z_wait(1)
    xg1[x] = dot(squeeze, zrecv[1].reshape(slots, SIDE)).astype(BF16)
    x_open(1)
    ring_steps(pieces, 3, 4)
    x_forward(1)
    ring_steps(pieces, 4, 5)
    x_wait(0)

    before = ones_where(iota((ALL_SLOTS, ALL_SLOTS), 0) < iota((ALL_SLOTS, ALL_SLOTS), 1))
    flag_lane = ones_where(iota((16, 128), 1) == TAIL)
    my_gain = gain[pl.ds(pl.multiple_of(y * NC * FEAT, 128), NC * FEAT)].reshape(1, NC * FEAT)
    my_gain = jnp.where(c == 0, my_gain[:, :FEAT], my_gain[:, FEAT:])
    table = jnp.zeros((8, 128), F32)
    sub = iota((8, 128), 0)

    def share(dx):
        return remote(
            xs.at[c, dx], xs.at[c, dx], cs_s.at[dx], cs_r.at[dx], dev(x, z, y, 1 - c)
        )

    def share_in(dx):
        return remote(
            xs.at[1 - c, dx], xs.at[1 - c, dx], cs_s.at[dx], cs_r.at[dx], dev(x, z, y, 1 - c)
        )

    def keep(dx, low_column, rows):
        high_column = low_column + rows.shape[1]
        judged[dx, :, low_column:high_column] = rows.astype(BF16)
        xs[c, dx, :, low_column:high_column] = (
            rows * my_gain[:, low_column:high_column]
        ).astype(BF16)
        return jnp.sum(rows * rows, axis=1, keepdims=True)

    places, sums = [], []
    for dx in range(NX):
        s = xg0[:, dx * KEPT:(dx + 1) * KEPT, :].reshape(ALL_SLOTS, WIDE)
        filled = dot(flag_lane, s[:, SIDE:WIDE], NTR)
        rank = dot(filled.astype(BF16), before)
        key = jnp.where(filled > 0.5, rank, -1.0)[0:1]
        place = ones_where(iota((ROWS, ALL_SLOTS), 0).astype(F32) == key)
        rows = dot(place, s)
        places.append(place)
        sums.append(
            keep(dx, 0, rows[:, 0:SIDE]) + keep(dx, 2 * SIDE, rows[:, SIDE:SIDE + TAIL])
        )

    ring_steps(pieces, 5, 6)
    x_wait(1)
    for dx in range(NX):
        s = xg1[:, dx * KEPT:(dx + 1) * KEPT, :].reshape(ALL_SLOTS, SIDE)
        total = sums[dx] + keep(dx, SIDE, dot(places[dx], s))
        share(dx).start()
        table = jnp.where(sub == dx, column_to_row(total), table)
        if dx == 1:
            ring_steps(pieces, 6, last - 1)

    sq_in[0] = table

    def squares_out(k):
        return remote(
            sq_in.at[0], sq_in.at[k], sq_s.at[k], sq_r.at[k],
            {"pair": pair, "tensor": (ten + k) % NT},
        )

    @pl.loop(1, NT)
    def _(k):
        squares_out(k).start()

    ring_last_sends(pieces)
    ring_close((0, 1))
    for dx in range(NX):
        share_in(dx).wait_recv()

    first = xs[0].reshape(NX * ROWS, FEAT)
    second = xs[1].reshape(NX * ROWS, FEAT)
    for p in (0, 1):
        w = w32[p].astype(BF16)
        t = dot(first, w[:FEAT]) + dot(second, w[FEAT:])
        part[:, :, p * 256:(p + 1) * 256] = t.astype(BF16).reshape(NX, ROWS, 256)

    def sum_out(k):
        t = (y + k) % NY
        return remote(part.at[t], part_in.at[k], rs_s.at[k], rs_r.at[k], dev(x, z, t, c))

    def far_out(k):
        t = (y + k) % NY
        return remote(
            part.at[(t + NY // 2) % NY, :, pl.ds(256, 256)], far_in.at[k],
            far_s.at[k], far_r.at[k], dev(x, z, t, c),
        )

    for k in (2, 1, 3):
        sum_out(k).start()
        far_out(k).start()

    ring_close((2,))

    @pl.loop(1, NT)
    def _(k):
        squares_out(k).wait_recv()

    total = sq_in[0]
    for k in range(1, NT):
        total = total + sq_in[k]
    far_y = (y + NY // 2) % NY
    width = float(NT * FEAT)

    def row_scale(which):
        row = jnp.sum(jnp.where(sub == which, total, 0.0), axis=0, keepdims=True)
        return lax.rsqrt(row_to_column(row, ROWS) / width + epsilon)

    scale_own, scale_far = row_scale(y), row_scale(far_y)
    for k in range(1, NY):
        sum_out(k).wait_recv()
        far_out(k).wait_recv()
    own = part[y].astype(F32)
    far = part[far_y, :, 256:512].astype(F32)
    for k in range(1, NY):
        own = own + part_in[k].astype(F32)
        far = far + far_in[k].astype(F32)
    own = (own * scale_own).astype(BF16)
    far = (far * scale_far).astype(BF16)

    queries = jnp.concatenate((own[:, 0:HD], own[:, HD:2 * HD]), axis=0)
    col = iota((2 * ROWS, ROWS), 1)
    row = iota((2 * ROWS, ROWS), 0)
    row = jnp.where(row >= ROWS, row - ROWS, row)
    resp_q, resp_k = row >> 5, col >> 5
    spot_q, spot_k = row & (LEN - 1), col & (LEN - 1)

    def by_response(resp, values):
        return jnp.where(resp == 0, values[0], jnp.where(resp == 1, values[1], values[2]))

    own_lens = [lens[(y * NZ + z) * RESP + k] for k in range(RESP)]
    far_lens = [lens[(far_y * NZ + z) * RESP + k] for k in range(RESP)]
    partner = by_response(resp_q, [slot_in[0:1, k:k + 1] for k in range(RESP)])
    own_ok = (resp_q == resp_k) & (spot_k <= spot_q) & (spot_k < by_response(resp_k, own_lens))
    far_ok = (partner == resp_k) & (spot_k < by_response(resp_k, far_lens))

    def powers(keys, ok):
        scores = dot(queries, keys, NTR) * score_scale
        scores = soft_cap * jnp.tanh(scores / soft_cap)
        return jnp.exp(jnp.where(ok, scores, negative))

    p_own = powers(own[:, 256:384], own_ok)
    p_far = powers(far[:, 0:HD], far_ok)
    whole = jnp.sum(p_own, axis=1, keepdims=True) + jnp.sum(p_far, axis=1, keepdims=True)
    mixed = dot((p_own / whole).astype(BF16), own[:, 384:512])
    mixed = mixed + dot((p_far / whole).astype(BF16), far[:, HD:2 * HD])
    row = iota((2 * ROWS, HD), 0)
    row = jnp.where(row >= ROWS, row - ROWS, row)
    present = (row & (LEN - 1)) < by_response(row >> 5, own_lens)
    mixed = jnp.where(present, mixed, 0.0).astype(BF16)
    ctx[y] = jnp.concatenate((mixed[:ROWS], mixed[ROWS:]), axis=1)

    def ctx_out(k):
        return remote(ctx.at[y], ctx.at[y], cx_s.at[k], cx_r.at[k], dev(x, z, (y + k) % NY, c))

    def ctx_in(k):
        f = (y + NY - k) % NY
        return remote(ctx.at[f], ctx.at[f], cx_s.at[k], cx_r.at[k], dev(x, z, f, c))

    for k in (2, 1, 3):
        ctx_out(k).start()

    def out_rows(half):
        return w32[2, pl.ds(pl.multiple_of(half * FEAT, 8), FEAT), :].astype(BF16)

    w_other, w_mine = out_rows(1 - c), out_rows(c)

    def swap(k):
        t = (y + NY - k) % NY
        return remote(
            co_out.at[t], co_in.at[t], co_s.at[k], co_r.at[k], dev(x, z, y, 1 - c)
        )

    def xsum(k):
        t = (x + k) % NX
        return remote(xo_out.at[t], xo_in.at[k], xo_s.at[k], xo_r.at[k], dev(t, z, y, c))

    order = (0, 1, 3, 2)
    for k in order:
        t = (y + NY - k) % NY
        if k > 0:
            ctx_in(k).wait_recv()
        co_out[t] = dot(ctx[t], w_other, NTR).astype(BF16)
        swap(k).start()
        xo_out[t] = dot(ctx[t], w_mine, NTR).astype(BF16)
    for k in order:
        t = (y + NY - k) % NY
        swap(k).wait_recv()
        xo_out[t] = (xo_out[t].astype(F32) + co_in[t].astype(F32)).astype(BF16)

        @pl.when(t != x)
        def _():
            xsum((t + NX - x) % NX).start()

    attended = xo_out[x].astype(F32)
    for k in (1, 3, 2):
        xsum(k).wait_recv()
        attended = attended + xo_in[k].astype(F32)

    squares = column_to_row(jnp.sum(attended * attended, axis=1, keepdims=True))
    fin_in[0] = jnp.where(sub == 0, squares, 0.0)

    def fin_out(k):
        return remote(
            fin_in.at[0], fin_in.at[k], fn_s.at[k], fn_r.at[k],
            {"pair": pair, "tensor": (ten + k) % NT},
        )

    @pl.loop(1, NT)
    def _(k):
        fin_out(k).start()

    @pl.when(off_diagonal)
    def _():
        turned(True).wait_send()
        turned(False).wait_send()

    for h in (0, 1):
        @pl.loop(1, NZ)
        def _(k):
            z_out(h, k).wait_send()

    for p in range(3):
        @pl.loop(0, NZ // 2 - 1)
        def _(s):
            ring(p, 0, s, s).wait_send()
            ring(p, 1, s, s).wait_send()

        ring(p, 0, NZ // 2 - 1, NZ // 2 - 1).wait_send()
    for h in (0, 1):
        for n in range(6):
            x_out(h, n).wait_send()
    for dx in range(NX):
        share(dx).wait_send()

    @pl.loop(1, NT)
    def _(k):
        squares_out(k).wait_send()

    for k in range(1, NY):
        sum_out(k).wait_send()
        far_out(k).wait_send()
        ctx_out(k).wait_send()
        xsum(k).wait_send()
    for k in order:
        swap(k).wait_send()

    residual = judged[x].astype(F32)
    gained = attended * post[...].reshape(1, FEAT)

    @pl.loop(1, NT)
    def _(k):
        fin_out(k).wait_recv()

    total = fin_in[0]
    for k in range(1, NT):
        total = total + fin_in[k]
    scale = lax.rsqrt(row_to_column(total[0:1], ROWS) / width + epsilon)
    out[...] = (residual + gained * scale).astype(BF16)

    @pl.loop(1, NT)
    def _(k):
        fin_out(k).wait_send()


def shards(
    rollout, counts, lengths, partner_slot, pre_gain, post_gain,
    query_weight, key_weight, value_weight, out_weight,
):
    vmem = pl.BlockSpec(memory_space=pltpu.VMEM)
    hbm = pl.BlockSpec(memory_space=pltpu.HBM)
    smem = pl.BlockSpec(memory_space=pltpu.SMEM)
    dma = pltpu.SemaphoreType.DMA
    scratch = [
        pltpu.VMEM((ROWS, FEAT), BF16),
        pltpu.VMEM((WROWS, 256), BF16),
        pltpu.VMEM((WROWS, HD), BF16),
        pltpu.VMEM((WROWS, HD), BF16),
        pltpu.VMEM((WROWS, 256), BF16),
        dma((5,)),
        pltpu.VMEM((ROWS, 128), BF16),
        pltpu.VMEM((2, NZ, SLOTS, SIDE), BF16),
        pltpu.VMEM((2, NZ, SLOTS, SIDE), BF16),
        pltpu.VMEM((3, 2 * WROWS, HD), BF16),
        pltpu.VMEM((NZ, 3, 2 * WROWS, HD), BF16),
        pltpu.VMEM((3, BLOCK, 2 * HD), F32),
        pltpu.VMEM((8, 128), I32),
        pltpu.VMEM((8, 128), I32),
        pltpu.VMEM((NX, ALL_SLOTS, WIDE), BF16),
        pltpu.VMEM((NX, ALL_SLOTS, SIDE), BF16),
        pltpu.VMEM((NC, NX, ROWS, FEAT), BF16),
        pltpu.VMEM((NX, ROWS, FEAT), BF16),
        pltpu.VMEM((NT, 8, 128), F32),
        pltpu.VMEM((NT, 8, 128), F32),
        pltpu.VMEM((NX, ROWS, 512), BF16),
        pltpu.VMEM((NY, ROWS, 512), BF16),
        pltpu.VMEM((NY, ROWS, 256), BF16),
        pltpu.VMEM((NY, ROWS, 256), BF16),
        pltpu.VMEM((NX, ROWS, FEAT), BF16),
        pltpu.VMEM((NX, ROWS, FEAT), BF16),
        pltpu.VMEM((NX, ROWS, FEAT), BF16),
        pltpu.VMEM((NX, ROWS, FEAT), BF16),
        dma((2,)), dma((2,)),
        dma((2, NZ)), dma((2, NZ)),
        dma((3, 2, NZ // 2)), dma((3, 2, NZ // 2)),
        dma((2, 6)), dma((2, 6)),
        dma((NX,)), dma((NX,)),
        dma((NT,)), dma((NT,)),
        dma((NY,)), dma((NY,)),
        dma((NY,)), dma((NY,)),
        dma((NY,)), dma((NY,)),
        dma((NX,)), dma((NX,)),
        dma((NX,)), dma((NX,)),
        dma((NT,)), dma((NT,)),
    ]
    return pl.pallas_call(
        kernel,
        out_shape=jax.ShapeDtypeStruct((ROWS, FEAT), BF16),
        in_specs=[hbm, vmem, smem, vmem, vmem, vmem, hbm, hbm, hbm, hbm],
        out_specs=vmem,
        scratch_shapes=scratch,
        compiler_params=pltpu.CompilerParams(
            collective_id=0, has_side_effects=True, vmem_limit_bytes=62 * 1024 * 1024
        ),
    )(
        rollout, counts, lengths, partner_slot, pre_gain,
        post_gain, query_weight, key_weight, value_weight, out_weight,
    )


def solution(mesh):
    placed = (
        P("pair", "tensor"),
        P("pair", None),
        P(),
        P("pair", None),
        P(),
        P("tensor"),
        P("pair", "tensor"),
        P("pair", "tensor"),
        P("pair", "tensor"),
        P("pair", "tensor"),
    )
    return jax.shard_map(
        shards, mesh=mesh, in_specs=placed, out_specs=P("pair", "tensor"), check_vma=False
    )
```

```python
import jax
import jax.numpy as jnp
from jax import lax
from jax.experimental import pallas as pl
from jax.experimental.pallas import tpu as pltpu
from jax.sharding import PartitionSpec as P

NX, NY, NZ, NC = 4, 4, 16, 2
NT = NY * NC
HD = 128
LEN = 32
RESP = 3
ROWS = RESP * LEN
FEAT = 576
SIDE = 256
TAIL = FEAT - 2 * SIDE
WIDE = SIDE + 128
WROWS = 72
BLOCK = NZ * WROWS
CAP = 3
SLOTS = NX * 4
KEPT = NZ * CAP
ALL_SLOTS = NX * KEPT
HALF = ALL_SLOTS // 2

score_scale = 144.0 ** (-0.5)
soft_cap = 50.0
epsilon = 1e-06
negative = -1e30

F32 = jnp.float32
BF16 = jnp.bfloat16
I32 = jnp.int32
MESH = pl.DeviceIdType.MESH
NN = (((1,), (0,)), ((), ()))
NTR = (((1,), (1,)), ((), ()))


def dot(a, b, dims=NN):
    return lax.dot_general(a, b, dims, preferred_element_type=F32)


def iota(shape, dim):
    return lax.broadcasted_iota(I32, shape, dim)


def ones_where(cond):
    return jnp.where(cond, 1.0, 0.0).astype(BF16)


def column_to_row(col):
    rows = col.shape[0]
    same = iota((rows, 128), 0) == iota((rows, 128), 1)
    return jnp.sum(jnp.where(same, col, 0.0), axis=0, keepdims=True)


def row_to_column(row, rows):
    same = iota((rows, 128), 0) == iota((rows, 128), 1)
    return jnp.sum(jnp.where(same, row, 0.0), axis=1, keepdims=True)


def kernel(
    roll_h, counts, lens, pslot, gain, post, wq_h, wk_h, wv_h, wo_h, out,
    roll, wq, wk, wv, wo, in_s, low, zsend, zrecv, wsend, wbuf, w32, slot_out, slot_in, xg0, xg1, xs, judged, sq_in, fin_in,
    part, part_in, ctx, co_out, co_in, xo_out, xo_in,
    tr_s, tr_r, za_s, za_r, ring_s, ring_r, xg_s, xg_r, cs_s, cs_r, sq_s, sq_r,
    rs_s, rs_r, cx_s, cx_r, co_s, co_r, xo_s, xo_r, fn_s, fn_r,
):
    pair = lax.axis_index("pair")
    ten = lax.axis_index("tensor")
    x, z = pair // NZ, pair % NZ
    y, c = ten // NC, ten % NC

    def dev(xx, zz, yy, cc):
        return {"pair": xx * NZ + zz, "tensor": yy * NC + cc}

    def remote(src, dst, send, recv, where):
        return pltpu.make_async_remote_copy(
            src_ref=src, dst_ref=dst, send_sem=send, recv_sem=recv,
            device_id=where, device_id_type=MESH,
        )

    off_diagonal = x != y

    loads = [
        pltpu.make_async_copy(a, b, in_s.at[n])
        for n, (a, b) in enumerate(
            ((roll_h, roll), (wq_h, wq), (wk_h, wk), (wv_h, wv), (wo_h, wo))
        )
    ]
    for load in loads:
        load.start()

    barrier = pltpu.get_barrier_semaphore()

    def greet(where):
        pl.semaphore_signal(barrier, inc=1, device_id=where, device_id_type=MESH)

    @pl.loop(1, NZ)
    def _(k):
        greet(dev(x, (z + k) % NZ, y, c))

    @pl.loop(1, NX)
    def _(k):
        greet(dev((x + k) % NX, z, y, c))

    @pl.loop(1, NT)
    def _(k):
        greet({"pair": pair, "tensor": (ten + k) % NT})

    @pl.when(off_diagonal)
    def _():
        greet(dev(y, z, x, c))

    slots = NZ * SLOTS
    j = iota((slots, NX * NZ), 0)
    dest = ((j >> 2) & (NX - 1)) * NZ + (j >> 4)
    other = iota((slots, NX * NZ), 1)
    sending = counts[...].astype(F32)
    start = jnp.sum(jnp.where(other < dest, sending, 0.0), axis=1, keepdims=True)
    amount = jnp.sum(jnp.where(other == dest, sending, 0.0), axis=1, keepdims=True)
    k_slot = (iota((slots, 1), 0) & 3).astype(F32)
    spare = k_slot == CAP
    row_of = iota((slots, ROWS), 1).astype(F32)

    def picking(cond, k):
        return ones_where(jnp.where(cond & (amount > k), start + k, -1.0) == row_of)

    pick = picking(k_slot < CAP, k_slot)
    pick_tail = [picking(spare, float(k)) for k in range(CAP)]
    spot = iota((slots, 128), 1) - TAIL
    flags = jnp.where(
        spare & (spot >= 0) & (spot < CAP) & (spot.astype(F32) < amount), 1.0, 0.0
    )
    low[...] = jnp.zeros((ROWS, 128), BF16)
    loads[0].wait()
    low[:, 0:TAIL] = roll[:, 2 * SIDE:FEAT]
    low_tail = low[...]
    high_tail = pltpu.roll(low_tail.astype(F32), TAIL, 1).astype(BF16)
    base = dot(pick, roll[:, 0:2 * SIDE])
    tile0 = base[:, 0:128] + dot(pick_tail[0], low_tail) + dot(pick_tail[1], high_tail)
    tile1 = base[:, 128:256] + dot(pick_tail[2], low_tail) + flags
    zsend[0] = jnp.concatenate((tile0, tile1), axis=1).astype(BF16).reshape(NZ, SLOTS, SIDE)
    zsend[1] = base[:, SIDE:].astype(BF16).reshape(NZ, SLOTS, SIDE)
    for h in (0, 1):
        zrecv[h, z] = zsend[h, z]

    for load in loads[1:]:
        load.wait()

    def pack(p, first, second):
        wsend[p] = jnp.concatenate(
            (first.astype(F32), second.astype(F32)), axis=0
        ).astype(BF16)

    pack(0, wq[:, :HD], wq[:, HD:])
    pack(1, wk[...], wv[...])
    pack(2, wo[:, :HD], wo[:, HD:])
    lane = iota((8, 128), 1)
    spread = jnp.zeros((8, 128), I32)
    for k in range(RESP):
        spread = jnp.where(lane == k, pslot[0:1, k:k + 1], spread)
    slot_out[...] = spread

    greeted = NZ - 1 + NX - 1 + NT - 1

    @pl.when(off_diagonal)
    def _():
        pl.semaphore_wait(barrier, greeted + 1)

    @pl.when(jnp.logical_not(off_diagonal))
    def _():
        pl.semaphore_wait(barrier, greeted)

    def z_out(h, k):
        t = (z + k) % NZ
        return remote(
            zsend.at[h, t], zrecv.at[h, z], za_s.at[h, k], za_r.at[h, k], dev(x, t, y, c)
        )

    def z_in(h, k):
        f = (z + NZ - k) % NZ
        return remote(
            zsend.at[h, f], zrecv.at[h, f], za_s.at[h, k], za_r.at[h, k], dev(x, f, y, c)
        )

    def turned(p):
        src, dst = (slot_out, slot_in) if p == 3 else (wsend.at[p], wbuf.at[z, p])
        return remote(src, dst, tr_s.at[p], tr_r.at[p], dev(y, z, x, c))

    @pl.when(off_diagonal)
    def _():
        for p in range(4):
            turned(p).start()

    for h in (0, 1):
        z_out(h, NZ // 2).start()

        @pl.loop(1, NZ // 2)
        def _(k):
            z_out(h, NZ // 2 - k).start()
            z_out(h, NZ // 2 + k).start()

    @pl.when(jnp.logical_not(off_diagonal))
    def _():
        wbuf[z] = wsend[...]
        slot_in[...] = slot_out[...]

    up, down = (z + 1) % NZ, (z + NZ - 1) % NZ

    def ring_block(d, s):
        return (z + NZ - s) % NZ if d == 0 else (z + s) % NZ

    def ring(p, d, s, distance):
        block = wbuf.at[ring_block(d, distance), p]
        return remote(
            block, block, ring_s.at[p, d, s], ring_r.at[p, d, s],
            dev(x, up if d == 0 else down, y, c),
        )

    def unpack(p, block):
        v = wbuf[block, p].astype(F32)
        at = pl.ds(pl.multiple_of(block * WROWS, 8), WROWS)
        w32[p, at, 0:HD] = v[:WROWS]
        w32[p, at, HD:2 * HD] = v[WROWS:]

    def ring_steps(pieces, low, high):
        @pl.loop(low, high)
        def _(s):
            for p in pieces:
                for d in (0, 1):
                    ring(p, d, s - 1, s).wait_recv()
                    ring(p, d, s, s).start()
            for p in pieces:
                for d in (0, 1):
                    unpack(p, ring_block(d, s))

    last = NZ // 2

    def ring_last_sends(pieces):
        for p in pieces:
            for d in (0, 1):
                ring(p, d, last - 2, last - 1).wait_recv()
            ring(p, 0, last - 1, last - 1).start()
        for p in pieces:
            for d in (0, 1):
                unpack(p, ring_block(d, last - 1))

    def ring_close(pieces):
        for p in pieces:
            ring(p, 0, last - 1, last).wait_recv()
            unpack(p, ring_block(0, last))

    pieces = (0, 1, 2)
    for p in pieces:
        @pl.when(off_diagonal)
        def _():
            turned(p).wait_recv()

        ring(p, 0, 0, 0).start()
        ring(p, 1, 0, 0).start()
    for p in pieces:
        unpack(p, z)

    @pl.when(off_diagonal)
    def _():
        turned(3).wait_recv()

    ring_steps(pieces, 1, 2)

    def z_wait(h):
        @pl.loop(1, NZ)
        def _(k):
            z_in(h, k).wait_recv()

    right, left = (x + 1) % NX, (x + NX - 1) % NX
    parts = (pl.ds(0, HALF), pl.ds(HALF, HALF))
    plan = (
        (0, 0, 1), (0, 1, 1), (1, 1, 1), (1, 0, 1), (0, 0, 2), (1, 1, 2),
    )
    held = (xg0, xg1)

    def x_block(d, distance):
        return (x + NX - distance) % NX if d == 0 else (x + distance) % NX

    def x_copy(h, n, distance):
        d, half, _ = plan[n]
        block = held[h].at[x_block(d, distance), parts[half]]
        return remote(
            block, block, xg_s.at[h, n], xg_r.at[h, n],
            dev(right if d == 0 else left, z, y, c),
        )

    def x_out(h, n):
        return x_copy(h, n, plan[n][2] - 1)

    def x_in(h, n):
        return x_copy(h, n, plan[n][2])

    def x_open(h):
        for n in (0, 2, 1, 3):
            x_out(h, n).start()

    def x_forward(h):
        x_in(h, 0).wait_recv()
        x_out(h, 4).start()
        x_in(h, 2).wait_recv()
        x_out(h, 5).start()

    def x_wait(h):
        for n in (1, 3, 4, 5):
            x_in(h, n).wait_recv()

    i = iota((ALL_SLOTS, slots), 0)
    q = (i * 171) >> 9
    at = iota((ALL_SLOTS, slots), 1) - (q & (NZ - 1)) * SLOTS - (q >> 4) * 4
    squeeze = ones_where(at == i - 3 * q)
    squeeze_spare = ones_where(at == CAP)
    i = iota((ALL_SLOTS, 128), 0)
    k_kept = i - 3 * ((i * 171) >> 9)
    lane = iota((ALL_SLOTS, 128), 1)

    z_wait(0)
    got = zrecv[0].reshape(slots, SIDE)
    spare_rows = dot(squeeze_spare, got)
    first, second = spare_rows[:, 0:128], spare_rows[:, 128:256]
    tail = jnp.where(
        k_kept == 0, first, jnp.where(k_kept == 1, pltpu.roll(first, TAIL, 1), second)
    )
    flag = jnp.sum(jnp.where(lane == TAIL + k_kept, second, 0.0), axis=1, keepdims=True)
    tail = jnp.where(lane < TAIL, tail, flag)
    xg0[x] = jnp.concatenate((dot(squeeze, got), tail), axis=1).astype(BF16)
    x_open(0)
    ring_steps(pieces, 2, 3)
    x_forward(0)
    ring_steps(pieces, 3, 4)
    z_wait(1)
    xg1[x] = dot(squeeze, zrecv[1].reshape(slots, SIDE)).astype(BF16)
    x_open(1)
    ring_steps(pieces, 4, 5)
    x_forward(1)
    x_wait(0)

    before = ones_where(iota((ALL_SLOTS, ALL_SLOTS), 0) < iota((ALL_SLOTS, ALL_SLOTS), 1))
    flag_lane = ones_where(iota((16, 128), 1) == TAIL)
    my_gain = gain[pl.ds(pl.multiple_of(y * NC * FEAT, 128), NC * FEAT)].reshape(1, NC * FEAT)
    my_gain = jnp.where(c == 0, my_gain[:, :FEAT], my_gain[:, FEAT:])
    table = jnp.zeros((8, 128), F32)
    sub = iota((8, 128), 0)

    def share(dx):
        return remote(
            xs.at[c, dx], xs.at[c, dx], cs_s.at[dx], cs_r.at[dx], dev(x, z, y, 1 - c)
        )

    def share_in(dx):
        return remote(
            xs.at[1 - c, dx], xs.at[1 - c, dx], cs_s.at[dx], cs_r.at[dx], dev(x, z, y, 1 - c)
        )

    def keep(dx, low_column, rows):
        high_column = low_column + rows.shape[1]
        judged[dx, :, low_column:high_column] = rows.astype(BF16)
        xs[c, dx, :, low_column:high_column] = (
            rows * my_gain[:, low_column:high_column]
        ).astype(BF16)
        return jnp.sum(rows * rows, axis=1, keepdims=True)

    places, sums = [], []
    for dx in range(NX):
        s = xg0[:, dx * KEPT:(dx + 1) * KEPT, :].reshape(ALL_SLOTS, WIDE)
        filled = dot(flag_lane, s[:, SIDE:WIDE], NTR)
        rank = dot(filled.astype(BF16), before)
        key = jnp.where(filled > 0.5, rank, -1.0)[0:1]
        place = ones_where(iota((ROWS, ALL_SLOTS), 0).astype(F32) == key)
        rows = dot(place, s)
        places.append(place)
        sums.append(
            keep(dx, 0, rows[:, 0:SIDE]) + keep(dx, 2 * SIDE, rows[:, SIDE:SIDE + TAIL])
        )
        if dx == 1:
            ring_steps(pieces, 5, 6)

    ring_steps(pieces, 6, last - 1)
    x_wait(1)
    for dx in range(NX):
        s = xg1[:, dx * KEPT:(dx + 1) * KEPT, :].reshape(ALL_SLOTS, SIDE)
        total = sums[dx] + keep(dx, SIDE, dot(places[dx], s))
        share(dx).start()
        table = jnp.where(sub == dx, column_to_row(total), table)
        if dx == 1:
            ring_last_sends(pieces)

    sq_in[0] = table

    def squares_out(k):
        return remote(
            sq_in.at[0], sq_in.at[k], sq_s.at[k], sq_r.at[k],
            {"pair": pair, "tensor": (ten + k) % NT},
        )

    @pl.loop(1, NT)
    def _(k):
        squares_out(k).start()

    ring_close((0, 1))
    for dx in range(NX):
        share_in(dx).wait_recv()

    first = xs[0].reshape(NX * ROWS, FEAT)
    second = xs[1].reshape(NX * ROWS, FEAT)
    def products(p):
        w = w32[p].astype(BF16)
        t = dot(first, w[:FEAT]) + dot(second, w[FEAT:])
        return t.astype(BF16).reshape(NX, ROWS, 256)

    def sum_out(n, k):
        t = (y + k) % NY
        src = (part.at[1, t], part.at[1, (t + NY // 2) % NY], part.at[0, t])[n]
        return remote(
            src, part_in.at[n, k], rs_s.at[n, k], rs_r.at[n, k], dev(x, z, t, c)
        )

    part[1] = products(1)
    for k in (2, 1, 3):
        for n in (0, 1):
            sum_out(n, k).start()
    part[0] = products(0)
    for k in (2, 1, 3):
        sum_out(2, k).start()

    ring_close((2,))

    @pl.loop(1, NT)
    def _(k):
        squares_out(k).wait_recv()

    total = sq_in[0]
    for k in range(1, NT):
        total = total + sq_in[k]
    far_y = (y + NY // 2) % NY
    width = float(NT * FEAT)

    def row_scale(which):
        row = jnp.sum(jnp.where(sub == which, total, 0.0), axis=0, keepdims=True)
        return lax.rsqrt(row_to_column(row, ROWS) / width + epsilon)

    scale_own, scale_far = row_scale(y), row_scale(far_y)
    for n in range(3):
        for k in range(1, NY):
            sum_out(n, k).wait_recv()
    kv, far, q_own = part[1, y].astype(F32), part[1, far_y].astype(F32), part[0, y].astype(F32)
    for k in range(1, NY):
        kv = kv + part_in[0, k].astype(F32)
        far = far + part_in[1, k].astype(F32)
        q_own = q_own + part_in[2, k].astype(F32)
    own = jnp.concatenate((q_own, kv), axis=1)
    own = (own * scale_own).astype(BF16)
    far = (far * scale_far).astype(BF16)

    queries = jnp.concatenate((own[:, 0:HD], own[:, HD:2 * HD]), axis=0)
    col = iota((2 * ROWS, ROWS), 1)
    row = iota((2 * ROWS, ROWS), 0)
    row = jnp.where(row >= ROWS, row - ROWS, row)
    resp_q, resp_k = row >> 5, col >> 5
    spot_q, spot_k = row & (LEN - 1), col & (LEN - 1)

    def by_response(resp, values):
        return jnp.where(resp == 0, values[0], jnp.where(resp == 1, values[1], values[2]))

    own_lens = [lens[(y * NZ + z) * RESP + k] for k in range(RESP)]
    far_lens = [lens[(far_y * NZ + z) * RESP + k] for k in range(RESP)]
    partner = by_response(resp_q, [slot_in[0:1, k:k + 1] for k in range(RESP)])
    own_ok = (resp_q == resp_k) & (spot_k <= spot_q) & (spot_k < by_response(resp_k, own_lens))
    far_ok = (partner == resp_k) & (spot_k < by_response(resp_k, far_lens))

    def powers(keys, ok):
        scores = dot(queries, keys, NTR) * score_scale
        scores = soft_cap * jnp.tanh(scores / soft_cap)
        return jnp.exp(jnp.where(ok, scores, negative))

    p_own = powers(own[:, 256:384], own_ok)
    p_far = powers(far[:, 0:HD], far_ok)
    whole = jnp.sum(p_own, axis=1, keepdims=True) + jnp.sum(p_far, axis=1, keepdims=True)
    mixed = dot((p_own / whole).astype(BF16), own[:, 384:512])
    mixed = mixed + dot((p_far / whole).astype(BF16), far[:, HD:2 * HD])
    row = iota((2 * ROWS, HD), 0)
    row = jnp.where(row >= ROWS, row - ROWS, row)
    present = (row & (LEN - 1)) < by_response(row >> 5, own_lens)
    mixed = jnp.where(present, mixed, 0.0).astype(BF16)
    ctx[y] = jnp.concatenate((mixed[:ROWS], mixed[ROWS:]), axis=1)

    def ctx_out(k):
        return remote(ctx.at[y], ctx.at[y], cx_s.at[k], cx_r.at[k], dev(x, z, (y + k) % NY, c))

    def ctx_in(k):
        f = (y + NY - k) % NY
        return remote(ctx.at[f], ctx.at[f], cx_s.at[k], cx_r.at[k], dev(x, z, f, c))

    for k in (2, 1, 3):
        ctx_out(k).start()

    def out_rows(half):
        return w32[2, pl.ds(pl.multiple_of(half * FEAT, 8), FEAT), :].astype(BF16)

    w_other, w_mine = out_rows(1 - c), out_rows(c)

    def swap(k):
        t = (y + NY - k) % NY
        return remote(
            co_out.at[t], co_in.at[t], co_s.at[k], co_r.at[k], dev(x, z, y, 1 - c)
        )

    def xsum(k):
        t = (x + k) % NX
        return remote(xo_out.at[t], xo_in.at[k], xo_s.at[k], xo_r.at[k], dev(t, z, y, c))

    order = (0, 1, 3, 2)
    for k in order:
        t = (y + NY - k) % NY
        if k > 0:
            ctx_in(k).wait_recv()
        co_out[t] = dot(ctx[t], w_other, NTR).astype(BF16)
        swap(k).start()
        xo_out[t] = dot(ctx[t], w_mine, NTR).astype(BF16)
    for k in order:
        t = (y + NY - k) % NY
        swap(k).wait_recv()
        xo_out[t] = (xo_out[t].astype(F32) + co_in[t].astype(F32)).astype(BF16)

        @pl.when(t != x)
        def _():
            xsum((t + NX - x) % NX).start()

    attended = xo_out[x].astype(F32)
    for k in (1, 3, 2):
        xsum(k).wait_recv()
        attended = attended + xo_in[k].astype(F32)

    squares = column_to_row(jnp.sum(attended * attended, axis=1, keepdims=True))
    fin_in[0] = jnp.where(sub == 0, squares, 0.0)

    def fin_out(k):
        return remote(
            fin_in.at[0], fin_in.at[k], fn_s.at[k], fn_r.at[k],
            {"pair": pair, "tensor": (ten + k) % NT},
        )

    @pl.loop(1, NT)
    def _(k):
        fin_out(k).start()

    @pl.when(off_diagonal)
    def _():
        for p in range(4):
            turned(p).wait_send()

    for h in (0, 1):
        @pl.loop(1, NZ)
        def _(k):
            z_out(h, k).wait_send()

    for p in range(3):
        @pl.loop(0, NZ // 2 - 1)
        def _(s):
            ring(p, 0, s, s).wait_send()
            ring(p, 1, s, s).wait_send()

        ring(p, 0, NZ // 2 - 1, NZ // 2 - 1).wait_send()
    for h in (0, 1):
        for n in range(6):
            x_out(h, n).wait_send()
    for dx in range(NX):
        share(dx).wait_send()

    @pl.loop(1, NT)
    def _(k):
        squares_out(k).wait_send()

    for k in range(1, NY):
        for n in range(3):
            sum_out(n, k).wait_send()
        ctx_out(k).wait_send()
        xsum(k).wait_send()
    for k in order:
        swap(k).wait_send()

    residual = judged[x].astype(F32)
    gained = attended * post[...].reshape(1, FEAT)

    @pl.loop(1, NT)
    def _(k):
        fin_out(k).wait_recv()

    total = fin_in[0]
    for k in range(1, NT):
        total = total + fin_in[k]
    scale = lax.rsqrt(row_to_column(total[0:1], ROWS) / width + epsilon)
    out[...] = (residual + gained * scale).astype(BF16)

    @pl.loop(1, NT)
    def _(k):
        fin_out(k).wait_send()


def shards(
    rollout, counts, lengths, partner_slot, pre_gain, post_gain,
    query_weight, key_weight, value_weight, out_weight,
):
    vmem = pl.BlockSpec(memory_space=pltpu.VMEM)
    hbm = pl.BlockSpec(memory_space=pltpu.HBM)
    smem = pl.BlockSpec(memory_space=pltpu.SMEM)
    dma = pltpu.SemaphoreType.DMA
    scratch = [
        pltpu.VMEM((ROWS, FEAT), BF16),
        pltpu.VMEM((WROWS, 256), BF16),
        pltpu.VMEM((WROWS, HD), BF16),
        pltpu.VMEM((WROWS, HD), BF16),
        pltpu.VMEM((WROWS, 256), BF16),
        dma((5,)),
        pltpu.VMEM((ROWS, 128), BF16),
        pltpu.VMEM((2, NZ, SLOTS, SIDE), BF16),
        pltpu.VMEM((2, NZ, SLOTS, SIDE), BF16),
        pltpu.VMEM((3, 2 * WROWS, HD), BF16),
        pltpu.VMEM((NZ, 3, 2 * WROWS, HD), BF16),
        pltpu.VMEM((3, BLOCK, 2 * HD), F32),
        pltpu.VMEM((8, 128), I32),
        pltpu.VMEM((8, 128), I32),
        pltpu.VMEM((NX, ALL_SLOTS, WIDE), BF16),
        pltpu.VMEM((NX, ALL_SLOTS, SIDE), BF16),
        pltpu.VMEM((NC, NX, ROWS, FEAT), BF16),
        pltpu.VMEM((NX, ROWS, FEAT), BF16),
        pltpu.VMEM((NT, 8, 128), F32),
        pltpu.VMEM((NT, 8, 128), F32),
        pltpu.VMEM((2, NX, ROWS, 256), BF16),
        pltpu.VMEM((3, NY, ROWS, 256), BF16),
        pltpu.VMEM((NY, ROWS, 256), BF16),
        pltpu.VMEM((NX, ROWS, FEAT), BF16),
        pltpu.VMEM((NX, ROWS, FEAT), BF16),
        pltpu.VMEM((NX, ROWS, FEAT), BF16),
        pltpu.VMEM((NX, ROWS, FEAT), BF16),
        dma((4,)), dma((4,)),
        dma((2, NZ)), dma((2, NZ)),
        dma((3, 2, NZ // 2)), dma((3, 2, NZ // 2)),
        dma((2, 6)), dma((2, 6)),
        dma((NX,)), dma((NX,)),
        dma((NT,)), dma((NT,)),
        dma((3, NY)), dma((3, NY)),
        dma((NY,)), dma((NY,)),
        dma((NX,)), dma((NX,)),
        dma((NX,)), dma((NX,)),
        dma((NT,)), dma((NT,)),
    ]
    return pl.pallas_call(
        kernel,
        out_shape=jax.ShapeDtypeStruct((ROWS, FEAT), BF16),
        in_specs=[hbm, vmem, smem, vmem, vmem, vmem, hbm, hbm, hbm, hbm],
        out_specs=vmem,
        scratch_shapes=scratch,
        compiler_params=pltpu.CompilerParams(
            collective_id=0, has_side_effects=True, vmem_limit_bytes=62 * 1024 * 1024
        ),
    )(
        rollout, counts, lengths, partner_slot, pre_gain,
        post_gain, query_weight, key_weight, value_weight, out_weight,
    )


def solution(mesh):
    placed = (
        P("pair", "tensor"),
        P("pair", None),
        P(),
        P("pair", None),
        P(),
        P("tensor"),
        P("pair", "tensor"),
        P("pair", "tensor"),
        P("pair", "tensor"),
        P("pair", "tensor"),
    )
    return jax.shard_map(
        shards, mesh=mesh, in_specs=placed, out_specs=P("pair", "tensor"), check_vma=False
    )
```

```python
import jax
import jax.numpy as jnp
from jax import lax
from jax.experimental import pallas as pl
from jax.experimental.pallas import tpu as pltpu
from jax.sharding import PartitionSpec as P

NX, NY, NZ, NC = 4, 4, 16, 2
NT = NY * NC
HD = 128
LEN = 32
RESP = 3
ROWS = RESP * LEN
FEAT = 576
SIDE = 256
TAIL = FEAT - 2 * SIDE
WIDE = SIDE + 128
WROWS = 72
BLOCK = NZ * WROWS
CAP = 3
SLOTS = NX * 4
KEPT = NZ * CAP
ALL_SLOTS = NX * KEPT
HALF = ALL_SLOTS // 2

score_scale = 144.0 ** (-0.5)
soft_cap = 50.0
epsilon = 1e-06
negative = -1e30

F32 = jnp.float32
BF16 = jnp.bfloat16
I32 = jnp.int32
MESH = pl.DeviceIdType.MESH
NN = (((1,), (0,)), ((), ()))
NTR = (((1,), (1,)), ((), ()))


def dot(a, b, dims=NN):
    return lax.dot_general(a, b, dims, preferred_element_type=F32)


def iota(shape, dim):
    return lax.broadcasted_iota(I32, shape, dim)


def ones_where(cond):
    return jnp.where(cond, 1.0, 0.0).astype(BF16)


def column_to_row(col):
    rows = col.shape[0]
    same = iota((rows, 128), 0) == iota((rows, 128), 1)
    return jnp.sum(jnp.where(same, col, 0.0), axis=0, keepdims=True)


def row_to_column(row, rows):
    same = iota((rows, 128), 0) == iota((rows, 128), 1)
    return jnp.sum(jnp.where(same, row, 0.0), axis=1, keepdims=True)


def kernel(
    roll_h, counts, lens, pslot, gain, post, wq_h, wk_h, wv_h, wo_h, out,
    roll, wq, wk, wv, wo, in_s, low, zsend, zrecv, wsend, wbuf, w32, slot_out, slot_in, xg0, xg1, xs, judged, sq_in, fin_in,
    part, part_in, ctx, co_out, co_in, xo_out, xo_in,
    tr_s, tr_r, za_s, za_r, ring_s, ring_r, xg_s, xg_r, cs_s, cs_r, sq_s, sq_r,
    rs_s, rs_r, cx_s, cx_r, co_s, co_r, xo_s, xo_r, fn_s, fn_r,
):
    pair = lax.axis_index("pair")
    ten = lax.axis_index("tensor")
    x, z = pair >> 4, pair & (NZ - 1)
    y, c = ten >> 1, ten & (NC - 1)

    def dev(xx, zz, yy, cc):
        return {"pair": xx * NZ + zz, "tensor": yy * NC + cc}

    def remote(src, dst, send, recv, where):
        return pltpu.make_async_remote_copy(
            src_ref=src, dst_ref=dst, send_sem=send, recv_sem=recv,
            device_id=where, device_id_type=MESH,
        )

    off_diagonal = x != y

    loads = [
        pltpu.make_async_copy(a, b, in_s.at[n])
        for n, (a, b) in enumerate(
            ((roll_h, roll), (wq_h, wq), (wk_h, wk), (wv_h, wv), (wo_h, wo))
        )
    ]
    for load in loads:
        load.start()

    barrier = pltpu.get_barrier_semaphore()

    def greet(where):
        pl.semaphore_signal(barrier, inc=1, device_id=where, device_id_type=MESH)

    @pl.loop(1, NZ)
    def _(k):
        greet(dev(x, ((z + k) & (NZ - 1)), y, c))

    @pl.loop(1, NX)
    def _(k):
        greet(dev(((x + k) & (NX - 1)), z, y, c))

    @pl.loop(1, NT)
    def _(k):
        greet({"pair": pair, "tensor": ((ten + k) & (NT - 1))})

    @pl.when(off_diagonal)
    def _():
        greet(dev(y, z, x, c))

    slots = NZ * SLOTS
    j = iota((slots, NX * NZ), 0)
    dest = ((j >> 2) & (NX - 1)) * NZ + (j >> 4)
    other = iota((slots, NX * NZ), 1)
    sending = counts[...].astype(F32)
    start = jnp.sum(jnp.where(other < dest, sending, 0.0), axis=1, keepdims=True)
    amount = jnp.sum(jnp.where(other == dest, sending, 0.0), axis=1, keepdims=True)
    k_slot = (iota((slots, 1), 0) & 3).astype(F32)
    spare = k_slot == CAP
    row_of = iota((slots, ROWS), 1).astype(F32)

    def picking(cond, k):
        return ones_where(jnp.where(cond & (amount > k), start + k, -1.0) == row_of)

    pick = picking(k_slot < CAP, k_slot)
    pick_tail = [picking(spare, float(k)) for k in range(CAP)]
    spot = iota((slots, 128), 1) - TAIL
    flags = jnp.where(
        spare & (spot >= 0) & (spot < CAP) & (spot.astype(F32) < amount), 1.0, 0.0
    )
    low[...] = jnp.zeros((ROWS, 128), BF16)
    loads[0].wait()
    low[:, 0:TAIL] = roll[:, 2 * SIDE:FEAT]
    low_tail = low[...]
    high_tail = pltpu.roll(low_tail.astype(F32), TAIL, 1).astype(BF16)
    base = dot(pick, roll[:, 0:2 * SIDE])
    tile0 = base[:, 0:128] + dot(pick_tail[0], low_tail) + dot(pick_tail[1], high_tail)
    tile1 = base[:, 128:256] + dot(pick_tail[2], low_tail) + flags
    zsend[0] = jnp.concatenate((tile0, tile1), axis=1).astype(BF16).reshape(NZ, SLOTS, SIDE)
    zsend[1] = base[:, SIDE:].astype(BF16).reshape(NZ, SLOTS, SIDE)
    for h in (0, 1):
        zrecv[h, z] = zsend[h, z]

    for load in loads[1:]:
        load.wait()

    def pack(p, first, second):
        wsend[p] = jnp.concatenate(
            (first.astype(F32), second.astype(F32)), axis=0
        ).astype(BF16)

    pack(0, wq[:, :HD], wq[:, HD:])
    pack(1, wk[...], wv[...])
    pack(2, wo[:, :HD], wo[:, HD:])
    lane = iota((8, 128), 1)
    spread = jnp.zeros((8, 128), I32)
    for k in range(RESP):
        spread = jnp.where(lane == k, pslot[0:1, k:k + 1], spread)
    slot_out[...] = spread

    greeted = NZ - 1 + NX - 1 + NT - 1

    @pl.when(off_diagonal)
    def _():
        pl.semaphore_wait(barrier, greeted + 1)

    @pl.when(jnp.logical_not(off_diagonal))
    def _():
        pl.semaphore_wait(barrier, greeted)

    def z_out(h, k):
        t = ((z + k) & (NZ - 1))
        return remote(
            zsend.at[h, t], zrecv.at[h, z], za_s.at[h, k], za_r.at[h, k], dev(x, t, y, c)
        )

    def z_in(h, k):
        f = ((z + NZ - k) & (NZ - 1))
        return remote(
            zsend.at[h, f], zrecv.at[h, f], za_s.at[h, k], za_r.at[h, k], dev(x, f, y, c)
        )

    def turned(p):
        src, dst = (slot_out, slot_in) if p == 3 else (wsend.at[p], wbuf.at[z, p])
        return remote(src, dst, tr_s.at[p], tr_r.at[p], dev(y, z, x, c))

    @pl.when(off_diagonal)
    def _():
        for p in range(4):
            turned(p).start()

    for h in (0, 1):
        z_out(h, NZ // 2).start()

        @pl.loop(1, NZ // 2)
        def _(k):
            z_out(h, NZ // 2 - k).start()
            z_out(h, NZ // 2 + k).start()

    @pl.when(jnp.logical_not(off_diagonal))
    def _():
        wbuf[z] = wsend[...]
        slot_in[...] = slot_out[...]

    up, down = ((z + 1) & (NZ - 1)), ((z + NZ - 1) & (NZ - 1))

    def ring_block(d, s):
        return ((z + NZ - s) & (NZ - 1)) if d == 0 else ((z + s) & (NZ - 1))

    def ring(p, d, s, distance):
        block = wbuf.at[ring_block(d, distance), p]
        return remote(
            block, block, ring_s.at[p, d, s], ring_r.at[p, d, s],
            dev(x, up if d == 0 else down, y, c),
        )

    def unpack(p, block):
        v = wbuf[block, p].astype(F32)
        at = pl.ds(pl.multiple_of(block * WROWS, 8), WROWS)
        w32[p, at, 0:HD] = v[:WROWS]
        w32[p, at, HD:2 * HD] = v[WROWS:]

    def ring_steps(pieces, low, high):
        @pl.loop(low, high)
        def _(s):
            for p in pieces:
                for d in (0, 1):
                    ring(p, d, s - 1, s).wait_recv()
                    ring(p, d, s, s).start()
            for p in pieces:
                for d in (0, 1):
                    unpack(p, ring_block(d, s))

    last = NZ // 2

    def ring_last_sends(pieces):
        for p in pieces:
            for d in (0, 1):
                ring(p, d, last - 2, last - 1).wait_recv()
            ring(p, 0, last - 1, last - 1).start()
        for p in pieces:
            for d in (0, 1):
                unpack(p, ring_block(d, last - 1))

    def ring_close(pieces):
        for p in pieces:
            ring(p, 0, last - 1, last).wait_recv()
            unpack(p, ring_block(0, last))

    pieces = (0, 1, 2)
    for p in pieces:
        @pl.when(off_diagonal)
        def _():
            turned(p).wait_recv()

        ring(p, 0, 0, 0).start()
        ring(p, 1, 0, 0).start()
    for p in pieces:
        unpack(p, z)

    @pl.when(off_diagonal)
    def _():
        turned(3).wait_recv()

    ring_steps(pieces, 1, 2)

    def z_wait(h):
        @pl.loop(1, NZ)
        def _(k):
            z_in(h, k).wait_recv()

    right, left = ((x + 1) & (NX - 1)), ((x + NX - 1) & (NX - 1))
    parts = (pl.ds(0, HALF), pl.ds(HALF, HALF))
    plan = (
        (0, 0, 1), (0, 1, 1), (1, 1, 1), (1, 0, 1), (0, 0, 2), (1, 1, 2),
    )
    held = (xg0, xg1)

    def x_block(d, distance):
        return ((x + NX - distance) & (NX - 1)) if d == 0 else ((x + distance) & (NX - 1))

    def x_copy(h, n, distance):
        d, half, _ = plan[n]
        block = held[h].at[x_block(d, distance), parts[half]]
        return remote(
            block, block, xg_s.at[h, n], xg_r.at[h, n],
            dev(right if d == 0 else left, z, y, c),
        )

    def x_out(h, n):
        return x_copy(h, n, plan[n][2] - 1)

    def x_in(h, n):
        return x_copy(h, n, plan[n][2])

    def x_open(h):
        for n in (0, 2, 1, 3):
            x_out(h, n).start()

    def x_forward(h):
        x_in(h, 0).wait_recv()
        x_out(h, 4).start()
        x_in(h, 2).wait_recv()
        x_out(h, 5).start()

    def x_wait(h):
        for n in (1, 3, 4, 5):
            x_in(h, n).wait_recv()

    i = iota((ALL_SLOTS, slots), 0)
    q = (i * 171) >> 9
    at = iota((ALL_SLOTS, slots), 1) - (q & (NZ - 1)) * SLOTS - (q >> 4) * 4
    squeeze = ones_where(at == i - 3 * q)
    squeeze_spare = ones_where(at == CAP)
    i = iota((ALL_SLOTS, 128), 0)
    k_kept = i - 3 * ((i * 171) >> 9)
    lane = iota((ALL_SLOTS, 128), 1)

    z_wait(0)
    got = zrecv[0].reshape(slots, SIDE)
    spare_rows = dot(squeeze_spare, got)
    first, second = spare_rows[:, 0:128], spare_rows[:, 128:256]
    tail = jnp.where(
        k_kept == 0, first, jnp.where(k_kept == 1, pltpu.roll(first, TAIL, 1), second)
    )
    flag = jnp.sum(jnp.where(lane == TAIL + k_kept, second, 0.0), axis=1, keepdims=True)
    tail = jnp.where(lane < TAIL, tail, flag)
    xg0[x] = jnp.concatenate((dot(squeeze, got), tail), axis=1).astype(BF16)
    x_open(0)
    ring_steps(pieces, 2, 3)
    x_forward(0)
    ring_steps(pieces, 3, 4)
    z_wait(1)
    xg1[x] = dot(squeeze, zrecv[1].reshape(slots, SIDE)).astype(BF16)
    x_open(1)
    ring_steps(pieces, 4, 5)
    x_forward(1)
    x_wait(0)

    before = ones_where(iota((ALL_SLOTS, ALL_SLOTS), 0) < iota((ALL_SLOTS, ALL_SLOTS), 1))
    flag_lane = ones_where(iota((16, 128), 1) == TAIL)
    my_gain = gain[pl.ds(pl.multiple_of(y * NC * FEAT, 128), NC * FEAT)].reshape(1, NC * FEAT)
    my_gain = jnp.where(c == 0, my_gain[:, :FEAT], my_gain[:, FEAT:])
    table = jnp.zeros((8, 128), F32)
    sub = iota((8, 128), 0)

    def share(dx):
        return remote(
            xs.at[c, dx], xs.at[c, dx], cs_s.at[dx], cs_r.at[dx], dev(x, z, y, 1 - c)
        )

    def share_in(dx):
        return remote(
            xs.at[1 - c, dx], xs.at[1 - c, dx], cs_s.at[dx], cs_r.at[dx], dev(x, z, y, 1 - c)
        )

    def keep(dx, low_column, rows):
        high_column = low_column + rows.shape[1]
        judged[dx, :, low_column:high_column] = rows.astype(BF16)
        xs[c, dx, :, low_column:high_column] = (
            rows * my_gain[:, low_column:high_column]
        ).astype(BF16)
        return jnp.sum(rows * rows, axis=1, keepdims=True)

    places, sums = [], []
    for dx in range(NX):
        s = xg0[:, dx * KEPT:(dx + 1) * KEPT, :].reshape(ALL_SLOTS, WIDE)
        filled = dot(flag_lane, s[:, SIDE:WIDE], NTR)
        rank = dot(filled.astype(BF16), before)
        key = jnp.where(filled > 0.5, rank, -1.0)[0:1]
        place = ones_where(iota((ROWS, ALL_SLOTS), 0).astype(F32) == key)
        rows = dot(place, s)
        places.append(place)
        sums.append(
            keep(dx, 0, rows[:, 0:SIDE]) + keep(dx, 2 * SIDE, rows[:, SIDE:SIDE + TAIL])
        )
        if dx == 1:
            ring_steps(pieces, 5, 6)

    ring_steps(pieces, 6, last - 1)
    x_wait(1)
    for dx in range(NX):
        s = xg1[:, dx * KEPT:(dx + 1) * KEPT, :].reshape(ALL_SLOTS, SIDE)
        total = sums[dx] + keep(dx, SIDE, dot(places[dx], s))
        share(dx).start()
        table = jnp.where(sub == dx, column_to_row(total), table)
        if dx == 1:
            ring_last_sends(pieces)

    sq_in[0] = table

    def squares_out(k):
        return remote(
            sq_in.at[0], sq_in.at[k], sq_s.at[k], sq_r.at[k],
            {"pair": pair, "tensor": ((ten + k) & (NT - 1))},
        )

    @pl.loop(1, NT)
    def _(k):
        squares_out(k).start()

    ring_close((0, 1))
    for dx in range(NX):
        share_in(dx).wait_recv()

    first = xs[0].reshape(NX * ROWS, FEAT)
    second = xs[1].reshape(NX * ROWS, FEAT)
    def products(p):
        w = w32[p].astype(BF16)
        t = dot(first, w[:FEAT]) + dot(second, w[FEAT:])
        return t.astype(BF16).reshape(NX, ROWS, 256)

    def sum_out(n, k):
        t = ((y + k) & (NY - 1))
        src = (part.at[1, t], part.at[1, ((t + NY // 2) & (NY - 1))], part.at[0, t])[n]
        return remote(
            src, part_in.at[n, k], rs_s.at[n, k], rs_r.at[n, k], dev(x, z, t, c)
        )

    part[1] = products(1)
    for k in (2, 1, 3):
        for n in (0, 1):
            sum_out(n, k).start()
    part[0] = products(0)
    for k in (2, 1, 3):
        sum_out(2, k).start()

    ring_close((2,))

    @pl.when(off_diagonal)
    def _():
        for p in range(4):
            turned(p).wait_send()

    for h in (0, 1):
        @pl.loop(1, NZ)
        def _(k):
            z_out(h, k).wait_send()

    for p in range(3):
        @pl.loop(0, NZ // 2 - 1)
        def _(s):
            ring(p, 0, s, s).wait_send()
            ring(p, 1, s, s).wait_send()

        ring(p, 0, NZ // 2 - 1, NZ // 2 - 1).wait_send()
    for h in (0, 1):
        for n in range(6):
            x_out(h, n).wait_send()
    for dx in range(NX):
        share(dx).wait_send()

    @pl.loop(1, NT)
    def _(k):
        squares_out(k).wait_send()

    @pl.loop(1, NT)
    def _(k):
        squares_out(k).wait_recv()

    total = sq_in[0]
    for k in range(1, NT):
        total = total + sq_in[k]
    far_y = ((y + NY // 2) & (NY - 1))
    width = float(NT * FEAT)

    def row_scale(which):
        row = jnp.sum(jnp.where(sub == which, total, 0.0), axis=0, keepdims=True)
        return lax.rsqrt(row_to_column(row, ROWS) / width + epsilon)

    scale_own, scale_far = row_scale(y), row_scale(far_y)
    for n in range(3):
        for k in range(1, NY):
            sum_out(n, k).wait_recv()
    kv, far, q_own = part[1, y].astype(F32), part[1, far_y].astype(F32), part[0, y].astype(F32)
    for k in range(1, NY):
        kv = kv + part_in[0, k].astype(F32)
        far = far + part_in[1, k].astype(F32)
        q_own = q_own + part_in[2, k].astype(F32)
    own = jnp.concatenate((q_own, kv), axis=1)
    own = (own * scale_own).astype(BF16)
    far = (far * scale_far).astype(BF16)

    queries = jnp.concatenate((own[:, 0:HD], own[:, HD:2 * HD]), axis=0)
    col = iota((2 * ROWS, ROWS), 1)
    row = iota((2 * ROWS, ROWS), 0)
    row = jnp.where(row >= ROWS, row - ROWS, row)
    resp_q, resp_k = row >> 5, col >> 5
    spot_q, spot_k = row & (LEN - 1), col & (LEN - 1)

    def by_response(resp, values):
        return jnp.where(resp == 0, values[0], jnp.where(resp == 1, values[1], values[2]))

    own_lens = [lens[(y * NZ + z) * RESP + k] for k in range(RESP)]
    far_lens = [lens[(far_y * NZ + z) * RESP + k] for k in range(RESP)]
    partner = by_response(resp_q, [slot_in[0:1, k:k + 1] for k in range(RESP)])
    own_ok = (resp_q == resp_k) & (spot_k <= spot_q) & (spot_k < by_response(resp_k, own_lens))
    far_ok = (partner == resp_k) & (spot_k < by_response(resp_k, far_lens))

    def powers(keys, ok):
        scores = dot(queries, keys, NTR) * score_scale
        scores = soft_cap * jnp.tanh(scores / soft_cap)
        return jnp.exp(jnp.where(ok, scores, negative))

    p_own = powers(own[:, 256:384], own_ok)
    p_far = powers(far[:, 0:HD], far_ok)
    whole = jnp.sum(p_own, axis=1, keepdims=True) + jnp.sum(p_far, axis=1, keepdims=True)
    mixed = dot((p_own / whole).astype(BF16), own[:, 384:512])
    mixed = mixed + dot((p_far / whole).astype(BF16), far[:, HD:2 * HD])
    row = iota((2 * ROWS, HD), 0)
    row = jnp.where(row >= ROWS, row - ROWS, row)
    present = (row & (LEN - 1)) < by_response(row >> 5, own_lens)
    mixed = jnp.where(present, mixed, 0.0).astype(BF16)
    ctx[y] = jnp.concatenate((mixed[:ROWS], mixed[ROWS:]), axis=1)

    def ctx_out(k):
        return remote(ctx.at[y], ctx.at[y], cx_s.at[k], cx_r.at[k], dev(x, z, ((y + k) & (NY - 1)), c))

    def ctx_in(k):
        f = ((y + NY - k) & (NY - 1))
        return remote(ctx.at[f], ctx.at[f], cx_s.at[k], cx_r.at[k], dev(x, z, f, c))

    for k in (2, 1, 3):
        ctx_out(k).start()

    def out_rows(half):
        return w32[2, pl.ds(pl.multiple_of(half * FEAT, 8), FEAT), :].astype(BF16)

    w_other, w_mine = out_rows(1 - c), out_rows(c)

    def swap(k):
        t = ((y + NY - k) & (NY - 1))
        return remote(
            co_out.at[t], co_in.at[t], co_s.at[k], co_r.at[k], dev(x, z, y, 1 - c)
        )

    def xsum(k):
        t = ((x + k) & (NX - 1))
        return remote(xo_out.at[t], xo_in.at[k], xo_s.at[k], xo_r.at[k], dev(t, z, y, c))

    order = (0, 1, 3, 2)
    for k in order:
        t = ((y + NY - k) & (NY - 1))
        if k > 0:
            ctx_in(k).wait_recv()
        co_out[t] = dot(ctx[t], w_other, NTR).astype(BF16)
        swap(k).start()
        xo_out[t] = dot(ctx[t], w_mine, NTR).astype(BF16)
    for k in order:
        t = ((y + NY - k) & (NY - 1))
        swap(k).wait_recv()
        xo_out[t] = (xo_out[t].astype(F32) + co_in[t].astype(F32)).astype(BF16)

        @pl.when(t != x)
        def _():
            xsum(((t + NX - x) & (NX - 1))).start()

    attended = xo_out[x].astype(F32)
    for k in (1, 3, 2):
        xsum(k).wait_recv()
        attended = attended + xo_in[k].astype(F32)

    squares = column_to_row(jnp.sum(attended * attended, axis=1, keepdims=True))
    fin_in[0] = jnp.where(sub == 0, squares, 0.0)

    def fin_out(k):
        return remote(
            fin_in.at[0], fin_in.at[k], fn_s.at[k], fn_r.at[k],
            {"pair": pair, "tensor": ((ten + k) & (NT - 1))},
        )

    @pl.loop(1, NT)
    def _(k):
        fin_out(k).start()

    for k in range(1, NY):
        for n in range(3):
            sum_out(n, k).wait_send()
        ctx_out(k).wait_send()
        xsum(k).wait_send()
    for k in order:
        swap(k).wait_send()

    residual = judged[x].astype(F32)
    gained = attended * post[...].reshape(1, FEAT)

    @pl.loop(1, NT)
    def _(k):
        fin_out(k).wait_recv()

    total = fin_in[0]
    for k in range(1, NT):
        total = total + fin_in[k]
    scale = lax.rsqrt(row_to_column(total[0:1], ROWS) / width + epsilon)
    out[...] = (residual + gained * scale).astype(BF16)

    @pl.loop(1, NT)
    def _(k):
        fin_out(k).wait_send()


def shards(
    rollout, counts, lengths, partner_slot, pre_gain, post_gain,
    query_weight, key_weight, value_weight, out_weight,
):
    vmem = pl.BlockSpec(memory_space=pltpu.VMEM)
    hbm = pl.BlockSpec(memory_space=pltpu.HBM)
    smem = pl.BlockSpec(memory_space=pltpu.SMEM)
    dma = pltpu.SemaphoreType.DMA
    scratch = [
        pltpu.VMEM((ROWS, FEAT), BF16),
        pltpu.VMEM((WROWS, 256), BF16),
        pltpu.VMEM((WROWS, HD), BF16),
        pltpu.VMEM((WROWS, HD), BF16),
        pltpu.VMEM((WROWS, 256), BF16),
        dma((5,)),
        pltpu.VMEM((ROWS, 128), BF16),
        pltpu.VMEM((2, NZ, SLOTS, SIDE), BF16),
        pltpu.VMEM((2, NZ, SLOTS, SIDE), BF16),
        pltpu.VMEM((3, 2 * WROWS, HD), BF16),
        pltpu.VMEM((NZ, 3, 2 * WROWS, HD), BF16),
        pltpu.VMEM((3, BLOCK, 2 * HD), F32),
        pltpu.VMEM((8, 128), I32),
        pltpu.VMEM((8, 128), I32),
        pltpu.VMEM((NX, ALL_SLOTS, WIDE), BF16),
        pltpu.VMEM((NX, ALL_SLOTS, SIDE), BF16),
        pltpu.VMEM((NC, NX, ROWS, FEAT), BF16),
        pltpu.VMEM((NX, ROWS, FEAT), BF16),
        pltpu.VMEM((NT, 8, 128), F32),
        pltpu.VMEM((NT, 8, 128), F32),
        pltpu.VMEM((2, NX, ROWS, 256), BF16),
        pltpu.VMEM((3, NY, ROWS, 256), BF16),
        pltpu.VMEM((NY, ROWS, 256), BF16),
        pltpu.VMEM((NX, ROWS, FEAT), BF16),
        pltpu.VMEM((NX, ROWS, FEAT), BF16),
        pltpu.VMEM((NX, ROWS, FEAT), BF16),
        pltpu.VMEM((NX, ROWS, FEAT), BF16),
        dma((4,)), dma((4,)),
        dma((2, NZ)), dma((2, NZ)),
        dma((3, 2, NZ // 2)), dma((3, 2, NZ // 2)),
        dma((2, 6)), dma((2, 6)),
        dma((NX,)), dma((NX,)),
        dma((NT,)), dma((NT,)),
        dma((3, NY)), dma((3, NY)),
        dma((NY,)), dma((NY,)),
        dma((NX,)), dma((NX,)),
        dma((NX,)), dma((NX,)),
        dma((NT,)), dma((NT,)),
    ]
    return pl.pallas_call(
        kernel,
        out_shape=jax.ShapeDtypeStruct((ROWS, FEAT), BF16),
        in_specs=[hbm, vmem, smem, vmem, vmem, vmem, hbm, hbm, hbm, hbm],
        out_specs=vmem,
        scratch_shapes=scratch,
        compiler_params=pltpu.CompilerParams(
            collective_id=0, has_side_effects=True, vmem_limit_bytes=62 * 1024 * 1024
        ),
    )(
        rollout, counts, lengths, partner_slot, pre_gain,
        post_gain, query_weight, key_weight, value_weight, out_weight,
    )


def solution(mesh):
    placed = (
        P("pair", "tensor"),
        P("pair", None),
        P(),
        P("pair", None),
        P(),
        P("tensor"),
        P("pair", "tensor"),
        P("pair", "tensor"),
        P("pair", "tensor"),
        P("pair", "tensor"),
    )
    return jax.shard_map(
        shards, mesh=mesh, in_specs=placed, out_specs=P("pair", "tensor"), check_vma=False
    )
```

```python
import jax
import jax.numpy as jnp
from jax import lax
from jax.experimental import pallas as pl
from jax.experimental.pallas import tpu as pltpu
from jax.sharding import PartitionSpec as P

NX, NY, NZ, NC = 4, 4, 16, 2
NT = NY * NC
HD = 128
LEN = 32
RESP = 3
ROWS = RESP * LEN
FEAT = 576
SIDE = 256
TAIL = FEAT - 2 * SIDE
WIDE = SIDE + 128
WROWS = 72
BLOCK = NZ * WROWS
CAP = 3
SLOTS = NX * 4
KEPT = NZ * CAP
ALL_SLOTS = NX * KEPT

score_scale = 144.0 ** (-0.5)
soft_cap = 50.0
epsilon = 1e-06
negative = -1e30

F32 = jnp.float32
BF16 = jnp.bfloat16
I32 = jnp.int32
MESH = pl.DeviceIdType.MESH
NN = (((1,), (0,)), ((), ()))
NTR = (((1,), (1,)), ((), ()))


def dot(a, b, dims=NN):
    return lax.dot_general(a, b, dims, preferred_element_type=F32)


def iota(shape, dim):
    return lax.broadcasted_iota(I32, shape, dim)


def ones_where(cond):
    return jnp.where(cond, 1.0, 0.0).astype(BF16)


def column_to_row(col):
    rows = col.shape[0]
    same = iota((rows, 128), 0) == iota((rows, 128), 1)
    return jnp.sum(jnp.where(same, col, 0.0), axis=0, keepdims=True)


def row_to_column(row, rows):
    same = iota((rows, 128), 0) == iota((rows, 128), 1)
    return jnp.sum(jnp.where(same, row, 0.0), axis=1, keepdims=True)


def kernel(
    roll_h, counts, lens, pslot, gain, post, wq_h, wk_h, wv_h, wo_h, out,
    roll, wq, wk, wv, wo, in_s, low, zsend, zrecv, wsend, wbuf, w32, slot_out, slot_in, xg0, xg1, xs, judged, sq_in, fin_in,
    part, part_in, ctx, co_out, co_in, xo_out, xo_in,
    tr_s, tr_r, za_s, za_r, ring_s, ring_r, xg_s, xg_r, cs_s, cs_r, sq_s, sq_r,
    rs_s, rs_r, cx_s, cx_r, co_s, co_r, xo_s, xo_r, fn_s, fn_r,
):
    pair = lax.axis_index("pair")
    ten = lax.axis_index("tensor")
    x, z = pair >> 4, pair & (NZ - 1)
    y, c = ten >> 1, ten & (NC - 1)

    def dev(xx, zz, yy, cc):
        return {"pair": xx * NZ + zz, "tensor": yy * NC + cc}

    def remote(src, dst, send, recv, where):
        return pltpu.make_async_remote_copy(
            src_ref=src, dst_ref=dst, send_sem=send, recv_sem=recv,
            device_id=where, device_id_type=MESH,
        )

    off_diagonal = x != y

    loads = [
        pltpu.make_async_copy(a, b, in_s.at[n])
        for n, (a, b) in enumerate(
            ((roll_h, roll), (wq_h, wq), (wk_h, wk), (wv_h, wv), (wo_h, wo))
        )
    ]
    for load in loads:
        load.start()

    barrier = pltpu.get_barrier_semaphore()

    def greet(where):
        pl.semaphore_signal(barrier, inc=1, device_id=where, device_id_type=MESH)

    @pl.loop(1, NZ)
    def _(k):
        greet(dev(x, ((z + k) & (NZ - 1)), y, c))

    @pl.loop(1, NX)
    def _(k):
        greet(dev(((x + k) & (NX - 1)), z, y, c))

    @pl.loop(1, NT)
    def _(k):
        greet({"pair": pair, "tensor": ((ten + k) & (NT - 1))})

    @pl.when(off_diagonal)
    def _():
        greet(dev(y, z, x, c))

    slots = NZ * SLOTS
    j = iota((slots, NX * NZ), 0)
    dest = ((j >> 2) & (NX - 1)) * NZ + (j >> 4)
    other = iota((slots, NX * NZ), 1)
    sending = counts[...].astype(F32)
    start = jnp.sum(jnp.where(other < dest, sending, 0.0), axis=1, keepdims=True)
    amount = jnp.sum(jnp.where(other == dest, sending, 0.0), axis=1, keepdims=True)
    k_slot = (iota((slots, 1), 0) & 3).astype(F32)
    spare = k_slot == CAP
    row_of = iota((slots, ROWS), 1).astype(F32)

    def picking(cond, k):
        return ones_where(jnp.where(cond & (amount > k), start + k, -1.0) == row_of)

    pick = picking(k_slot < CAP, k_slot)
    pick_tail = [picking(spare, float(k)) for k in range(CAP)]
    spot = iota((slots, 128), 1) - TAIL
    flags = jnp.where(
        spare & (spot >= 0) & (spot < CAP) & (spot.astype(F32) < amount), 1.0, 0.0
    )
    low[...] = jnp.zeros((ROWS, 128), BF16)
    loads[0].wait()
    low[:, 0:TAIL] = roll[:, 2 * SIDE:FEAT]
    low_tail = low[...]
    high_tail = pltpu.roll(low_tail.astype(F32), TAIL, 1).astype(BF16)
    base = dot(pick, roll[:, 0:2 * SIDE])
    tile0 = base[:, 0:128] + dot(pick_tail[0], low_tail) + dot(pick_tail[1], high_tail)
    tile1 = base[:, 128:256] + dot(pick_tail[2], low_tail) + flags
    zsend[0] = jnp.concatenate((tile0, tile1), axis=1).astype(BF16).reshape(NZ, SLOTS, SIDE)
    zsend[1] = base[:, SIDE:].astype(BF16).reshape(NZ, SLOTS, SIDE)
    for h in (0, 1):
        zrecv[h, z] = zsend[h, z]

    for load in loads[1:]:
        load.wait()

    def pack(p, first, second):
        wsend[p] = jnp.concatenate(
            (first.astype(F32), second.astype(F32)), axis=0
        ).astype(BF16)

    pack(0, wq[:, :HD], wq[:, HD:])
    pack(1, wk[...], wv[...])
    pack(2, wo[:, :HD], wo[:, HD:])
    lane = iota((8, 128), 1)
    spread = jnp.zeros((8, 128), I32)
    for k in range(RESP):
        spread = jnp.where(lane == k, pslot[0:1, k:k + 1], spread)
    slot_out[...] = spread

    greeted = NZ - 1 + NX - 1 + NT - 1

    @pl.when(off_diagonal)
    def _():
        pl.semaphore_wait(barrier, greeted + 1)

    @pl.when(jnp.logical_not(off_diagonal))
    def _():
        pl.semaphore_wait(barrier, greeted)

    def z_out(h, k):
        t = ((z + k) & (NZ - 1))
        return remote(
            zsend.at[h, t], zrecv.at[h, z], za_s.at[h, k], za_r.at[h, k], dev(x, t, y, c)
        )

    def z_in(h, k):
        f = ((z + NZ - k) & (NZ - 1))
        return remote(
            zsend.at[h, f], zrecv.at[h, f], za_s.at[h, k], za_r.at[h, k], dev(x, f, y, c)
        )

    def turned(p):
        src, dst = (slot_out, slot_in) if p == 3 else (wsend.at[p], wbuf.at[z, p])
        return remote(src, dst, tr_s.at[p], tr_r.at[p], dev(y, z, x, c))

    @pl.when(off_diagonal)
    def _():
        for p in range(4):
            turned(p).start()

    for h in (0, 1):
        z_out(h, NZ // 2).start()

        @pl.loop(1, NZ // 2)
        def _(k):
            z_out(h, NZ // 2 - k).start()
            z_out(h, NZ // 2 + k).start()

    @pl.when(jnp.logical_not(off_diagonal))
    def _():
        wbuf[z] = wsend[...]
        slot_in[...] = slot_out[...]

    up, down = ((z + 1) & (NZ - 1)), ((z + NZ - 1) & (NZ - 1))

    def ring_block(d, s):
        return ((z + NZ - s) & (NZ - 1)) if d == 0 else ((z + s) & (NZ - 1))

    def ring(p, d, s, distance):
        block = wbuf.at[ring_block(d, distance), p]
        return remote(
            block, block, ring_s.at[p, d, s], ring_r.at[p, d, s],
            dev(x, up if d == 0 else down, y, c),
        )

    def unpack(p, block):
        v = wbuf[block, p].astype(F32)
        at = pl.ds(pl.multiple_of(block * WROWS, 8), WROWS)
        w32[p, at, 0:HD] = v[:WROWS]
        w32[p, at, HD:2 * HD] = v[WROWS:]

    def ring_steps(pieces, low, high):
        @pl.loop(low, high)
        def _(s):
            for p in pieces:
                for d in (0, 1):
                    ring(p, d, s - 1, s).wait_recv()
                    ring(p, d, s, s).start()
            for p in pieces:
                for d in (0, 1):
                    unpack(p, ring_block(d, s))

    last = NZ // 2

    def ring_last_sends(pieces):
        for p in pieces:
            for d in (0, 1):
                ring(p, d, last - 2, last - 1).wait_recv()
            ring(p, 0, last - 1, last - 1).start()
        for p in pieces:
            for d in (0, 1):
                unpack(p, ring_block(d, last - 1))

    def ring_close(pieces):
        for p in pieces:
            ring(p, 0, last - 1, last).wait_recv()
            unpack(p, ring_block(0, last))

    pieces = (0, 1, 2)
    for p in pieces:
        @pl.when(off_diagonal)
        def _():
            turned(p).wait_recv()

        ring(p, 0, 0, 0).start()
        ring(p, 1, 0, 0).start()
    for p in pieces:
        unpack(p, z)

    @pl.when(off_diagonal)
    def _():
        turned(3).wait_recv()

    ring_steps(pieces, 1, 2)

    def z_wait(h):
        @pl.loop(1, NZ)
        def _(k):
            z_in(h, k).wait_recv()

    held = (xg0, xg1)

    def x_copy(h, k, block, target):
        ref = held[h].at[block]
        return remote(ref, ref, xg_s.at[h, k], xg_r.at[h, k], dev(target, z, y, c))

    def x_out(h, k):
        return x_copy(h, k, x, (x + k) & (NX - 1))

    def x_in(h, k):
        f = (x + NX - k) & (NX - 1)
        return x_copy(h, k, f, f)

    def x_open(h):
        for k in (2, 1, 3):
            x_out(h, k).start()

    def x_wait(h):
        for k in (1, 3, 2):
            x_in(h, k).wait_recv()

    i = iota((ALL_SLOTS, slots), 0)
    q = (i * 171) >> 9
    at = iota((ALL_SLOTS, slots), 1) - (q & (NZ - 1)) * SLOTS - (q >> 4) * 4
    squeeze = ones_where(at == i - 3 * q)
    squeeze_spare = ones_where(at == CAP)
    i = iota((ALL_SLOTS, 128), 0)
    k_kept = i - 3 * ((i * 171) >> 9)
    lane = iota((ALL_SLOTS, 128), 1)

    z_wait(0)
    got = zrecv[0].reshape(slots, SIDE)
    spare_rows = dot(squeeze_spare, got)
    first, second = spare_rows[:, 0:128], spare_rows[:, 128:256]
    tail = jnp.where(
        k_kept == 0, first, jnp.where(k_kept == 1, pltpu.roll(first, TAIL, 1), second)
    )
    flag = jnp.sum(jnp.where(lane == TAIL + k_kept, second, 0.0), axis=1, keepdims=True)
    tail = jnp.where(lane < TAIL, tail, flag)
    xg0[x] = jnp.concatenate((dot(squeeze, got), tail), axis=1).astype(BF16)
    x_open(0)
    ring_steps(pieces, 2, 3)
    ring_steps(pieces, 3, 4)
    z_wait(1)
    xg1[x] = dot(squeeze, zrecv[1].reshape(slots, SIDE)).astype(BF16)
    x_open(1)
    ring_steps(pieces, 4, 5)
    x_wait(0)

    before = ones_where(iota((ALL_SLOTS, ALL_SLOTS), 0) < iota((ALL_SLOTS, ALL_SLOTS), 1))
    flag_lane = ones_where(iota((16, 128), 1) == TAIL)
    my_gain = gain[pl.ds(pl.multiple_of(y * NC * FEAT, 128), NC * FEAT)].reshape(1, NC * FEAT)
    my_gain = jnp.where(c == 0, my_gain[:, :FEAT], my_gain[:, FEAT:])
    table = jnp.zeros((8, 128), F32)
    sub = iota((8, 128), 0)

    def share(dx):
        return remote(
            xs.at[c, dx], xs.at[c, dx], cs_s.at[dx], cs_r.at[dx], dev(x, z, y, 1 - c)
        )

    def share_in(dx):
        return remote(
            xs.at[1 - c, dx], xs.at[1 - c, dx], cs_s.at[dx], cs_r.at[dx], dev(x, z, y, 1 - c)
        )

    def keep(dx, low_column, rows):
        high_column = low_column + rows.shape[1]
        judged[dx, :, low_column:high_column] = rows.astype(BF16)
        xs[c, dx, :, low_column:high_column] = (
            rows * my_gain[:, low_column:high_column]
        ).astype(BF16)
        return jnp.sum(rows * rows, axis=1, keepdims=True)

    places, sums = [], []
    for dx in range(NX):
        s = xg0[:, dx * KEPT:(dx + 1) * KEPT, :].reshape(ALL_SLOTS, WIDE)
        filled = dot(flag_lane, s[:, SIDE:WIDE], NTR)
        rank = dot(filled.astype(BF16), before)
        key = jnp.where(filled > 0.5, rank, -1.0)[0:1]
        place = ones_where(iota((ROWS, ALL_SLOTS), 0).astype(F32) == key)
        rows = dot(place, s)
        places.append(place)
        sums.append(
            keep(dx, 0, rows[:, 0:SIDE]) + keep(dx, 2 * SIDE, rows[:, SIDE:SIDE + TAIL])
        )
        if dx == 1:
            ring_steps(pieces, 5, 6)

    ring_steps(pieces, 6, last - 1)
    x_wait(1)
    for dx in range(NX):
        s = xg1[:, dx * KEPT:(dx + 1) * KEPT, :].reshape(ALL_SLOTS, SIDE)
        total = sums[dx] + keep(dx, SIDE, dot(places[dx], s))
        share(dx).start()
        table = jnp.where(sub == dx, column_to_row(total), table)
        if dx == 1:
            ring_last_sends(pieces)

    sq_in[0] = table

    def squares_out(k):
        return remote(
            sq_in.at[0], sq_in.at[k], sq_s.at[k], sq_r.at[k],
            {"pair": pair, "tensor": ((ten + k) & (NT - 1))},
        )

    @pl.loop(1, NT)
    def _(k):
        squares_out(k).start()

    ring_close((0, 1))
    for dx in range(NX):
        share_in(dx).wait_recv()

    first = xs[0].reshape(NX * ROWS, FEAT)
    second = xs[1].reshape(NX * ROWS, FEAT)
    def products(p):
        w = w32[p].astype(BF16)
        t = dot(first, w[:FEAT]) + dot(second, w[FEAT:])
        return t.astype(BF16).reshape(NX, ROWS, 256)

    def sum_out(n, k):
        t = ((y + k) & (NY - 1))
        src = (part.at[1, t], part.at[1, ((t + NY // 2) & (NY - 1))], part.at[0, t])[n]
        return remote(
            src, part_in.at[n, k], rs_s.at[n, k], rs_r.at[n, k], dev(x, z, t, c)
        )

    part[1] = products(1)
    for k in (2, 1, 3):
        sum_out(0, k).start()
    part[0] = products(0)
    for n in (2, 1):
        for k in (2, 1, 3):
            sum_out(n, k).start()

    ring_close((2,))

    @pl.when(off_diagonal)
    def _():
        for p in range(4):
            turned(p).wait_send()

    for h in (0, 1):
        @pl.loop(1, NZ)
        def _(k):
            z_out(h, k).wait_send()

    for p in range(3):
        @pl.loop(0, NZ // 2 - 1)
        def _(s):
            ring(p, 0, s, s).wait_send()
            ring(p, 1, s, s).wait_send()

        ring(p, 0, NZ // 2 - 1, NZ // 2 - 1).wait_send()
    for h in (0, 1):
        for k in range(1, NX):
            x_out(h, k).wait_send()
    for dx in range(NX):
        share(dx).wait_send()

    @pl.loop(1, NT)
    def _(k):
        squares_out(k).wait_send()

    @pl.loop(1, NT)
    def _(k):
        squares_out(k).wait_recv()

    total = sq_in[0]
    for k in range(1, NT):
        total = total + sq_in[k]
    far_y = ((y + NY // 2) & (NY - 1))
    width = float(NT * FEAT)

    def row_scale(which):
        row = jnp.sum(jnp.where(sub == which, total, 0.0), axis=0, keepdims=True)
        return lax.rsqrt(row_to_column(row, ROWS) / width + epsilon)

    scale_own, scale_far = row_scale(y), row_scale(far_y)
    def summed(n, mine, scale):
        for k in range(1, NY):
            sum_out(n, k).wait_recv()
        t = mine.astype(F32)
        for k in range(1, NY):
            t = t + part_in[n, k].astype(F32)
        return (t * scale).astype(BF16)

    kv = summed(0, part[1, y], scale_own)
    q_own = summed(2, part[0, y], scale_own)

    queries = jnp.concatenate((q_own[:, 0:HD], q_own[:, HD:2 * HD]), axis=0)
    col = iota((2 * ROWS, ROWS), 1)
    row = iota((2 * ROWS, ROWS), 0)
    row = jnp.where(row >= ROWS, row - ROWS, row)
    resp_q, resp_k = row >> 5, col >> 5
    spot_q, spot_k = row & (LEN - 1), col & (LEN - 1)

    def by_response(resp, values):
        return jnp.where(resp == 0, values[0], jnp.where(resp == 1, values[1], values[2]))

    own_lens = [lens[(y * NZ + z) * RESP + k] for k in range(RESP)]
    far_lens = [lens[(far_y * NZ + z) * RESP + k] for k in range(RESP)]
    partner = by_response(resp_q, [slot_in[0:1, k:k + 1] for k in range(RESP)])
    own_ok = (resp_q == resp_k) & (spot_k <= spot_q) & (spot_k < by_response(resp_k, own_lens))
    far_ok = (partner == resp_k) & (spot_k < by_response(resp_k, far_lens))

    def powers(keys, ok):
        scores = dot(queries, keys, NTR) * score_scale
        scores = soft_cap * jnp.tanh(scores / soft_cap)
        return jnp.exp(jnp.where(ok, scores, negative))

    def weigh(keys_values, ok):
        p = powers(keys_values[:, 0:HD], ok)
        return jnp.sum(p, axis=1, keepdims=True), dot(p.astype(BF16), keys_values[:, HD:2 * HD])

    whole, mixed = weigh(kv, own_ok)
    far_whole, far_mixed = weigh(summed(1, part[1, far_y], scale_far), far_ok)
    mixed = (mixed + far_mixed) / (whole + far_whole)
    row = iota((2 * ROWS, HD), 0)
    row = jnp.where(row >= ROWS, row - ROWS, row)
    present = (row & (LEN - 1)) < by_response(row >> 5, own_lens)
    mixed = jnp.where(present, mixed, 0.0).astype(BF16)
    ctx[y] = jnp.concatenate((mixed[:ROWS], mixed[ROWS:]), axis=1)

    def ctx_out(k):
        return remote(ctx.at[y], ctx.at[y], cx_s.at[k], cx_r.at[k], dev(x, z, ((y + k) & (NY - 1)), c))

    def ctx_in(k):
        f = ((y + NY - k) & (NY - 1))
        return remote(ctx.at[f], ctx.at[f], cx_s.at[k], cx_r.at[k], dev(x, z, f, c))

    for k in (2, 1, 3):
        ctx_out(k).start()

    def out_rows(half):
        return w32[2, pl.ds(pl.multiple_of(half * FEAT, 8), FEAT), :].astype(BF16)

    w_other, w_mine = out_rows(1 - c), out_rows(c)

    def swap(k):
        t = ((y + NY - k) & (NY - 1))
        return remote(
            co_out.at[t], co_in.at[t], co_s.at[k], co_r.at[k], dev(x, z, y, 1 - c)
        )

    def xsum(k):
        t = ((x + k) & (NX - 1))
        return remote(xo_out.at[t], xo_in.at[k], xo_s.at[k], xo_r.at[k], dev(t, z, y, c))

    order = (0, 1, 3, 2)
    for k in order:
        t = ((y + NY - k) & (NY - 1))
        if k > 0:
            ctx_in(k).wait_recv()
        co_out[t] = dot(ctx[t], w_other, NTR).astype(BF16)
        swap(k).start()
        xo_out[t] = dot(ctx[t], w_mine, NTR).astype(BF16)
    for k in order:
        t = ((y + NY - k) & (NY - 1))
        swap(k).wait_recv()
        xo_out[t] = (xo_out[t].astype(F32) + co_in[t].astype(F32)).astype(BF16)

        @pl.when(t != x)
        def _():
            xsum(((t + NX - x) & (NX - 1))).start()

    attended = xo_out[x].astype(F32)
    for k in (1, 3, 2):
        xsum(k).wait_recv()
        attended = attended + xo_in[k].astype(F32)

    squares = column_to_row(jnp.sum(attended * attended, axis=1, keepdims=True))
    fin_in[0] = jnp.where(sub == 0, squares, 0.0)

    def fin_out(k):
        return remote(
            fin_in.at[0], fin_in.at[k], fn_s.at[k], fn_r.at[k],
            {"pair": pair, "tensor": ((ten + k) & (NT - 1))},
        )

    @pl.loop(1, NT)
    def _(k):
        fin_out(k).start()

    for k in range(1, NY):
        for n in range(3):
            sum_out(n, k).wait_send()
        ctx_out(k).wait_send()
        xsum(k).wait_send()
    for k in order:
        swap(k).wait_send()

    residual = judged[x].astype(F32)
    gained = attended * post[...].reshape(1, FEAT)

    @pl.loop(1, NT)
    def _(k):
        fin_out(k).wait_recv()

    total = fin_in[0]
    for k in range(1, NT):
        total = total + fin_in[k]
    scale = lax.rsqrt(row_to_column(total[0:1], ROWS) / width + epsilon)
    out[...] = (residual + gained * scale).astype(BF16)

    @pl.loop(1, NT)
    def _(k):
        fin_out(k).wait_send()


def shards(
    rollout, counts, lengths, partner_slot, pre_gain, post_gain,
    query_weight, key_weight, value_weight, out_weight,
):
    vmem = pl.BlockSpec(memory_space=pltpu.VMEM)
    hbm = pl.BlockSpec(memory_space=pltpu.HBM)
    smem = pl.BlockSpec(memory_space=pltpu.SMEM)
    dma = pltpu.SemaphoreType.DMA
    scratch = [
        pltpu.VMEM((ROWS, FEAT), BF16),
        pltpu.VMEM((WROWS, 256), BF16),
        pltpu.VMEM((WROWS, HD), BF16),
        pltpu.VMEM((WROWS, HD), BF16),
        pltpu.VMEM((WROWS, 256), BF16),
        dma((5,)),
        pltpu.VMEM((ROWS, 128), BF16),
        pltpu.VMEM((2, NZ, SLOTS, SIDE), BF16),
        pltpu.VMEM((2, NZ, SLOTS, SIDE), BF16),
        pltpu.VMEM((3, 2 * WROWS, HD), BF16),
        pltpu.VMEM((NZ, 3, 2 * WROWS, HD), BF16),
        pltpu.VMEM((3, BLOCK, 2 * HD), F32),
        pltpu.VMEM((8, 128), I32),
        pltpu.VMEM((8, 128), I32),
        pltpu.VMEM((NX, ALL_SLOTS, WIDE), BF16),
        pltpu.VMEM((NX, ALL_SLOTS, SIDE), BF16),
        pltpu.VMEM((NC, NX, ROWS, FEAT), BF16),
        pltpu.VMEM((NX, ROWS, FEAT), BF16),
        pltpu.VMEM((NT, 8, 128), F32),
        pltpu.VMEM((NT, 8, 128), F32),
        pltpu.VMEM((2, NX, ROWS, 256), BF16),
        pltpu.VMEM((3, NY, ROWS, 256), BF16),
        pltpu.VMEM((NY, ROWS, 256), BF16),
        pltpu.VMEM((NX, ROWS, FEAT), BF16),
        pltpu.VMEM((NX, ROWS, FEAT), BF16),
        pltpu.VMEM((NX, ROWS, FEAT), BF16),
        pltpu.VMEM((NX, ROWS, FEAT), BF16),
        dma((4,)), dma((4,)),
        dma((2, NZ)), dma((2, NZ)),
        dma((3, 2, NZ // 2)), dma((3, 2, NZ // 2)),
        dma((2, NX)), dma((2, NX)),
        dma((NX,)), dma((NX,)),
        dma((NT,)), dma((NT,)),
        dma((3, NY)), dma((3, NY)),
        dma((NY,)), dma((NY,)),
        dma((NX,)), dma((NX,)),
        dma((NX,)), dma((NX,)),
        dma((NT,)), dma((NT,)),
    ]
    return pl.pallas_call(
        kernel,
        out_shape=jax.ShapeDtypeStruct((ROWS, FEAT), BF16),
        in_specs=[hbm, vmem, smem, vmem, vmem, vmem, hbm, hbm, hbm, hbm],
        out_specs=vmem,
        scratch_shapes=scratch,
        compiler_params=pltpu.CompilerParams(
            collective_id=0, has_side_effects=True, vmem_limit_bytes=62 * 1024 * 1024
        ),
    )(
        rollout, counts, lengths, partner_slot, pre_gain,
        post_gain, query_weight, key_weight, value_weight, out_weight,
    )


def solution(mesh):
    placed = (
        P("pair", "tensor"),
        P("pair", None),
        P(),
        P("pair", None),
        P(),
        P("tensor"),
        P("pair", "tensor"),
        P("pair", "tensor"),
        P("pair", "tensor"),
        P("pair", "tensor"),
    )
    return jax.shard_map(
        shards, mesh=mesh, in_specs=placed, out_specs=P("pair", "tensor"), check_vma=False
    )
```

```python
import jax
import jax.numpy as jnp
from jax import lax
from jax.experimental import pallas as pl
from jax.experimental.pallas import tpu as pltpu
from jax.sharding import PartitionSpec as P

NX, NY, NZ, NC = 4, 4, 16, 2
NT = NY * NC
HD = 128
LEN = 32
RESP = 3
ROWS = RESP * LEN
FEAT = 576
SIDE = 256
TAIL = FEAT - 2 * SIDE
WIDE = SIDE + 128
WROWS = 72
BLOCK = NZ * WROWS
CAP = 3
SLOTS = NX * 4
KEPT = NZ * CAP
ALL_SLOTS = NX * KEPT

score_scale = 144.0 ** (-0.5)
soft_cap = 50.0
epsilon = 1e-06
negative = -1e30

F32 = jnp.float32
BF16 = jnp.bfloat16
I32 = jnp.int32
MESH = pl.DeviceIdType.MESH
NN = (((1,), (0,)), ((), ()))
NTR = (((1,), (1,)), ((), ()))


def dot(a, b, dims=NN):
    return lax.dot_general(a, b, dims, preferred_element_type=F32)


def iota(shape, dim):
    return lax.broadcasted_iota(I32, shape, dim)


def ones_where(cond):
    return jnp.where(cond, 1.0, 0.0).astype(BF16)


def column_to_row(col):
    rows = col.shape[0]
    same = iota((rows, 128), 0) == iota((rows, 128), 1)
    return jnp.sum(jnp.where(same, col, 0.0), axis=0, keepdims=True)


def row_to_column(row, rows):
    same = iota((rows, 128), 0) == iota((rows, 128), 1)
    return jnp.sum(jnp.where(same, row, 0.0), axis=1, keepdims=True)


def kernel(
    roll_h, counts, lens, pslot, gain, post, wq_h, wk_h, wv_h, wo_h, out,
    roll, wq, wk, wv, wo, in_s, low, zsend, zrecv, wsend, wbuf, w32, slot_out, slot_in, xg0, xg1, xs, judged, sq_in, fin_in,
    part, part_in, ctx, co_out, co_in, xo_out, xo_in,
    tr_s, tr_r, za_s, za_r, ring_s, ring_r, xg_s, xg_r, cs_s, cs_r, sq_s, sq_r,
    rs_s, rs_r, cx_s, cx_r, co_s, co_r, xo_s, xo_r, fn_s, fn_r,
):
    pair = lax.axis_index("pair")
    ten = lax.axis_index("tensor")
    x, z = pair >> 4, pair & (NZ - 1)
    y, c = ten >> 1, ten & (NC - 1)

    def dev(xx, zz, yy, cc):
        return {"pair": xx * NZ + zz, "tensor": yy * NC + cc}

    def remote(src, dst, send, recv, where):
        return pltpu.make_async_remote_copy(
            src_ref=src, dst_ref=dst, send_sem=send, recv_sem=recv,
            device_id=where, device_id_type=MESH,
        )

    off_diagonal = x != y

    loads = [
        pltpu.make_async_copy(a, b, in_s.at[n])
        for n, (a, b) in enumerate(
            ((roll_h, roll), (wq_h, wq), (wk_h, wk), (wv_h, wv), (wo_h, wo))
        )
    ]
    for load in loads:
        load.start()

    barrier = pltpu.get_barrier_semaphore()

    def greet(where):
        pl.semaphore_signal(barrier, inc=1, device_id=where, device_id_type=MESH)

    @pl.loop(1, NZ)
    def _(k):
        greet(dev(x, ((z + k) & (NZ - 1)), y, c))

    @pl.loop(1, NX)
    def _(k):
        greet(dev(((x + k) & (NX - 1)), z, y, c))

    @pl.loop(1, NT)
    def _(k):
        greet({"pair": pair, "tensor": ((ten + k) & (NT - 1))})

    @pl.when(off_diagonal)
    def _():
        greet(dev(y, z, x, c))

    slots = NZ * SLOTS
    j = iota((slots, NX * NZ), 0)
    dest = ((j >> 2) & (NX - 1)) * NZ + (j >> 4)
    other = iota((slots, NX * NZ), 1)
    sending = counts[...].astype(F32)
    start = jnp.sum(jnp.where(other < dest, sending, 0.0), axis=1, keepdims=True)
    amount = jnp.sum(jnp.where(other == dest, sending, 0.0), axis=1, keepdims=True)
    k_slot = (iota((slots, 1), 0) & 3).astype(F32)
    spare = k_slot == CAP
    row_of = iota((slots, ROWS), 1).astype(F32)

    def picking(cond, k):
        return ones_where(jnp.where(cond & (amount > k), start + k, -1.0) == row_of)

    pick = picking(k_slot < CAP, k_slot)
    pick_tail = [picking(spare, float(k)) for k in range(CAP)]
    spot = iota((slots, 128), 1) - TAIL
    flags = jnp.where(
        spare & (spot >= 0) & (spot < CAP) & (spot.astype(F32) < amount), 1.0, 0.0
    )
    low[...] = jnp.zeros((ROWS, 128), BF16)
    loads[0].wait()
    low[:, 0:TAIL] = roll[:, 2 * SIDE:FEAT]
    low_tail = low[...]
    high_tail = pltpu.roll(low_tail.astype(F32), TAIL, 1).astype(BF16)
    base = dot(pick, roll[:, 0:2 * SIDE])
    tile0 = base[:, 0:128] + dot(pick_tail[0], low_tail) + dot(pick_tail[1], high_tail)
    tile1 = base[:, 128:256] + dot(pick_tail[2], low_tail) + flags
    zsend[0] = jnp.concatenate((tile0, tile1), axis=1).astype(BF16).reshape(NZ, SLOTS, SIDE)
    zsend[1] = base[:, SIDE:].astype(BF16).reshape(NZ, SLOTS, SIDE)
    for h in (0, 1):
        zrecv[h, z] = zsend[h, z]

    for load in loads[1:]:
        load.wait()

    def pack(p, first, second):
        wsend[p] = jnp.concatenate(
            (first.astype(F32), second.astype(F32)), axis=0
        ).astype(BF16)

    pack(0, wq[:, :HD], wq[:, HD:])
    pack(1, wk[...], wv[...])
    pack(2, wo[:, :HD], wo[:, HD:])
    lane = iota((8, 128), 1)
    spread = jnp.zeros((8, 128), I32)
    for k in range(RESP):
        spread = jnp.where(lane == k, pslot[0:1, k:k + 1], spread)
    slot_out[...] = spread

    greeted = NZ - 1 + NX - 1 + NT - 1

    @pl.when(off_diagonal)
    def _():
        pl.semaphore_wait(barrier, greeted + 1)

    @pl.when(jnp.logical_not(off_diagonal))
    def _():
        pl.semaphore_wait(barrier, greeted)

    def z_out(h, k):
        t = ((z + k) & (NZ - 1))
        return remote(
            zsend.at[h, t], zrecv.at[h, z], za_s.at[h, k], za_r.at[h, k], dev(x, t, y, c)
        )

    def z_in(h, k):
        f = ((z + NZ - k) & (NZ - 1))
        return remote(
            zsend.at[h, f], zrecv.at[h, f], za_s.at[h, k], za_r.at[h, k], dev(x, f, y, c)
        )

    def turned(p):
        src, dst = (slot_out, slot_in) if p == 3 else (wsend.at[p], wbuf.at[z, p])
        return remote(src, dst, tr_s.at[p], tr_r.at[p], dev(y, z, x, c))

    @pl.when(off_diagonal)
    def _():
        for p in range(4):
            turned(p).start()

    for h in (0, 1):
        z_out(h, NZ // 2).start()

        @pl.loop(1, NZ // 2)
        def _(k):
            z_out(h, NZ // 2 - k).start()
            z_out(h, NZ // 2 + k).start()

    @pl.when(jnp.logical_not(off_diagonal))
    def _():
        wbuf[z] = wsend[...]
        slot_in[...] = slot_out[...]

    up, down = ((z + 1) & (NZ - 1)), ((z + NZ - 1) & (NZ - 1))

    def ring_block(d, s):
        return ((z + NZ - s) & (NZ - 1)) if d == 0 else ((z + s) & (NZ - 1))

    def ring(p, d, s, distance):
        block = wbuf.at[ring_block(d, distance), p]
        return remote(
            block, block, ring_s.at[p, d, s], ring_r.at[p, d, s],
            dev(x, up if d == 0 else down, y, c),
        )

    def unpack(p, block):
        v = wbuf[block, p].astype(F32)
        at = pl.ds(pl.multiple_of(block * WROWS, 8), WROWS)
        w32[p, at, 0:HD] = v[:WROWS]
        w32[p, at, HD:2 * HD] = v[WROWS:]

    def ring_steps(pieces, low, high):
        @pl.loop(low, high)
        def _(s):
            for p in pieces:
                for d in (0, 1):
                    ring(p, d, s - 1, s).wait_recv()
                    ring(p, d, s, s).start()
            for p in pieces:
                for d in (0, 1):
                    unpack(p, ring_block(d, s))

    last = NZ // 2

    def ring_last_sends(pieces):
        for p in pieces:
            for d in (0, 1):
                ring(p, d, last - 2, last - 1).wait_recv()
            ring(p, 0, last - 1, last - 1).start()
        for p in pieces:
            for d in (0, 1):
                unpack(p, ring_block(d, last - 1))

    def ring_close(pieces):
        for p in pieces:
            ring(p, 0, last - 1, last).wait_recv()
            unpack(p, ring_block(0, last))

    early, late = (0, 1), (2,)
    for p in (0, 1, 2):
        @pl.when(off_diagonal)
        def _():
            turned(p).wait_recv()

        if p in early:
            ring(p, 0, 0, 0).start()
            ring(p, 1, 0, 0).start()
    for p in (0, 1, 2):
        unpack(p, z)

    @pl.when(off_diagonal)
    def _():
        turned(3).wait_recv()

    ring_steps(early, 1, 2)

    def z_wait(h):
        @pl.loop(1, NZ)
        def _(k):
            z_in(h, k).wait_recv()

    held = (xg0, xg1)

    def x_copy(h, k, block, target):
        ref = held[h].at[block]
        return remote(ref, ref, xg_s.at[h, k], xg_r.at[h, k], dev(target, z, y, c))

    def x_out(h, k):
        return x_copy(h, k, x, (x + k) & (NX - 1))

    def x_in(h, k):
        f = (x + NX - k) & (NX - 1)
        return x_copy(h, k, f, f)

    def x_open(h):
        for k in (2, 1, 3):
            x_out(h, k).start()

    def x_wait(h):
        for k in (1, 3, 2):
            x_in(h, k).wait_recv()

    i = iota((ALL_SLOTS, slots), 0)
    q = (i * 171) >> 9
    at = iota((ALL_SLOTS, slots), 1) - (q & (NZ - 1)) * SLOTS - (q >> 4) * 4
    squeeze = ones_where(at == i - 3 * q)
    squeeze_spare = ones_where(at == CAP)
    i = iota((ALL_SLOTS, 128), 0)
    k_kept = i - 3 * ((i * 171) >> 9)
    lane = iota((ALL_SLOTS, 128), 1)

    z_wait(0)
    got = zrecv[0].reshape(slots, SIDE)
    spare_rows = dot(squeeze_spare, got)
    first, second = spare_rows[:, 0:128], spare_rows[:, 128:256]
    tail = jnp.where(
        k_kept == 0, first, jnp.where(k_kept == 1, pltpu.roll(first, TAIL, 1), second)
    )
    flag = jnp.sum(jnp.where(lane == TAIL + k_kept, second, 0.0), axis=1, keepdims=True)
    tail = jnp.where(lane < TAIL, tail, flag)
    xg0[x] = jnp.concatenate((dot(squeeze, got), tail), axis=1).astype(BF16)
    x_open(0)
    ring_steps(early, 2, 3)
    for d in (0, 1):
        ring(2, d, 0, 0).start()
    ring_steps(early, 3, 4)
    z_wait(1)
    xg1[x] = dot(squeeze, zrecv[1].reshape(slots, SIDE)).astype(BF16)
    x_open(1)
    ring_steps(early, 4, 5)
    ring_steps(late, 1, 2)
    x_wait(0)

    before = ones_where(iota((ALL_SLOTS, ALL_SLOTS), 0) < iota((ALL_SLOTS, ALL_SLOTS), 1))
    flag_lane = ones_where(iota((16, 128), 1) == TAIL)
    my_gain = gain[pl.ds(pl.multiple_of(y * NC * FEAT, 128), NC * FEAT)].reshape(1, NC * FEAT)
    my_gain = jnp.where(c == 0, my_gain[:, :FEAT], my_gain[:, FEAT:])
    table = jnp.zeros((8, 128), F32)
    sub = iota((8, 128), 0)

    def share(dx):
        return remote(
            xs.at[c, dx], xs.at[c, dx], cs_s.at[dx], cs_r.at[dx], dev(x, z, y, 1 - c)
        )

    def share_in(dx):
        return remote(
            xs.at[1 - c, dx], xs.at[1 - c, dx], cs_s.at[dx], cs_r.at[dx], dev(x, z, y, 1 - c)
        )

    def keep(dx, low_column, rows):
        high_column = low_column + rows.shape[1]
        judged[dx, :, low_column:high_column] = rows.astype(BF16)
        xs[c, dx, :, low_column:high_column] = (
            rows * my_gain[:, low_column:high_column]
        ).astype(BF16)
        return jnp.sum(rows * rows, axis=1, keepdims=True)

    places, sums = [], []
    for dx in range(NX):
        s = xg0[:, dx * KEPT:(dx + 1) * KEPT, :].reshape(ALL_SLOTS, WIDE)
        filled = dot(flag_lane, s[:, SIDE:WIDE], NTR)
        rank = dot(filled.astype(BF16), before)
        key = jnp.where(filled > 0.5, rank, -1.0)[0:1]
        place = ones_where(iota((ROWS, ALL_SLOTS), 0).astype(F32) == key)
        rows = dot(place, s)
        places.append(place)
        sums.append(
            keep(dx, 0, rows[:, 0:SIDE]) + keep(dx, 2 * SIDE, rows[:, SIDE:SIDE + TAIL])
        )
        if dx == 1:
            ring_steps(early, 5, 6)
            ring_steps(late, 2, 3)

    ring_steps(early, 6, last - 1)
    ring_steps(late, 3, 4)
    x_wait(1)
    for dx in range(NX):
        s = xg1[:, dx * KEPT:(dx + 1) * KEPT, :].reshape(ALL_SLOTS, SIDE)
        total = sums[dx] + keep(dx, SIDE, dot(places[dx], s))
        share(dx).start()
        table = jnp.where(sub == dx, column_to_row(total), table)
        if dx == 1:
            ring_last_sends(early)
            ring_steps(late, 4, 5)

    sq_in[0] = table

    def squares_out(k):
        return remote(
            sq_in.at[0], sq_in.at[k], sq_s.at[k], sq_r.at[k],
            {"pair": pair, "tensor": ((ten + k) & (NT - 1))},
        )

    @pl.loop(1, NT)
    def _(k):
        squares_out(k).start()

    ring_close(early)
    for dx in range(NX):
        share_in(dx).wait_recv()

    first = xs[0].reshape(NX * ROWS, FEAT)
    second = xs[1].reshape(NX * ROWS, FEAT)
    def products(p):
        w = w32[p].astype(BF16)
        t = dot(first, w[:FEAT]) + dot(second, w[FEAT:])
        return t.astype(BF16).reshape(NX, ROWS, 256)

    def sum_out(n, k):
        t = ((y + k) & (NY - 1))
        src = (part.at[1, t], part.at[1, ((t + NY // 2) & (NY - 1))], part.at[0, t])[n]
        return remote(
            src, part_in.at[n, k], rs_s.at[n, k], rs_r.at[n, k], dev(x, z, t, c)
        )

    part[1] = products(1)
    for k in (2, 1, 3):
        sum_out(0, k).start()
    part[0] = products(0)
    for n in (2, 1):
        for k in (2, 1, 3):
            sum_out(n, k).start()

    ring_steps(late, 5, last - 1)

    @pl.when(off_diagonal)
    def _():
        for p in range(4):
            turned(p).wait_send()

    for h in (0, 1):
        @pl.loop(1, NZ)
        def _(k):
            z_out(h, k).wait_send()

    def ring_left(p):
        @pl.loop(0, last - 1)
        def _(s):
            ring(p, 0, s, s).wait_send()
            ring(p, 1, s, s).wait_send()

        ring(p, 0, last - 1, last - 1).wait_send()

    for p in early:
        ring_left(p)
    for h in (0, 1):
        for k in range(1, NX):
            x_out(h, k).wait_send()
    for dx in range(NX):
        share(dx).wait_send()

    @pl.loop(1, NT)
    def _(k):
        squares_out(k).wait_send()

    @pl.loop(1, NT)
    def _(k):
        squares_out(k).wait_recv()

    total = sq_in[0]
    for k in range(1, NT):
        total = total + sq_in[k]
    far_y = ((y + NY // 2) & (NY - 1))
    width = float(NT * FEAT)

    def row_scale(which):
        row = jnp.sum(jnp.where(sub == which, total, 0.0), axis=0, keepdims=True)
        return lax.rsqrt(row_to_column(row, ROWS) / width + epsilon)

    scale_own, scale_far = row_scale(y), row_scale(far_y)
    def summed(n, mine, scale):
        for k in range(1, NY):
            sum_out(n, k).wait_recv()
        t = mine.astype(F32)
        for k in range(1, NY):
            t = t + part_in[n, k].astype(F32)
        return (t * scale).astype(BF16)

    kv = summed(0, part[1, y], scale_own)
    q_own = summed(2, part[0, y], scale_own)

    queries = jnp.concatenate((q_own[:, 0:HD], q_own[:, HD:2 * HD]), axis=0)
    col = iota((2 * ROWS, ROWS), 1)
    row = iota((2 * ROWS, ROWS), 0)
    row = jnp.where(row >= ROWS, row - ROWS, row)
    resp_q, resp_k = row >> 5, col >> 5
    spot_q, spot_k = row & (LEN - 1), col & (LEN - 1)

    def by_response(resp, values):
        return jnp.where(resp == 0, values[0], jnp.where(resp == 1, values[1], values[2]))

    own_lens = [lens[(y * NZ + z) * RESP + k] for k in range(RESP)]
    far_lens = [lens[(far_y * NZ + z) * RESP + k] for k in range(RESP)]
    partner = by_response(resp_q, [slot_in[0:1, k:k + 1] for k in range(RESP)])
    own_ok = (resp_q == resp_k) & (spot_k <= spot_q) & (spot_k < by_response(resp_k, own_lens))
    far_ok = (partner == resp_k) & (spot_k < by_response(resp_k, far_lens))

    def powers(keys, ok):
        scores = dot(queries, keys, NTR) * score_scale
        scores = soft_cap * jnp.tanh(scores / soft_cap)
        return jnp.exp(jnp.where(ok, scores, negative))

    def weigh(keys_values, ok):
        p = powers(keys_values[:, 0:HD], ok)
        return jnp.sum(p, axis=1, keepdims=True), dot(p.astype(BF16), keys_values[:, HD:2 * HD])

    whole, mixed = weigh(kv, own_ok)
    ring_last_sends(late)
    far_whole, far_mixed = weigh(summed(1, part[1, far_y], scale_far), far_ok)
    mixed = (mixed + far_mixed) / (whole + far_whole)
    row = iota((2 * ROWS, HD), 0)
    row = jnp.where(row >= ROWS, row - ROWS, row)
    present = (row & (LEN - 1)) < by_response(row >> 5, own_lens)
    mixed = jnp.where(present, mixed, 0.0).astype(BF16)
    ctx[y] = jnp.concatenate((mixed[:ROWS], mixed[ROWS:]), axis=1)

    def ctx_out(k):
        return remote(ctx.at[y], ctx.at[y], cx_s.at[k], cx_r.at[k], dev(x, z, ((y + k) & (NY - 1)), c))

    def ctx_in(k):
        f = ((y + NY - k) & (NY - 1))
        return remote(ctx.at[f], ctx.at[f], cx_s.at[k], cx_r.at[k], dev(x, z, f, c))

    for k in (2, 1, 3):
        ctx_out(k).start()
    ring_close(late)

    def out_rows(half):
        return w32[2, pl.ds(pl.multiple_of(half * FEAT, 8), FEAT), :].astype(BF16)

    w_other, w_mine = out_rows(1 - c), out_rows(c)

    def swap(k):
        t = ((y + NY - k) & (NY - 1))
        return remote(
            co_out.at[t], co_in.at[t], co_s.at[k], co_r.at[k], dev(x, z, y, 1 - c)
        )

    def xsum(k):
        t = ((x + k) & (NX - 1))
        return remote(xo_out.at[t], xo_in.at[k], xo_s.at[k], xo_r.at[k], dev(t, z, y, c))

    order = (0, 1, 3, 2)
    for k in order:
        t = ((y + NY - k) & (NY - 1))
        if k > 0:
            ctx_in(k).wait_recv()
        co_out[t] = dot(ctx[t], w_other, NTR).astype(BF16)
        swap(k).start()
        xo_out[t] = dot(ctx[t], w_mine, NTR).astype(BF16)
    for k in order:
        t = ((y + NY - k) & (NY - 1))
        swap(k).wait_recv()
        xo_out[t] = (xo_out[t].astype(F32) + co_in[t].astype(F32)).astype(BF16)

        @pl.when(t != x)
        def _():
            xsum(((t + NX - x) & (NX - 1))).start()

    attended = xo_out[x].astype(F32)
    for k in (1, 3, 2):
        xsum(k).wait_recv()
        attended = attended + xo_in[k].astype(F32)

    squares = column_to_row(jnp.sum(attended * attended, axis=1, keepdims=True))
    fin_in[0] = jnp.where(sub == 0, squares, 0.0)

    def fin_out(k):
        return remote(
            fin_in.at[0], fin_in.at[k], fn_s.at[k], fn_r.at[k],
            {"pair": pair, "tensor": ((ten + k) & (NT - 1))},
        )

    @pl.loop(1, NT)
    def _(k):
        fin_out(k).start()

    ring_left(2)
    for k in range(1, NY):
        for n in range(3):
            sum_out(n, k).wait_send()
        ctx_out(k).wait_send()
        xsum(k).wait_send()
    for k in order:
        swap(k).wait_send()

    residual = judged[x].astype(F32)
    gained = attended * post[...].reshape(1, FEAT)

    @pl.loop(1, NT)
    def _(k):
        fin_out(k).wait_recv()

    total = fin_in[0]
    for k in range(1, NT):
        total = total + fin_in[k]
    scale = lax.rsqrt(row_to_column(total[0:1], ROWS) / width + epsilon)
    out[...] = (residual + gained * scale).astype(BF16)

    @pl.loop(1, NT)
    def _(k):
        fin_out(k).wait_send()


def shards(
    rollout, counts, lengths, partner_slot, pre_gain, post_gain,
    query_weight, key_weight, value_weight, out_weight,
):
    vmem = pl.BlockSpec(memory_space=pltpu.VMEM)
    hbm = pl.BlockSpec(memory_space=pltpu.HBM)
    smem = pl.BlockSpec(memory_space=pltpu.SMEM)
    dma = pltpu.SemaphoreType.DMA
    scratch = [
        pltpu.VMEM((ROWS, FEAT), BF16),
        pltpu.VMEM((WROWS, 256), BF16),
        pltpu.VMEM((WROWS, HD), BF16),
        pltpu.VMEM((WROWS, HD), BF16),
        pltpu.VMEM((WROWS, 256), BF16),
        dma((5,)),
        pltpu.VMEM((ROWS, 128), BF16),
        pltpu.VMEM((2, NZ, SLOTS, SIDE), BF16),
        pltpu.VMEM((2, NZ, SLOTS, SIDE), BF16),
        pltpu.VMEM((3, 2 * WROWS, HD), BF16),
        pltpu.VMEM((NZ, 3, 2 * WROWS, HD), BF16),
        pltpu.VMEM((3, BLOCK, 2 * HD), F32),
        pltpu.VMEM((8, 128), I32),
        pltpu.VMEM((8, 128), I32),
        pltpu.VMEM((NX, ALL_SLOTS, WIDE), BF16),
        pltpu.VMEM((NX, ALL_SLOTS, SIDE), BF16),
        pltpu.VMEM((NC, NX, ROWS, FEAT), BF16),
        pltpu.VMEM((NX, ROWS, FEAT), BF16),
        pltpu.VMEM((NT, 8, 128), F32),
        pltpu.VMEM((NT, 8, 128), F32),
        pltpu.VMEM((2, NX, ROWS, 256), BF16),
        pltpu.VMEM((3, NY, ROWS, 256), BF16),
        pltpu.VMEM((NY, ROWS, 256), BF16),
        pltpu.VMEM((NX, ROWS, FEAT), BF16),
        pltpu.VMEM((NX, ROWS, FEAT), BF16),
        pltpu.VMEM((NX, ROWS, FEAT), BF16),
        pltpu.VMEM((NX, ROWS, FEAT), BF16),
        dma((4,)), dma((4,)),
        dma((2, NZ)), dma((2, NZ)),
        dma((3, 2, NZ // 2)), dma((3, 2, NZ // 2)),
        dma((2, NX)), dma((2, NX)),
        dma((NX,)), dma((NX,)),
        dma((NT,)), dma((NT,)),
        dma((3, NY)), dma((3, NY)),
        dma((NY,)), dma((NY,)),
        dma((NX,)), dma((NX,)),
        dma((NX,)), dma((NX,)),
        dma((NT,)), dma((NT,)),
    ]
    return pl.pallas_call(
        kernel,
        out_shape=jax.ShapeDtypeStruct((ROWS, FEAT), BF16),
        in_specs=[hbm, vmem, smem, vmem, vmem, vmem, hbm, hbm, hbm, hbm],
        out_specs=vmem,
        scratch_shapes=scratch,
        compiler_params=pltpu.CompilerParams(
            collective_id=0, has_side_effects=True, vmem_limit_bytes=62 * 1024 * 1024
        ),
    )(
        rollout, counts, lengths, partner_slot, pre_gain,
        post_gain, query_weight, key_weight, value_weight, out_weight,
    )


def solution(mesh):
    placed = (
        P("pair", "tensor"),
        P("pair", None),
        P(),
        P("pair", None),
        P(),
        P("tensor"),
        P("pair", "tensor"),
        P("pair", "tensor"),
        P("pair", "tensor"),
        P("pair", "tensor"),
    )
    return jax.shard_map(
        shards, mesh=mesh, in_specs=placed, out_specs=P("pair", "tensor"), check_vma=False
    )
```

```python
import jax
import jax.numpy as jnp
from jax import lax
from jax.experimental import pallas as pl
from jax.experimental.pallas import tpu as pltpu
from jax.sharding import PartitionSpec as P

NX, NY, NZ, NC = 4, 4, 16, 2
NT = NY * NC
HD = 128
LEN = 32
RESP = 3
ROWS = RESP * LEN
FEAT = 576
SIDE = 256
TAIL = FEAT - 2 * SIDE
WIDE = SIDE + 128
WROWS = 72
BLOCK = NZ * WROWS
CAP = 3
SLOTS = NX * 4
KEPT = NZ * CAP
ALL_SLOTS = NX * KEPT

score_scale = 144.0 ** (-0.5)
soft_cap = 50.0
epsilon = 1e-06
negative = -1e30

F32 = jnp.float32
BF16 = jnp.bfloat16
I32 = jnp.int32
MESH = pl.DeviceIdType.MESH
NN = (((1,), (0,)), ((), ()))
NTR = (((1,), (1,)), ((), ()))


def dot(a, b, dims=NN):
    return lax.dot_general(a, b, dims, preferred_element_type=F32)


def iota(shape, dim):
    return lax.broadcasted_iota(I32, shape, dim)


def ones_where(cond):
    return jnp.where(cond, 1.0, 0.0).astype(BF16)


def column_to_row(col):
    rows = col.shape[0]
    same = iota((rows, 128), 0) == iota((rows, 128), 1)
    return jnp.sum(jnp.where(same, col, 0.0), axis=0, keepdims=True)


def row_to_column(row, rows):
    same = iota((rows, 128), 0) == iota((rows, 128), 1)
    return jnp.sum(jnp.where(same, row, 0.0), axis=1, keepdims=True)


def kernel(
    roll_h, counts, lens, pslot, gain, post, wq_h, wk_h, wv_h, wo_h, out,
    roll, wq, wk, wv, wo, in_s, low, zsend, zrecv, wsend, wbuf, w32, slot_out, slot_in, xg0, xg1, xs, judged, sq_in, fin_in,
    part, part_in, ctx, co_out, co_in, xo_out, xo_in,
    tr_s, tr_r, za_s, za_r, ring_s, ring_r, xg_s, xg_r, cs_s, cs_r, sq_s, sq_r,
    rs_s, rs_r, cx_s, cx_r, co_s, co_r, xo_s, xo_r, fn_s, fn_r,
):
    pair = lax.axis_index("pair")
    ten = lax.axis_index("tensor")
    x, z = pair >> 4, pair & (NZ - 1)
    y, c = ten >> 1, ten & (NC - 1)

    def dev(xx, zz, yy, cc):
        return {"pair": xx * NZ + zz, "tensor": yy * NC + cc}

    def remote(src, dst, send, recv, where):
        return pltpu.make_async_remote_copy(
            src_ref=src, dst_ref=dst, send_sem=send, recv_sem=recv,
            device_id=where, device_id_type=MESH,
        )

    off_diagonal = x != y

    loads = [
        pltpu.make_async_copy(a, b, in_s.at[n])
        for n, (a, b) in enumerate(
            ((roll_h, roll), (wq_h, wq), (wk_h, wk), (wv_h, wv), (wo_h, wo))
        )
    ]
    for load in loads:
        load.start()

    barrier = pltpu.get_barrier_semaphore()

    def greet(where):
        pl.semaphore_signal(barrier, inc=1, device_id=where, device_id_type=MESH)

    @pl.loop(1, NZ)
    def _(k):
        greet(dev(x, ((z + k) & (NZ - 1)), y, c))

    @pl.loop(1, NX)
    def _(k):
        greet(dev(((x + k) & (NX - 1)), z, y, c))

    @pl.loop(1, NT)
    def _(k):
        greet({"pair": pair, "tensor": ((ten + k) & (NT - 1))})

    @pl.when(off_diagonal)
    def _():
        greet(dev(y, z, x, c))

    slots = NZ * SLOTS
    j = iota((slots, NX * NZ), 0)
    dest = ((j >> 2) & (NX - 1)) * NZ + (j >> 4)
    other = iota((slots, NX * NZ), 1)
    sending = counts[...].astype(F32)
    start = jnp.sum(jnp.where(other < dest, sending, 0.0), axis=1, keepdims=True)
    amount = jnp.sum(jnp.where(other == dest, sending, 0.0), axis=1, keepdims=True)
    k_slot = (iota((slots, 1), 0) & 3).astype(F32)
    spare = k_slot == CAP
    row_of = iota((slots, ROWS), 1).astype(F32)

    def picking(cond, k):
        return ones_where(jnp.where(cond & (amount > k), start + k, -1.0) == row_of)

    pick = picking(k_slot < CAP, k_slot)
    pick_tail = [picking(spare, float(k)) for k in range(CAP)]
    spot = iota((slots, 128), 1) - TAIL
    flags = jnp.where(
        spare & (spot >= 0) & (spot < CAP) & (spot.astype(F32) < amount), 1.0, 0.0
    )
    low[...] = jnp.zeros((ROWS, 128), BF16)
    loads[0].wait()
    low[:, 0:TAIL] = roll[:, 2 * SIDE:FEAT]
    low_tail = low[...]
    high_tail = pltpu.roll(low_tail.astype(F32), TAIL, 1).astype(BF16)
    base = dot(pick, roll[:, 0:2 * SIDE])
    tile0 = base[:, 0:128] + dot(pick_tail[0], low_tail) + dot(pick_tail[1], high_tail)
    tile1 = base[:, 128:256] + dot(pick_tail[2], low_tail) + flags
    zsend[0] = jnp.concatenate((tile0, tile1), axis=1).astype(BF16).reshape(NZ, SLOTS, SIDE)
    zsend[1] = base[:, SIDE:].astype(BF16).reshape(NZ, SLOTS, SIDE)
    for h in (0, 1):
        zrecv[h, z] = zsend[h, z]

    for load in loads[1:]:
        load.wait()

    def pack(p, first, second):
        wsend[p] = jnp.concatenate(
            (first.astype(F32), second.astype(F32)), axis=0
        ).astype(BF16)

    pack(0, wq[:, :HD], wq[:, HD:])
    pack(1, wk[...], wv[...])
    pack(2, wo[:, :HD], wo[:, HD:])
    lane = iota((8, 128), 1)
    spread = jnp.zeros((8, 128), I32)
    for k in range(RESP):
        spread = jnp.where(lane == k, pslot[0:1, k:k + 1], spread)
    slot_out[...] = spread

    greeted = NZ - 1 + NX - 1 + NT - 1

    @pl.when(off_diagonal)
    def _():
        pl.semaphore_wait(barrier, greeted + 1)

    @pl.when(jnp.logical_not(off_diagonal))
    def _():
        pl.semaphore_wait(barrier, greeted)

    def z_out(h, k):
        t = ((z + k) & (NZ - 1))
        return remote(
            zsend.at[h, t], zrecv.at[h, z], za_s.at[h, k], za_r.at[h, k], dev(x, t, y, c)
        )

    def z_in(h, k):
        f = ((z + NZ - k) & (NZ - 1))
        return remote(
            zsend.at[h, f], zrecv.at[h, f], za_s.at[h, k], za_r.at[h, k], dev(x, f, y, c)
        )

    def turned(p):
        src, dst = (slot_out, slot_in) if p == 3 else (wsend.at[p], wbuf.at[z, p])
        return remote(src, dst, tr_s.at[p], tr_r.at[p], dev(y, z, x, c))

    @pl.when(off_diagonal)
    def _():
        for p in range(4):
            turned(p).start()

    for h in (0, 1):
        z_out(h, NZ // 2).start()

        @pl.loop(1, NZ // 2)
        def _(k):
            z_out(h, NZ // 2 - k).start()
            z_out(h, NZ // 2 + k).start()

    @pl.when(jnp.logical_not(off_diagonal))
    def _():
        wbuf[z] = wsend[...]
        slot_in[...] = slot_out[...]

    up, down = ((z + 1) & (NZ - 1)), ((z + NZ - 1) & (NZ - 1))

    def ring_block(d, s):
        return ((z + NZ - s) & (NZ - 1)) if d == 1 else ((z + s) & (NZ - 1))

    def ring(p, d, s, distance):
        block = wbuf.at[ring_block(d, distance), p]
        return remote(
            block, block, ring_s.at[p, d, s], ring_r.at[p, d, s],
            dev(x, up if d == 1 else down, y, c),
        )

    def unpack(p, block):
        v = wbuf[block, p].astype(F32)
        at = pl.ds(pl.multiple_of(block * WROWS, 8), WROWS)
        w32[p, at, 0:HD] = v[:WROWS]
        w32[p, at, HD:2 * HD] = v[WROWS:]

    def ring_steps(pieces, low, high):
        @pl.loop(low, high)
        def _(s):
            for p in pieces:
                for d in (0, 1):
                    ring(p, d, s - 1, s).wait_recv()
                    ring(p, d, s, s).start()
            for p in pieces:
                for d in (0, 1):
                    unpack(p, ring_block(d, s))

    last = NZ // 2

    def ring_last_sends(pieces):
        for p in pieces:
            for d in (0, 1):
                ring(p, d, last - 2, last - 1).wait_recv()
            ring(p, 0, last - 1, last - 1).start()
        for p in pieces:
            for d in (0, 1):
                unpack(p, ring_block(d, last - 1))

    def ring_close(pieces):
        for p in pieces:
            ring(p, 0, last - 1, last).wait_recv()
            unpack(p, ring_block(0, last))

    early, late = (0, 1), (2,)
    for p in (0, 1, 2):
        @pl.when(off_diagonal)
        def _():
            turned(p).wait_recv()

        if p in early:
            ring(p, 0, 0, 0).start()
            ring(p, 1, 0, 0).start()
    for p in (0, 1, 2):
        unpack(p, z)

    @pl.when(off_diagonal)
    def _():
        turned(3).wait_recv()

    ring_steps(early, 1, 2)

    def z_wait(h):
        @pl.loop(1, NZ)
        def _(k):
            z_in(h, k).wait_recv()

    held = (xg0, xg1)

    def x_copy(h, k, block, target):
        ref = held[h].at[block]
        return remote(ref, ref, xg_s.at[h, k], xg_r.at[h, k], dev(target, z, y, c))

    def x_out(h, k):
        return x_copy(h, k, x, (x + k) & (NX - 1))

    def x_in(h, k):
        f = (x + NX - k) & (NX - 1)
        return x_copy(h, k, f, f)

    def x_open(h):
        for k in (2, 1, 3):
            x_out(h, k).start()

    def x_wait(h):
        for k in (1, 3, 2):
            x_in(h, k).wait_recv()

    i = iota((ALL_SLOTS, slots), 0)
    q = (i * 171) >> 9
    at = iota((ALL_SLOTS, slots), 1) - (q & (NZ - 1)) * SLOTS - (q >> 4) * 4
    squeeze = ones_where(at == i - 3 * q)
    squeeze_spare = ones_where(at == CAP)
    i = iota((ALL_SLOTS, 128), 0)
    k_kept = i - 3 * ((i * 171) >> 9)
    lane = iota((ALL_SLOTS, 128), 1)

    z_wait(0)
    got = zrecv[0].reshape(slots, SIDE)
    spare_rows = dot(squeeze_spare, got)
    first, second = spare_rows[:, 0:128], spare_rows[:, 128:256]
    tail = jnp.where(
        k_kept == 0, first, jnp.where(k_kept == 1, pltpu.roll(first, TAIL, 1), second)
    )
    flag = jnp.sum(jnp.where(lane == TAIL + k_kept, second, 0.0), axis=1, keepdims=True)
    tail = jnp.where(lane < TAIL, tail, flag)
    xg0[x] = jnp.concatenate((dot(squeeze, got), tail), axis=1).astype(BF16)
    x_open(0)
    ring_steps(early, 2, 3)
    for d in (0, 1):
        ring(2, d, 0, 0).start()
    ring_steps(early, 3, 4)
    z_wait(1)
    xg1[x] = dot(squeeze, zrecv[1].reshape(slots, SIDE)).astype(BF16)
    x_open(1)
    ring_steps(early, 4, 5)
    ring_steps(late, 1, 2)
    x_wait(0)

    before = ones_where(iota((ALL_SLOTS, ALL_SLOTS), 0) < iota((ALL_SLOTS, ALL_SLOTS), 1))
    flag_lane = ones_where(iota((16, 128), 1) == TAIL)
    my_gain = gain[pl.ds(pl.multiple_of(y * NC * FEAT, 128), NC * FEAT)].reshape(1, NC * FEAT)
    my_gain = jnp.where(c == 0, my_gain[:, :FEAT], my_gain[:, FEAT:])
    table = jnp.zeros((8, 128), F32)
    sub = iota((8, 128), 0)

    def share(dx):
        return remote(
            xs.at[c, dx], xs.at[c, dx], cs_s.at[dx], cs_r.at[dx], dev(x, z, y, 1 - c)
        )

    def share_in(dx):
        return remote(
            xs.at[1 - c, dx], xs.at[1 - c, dx], cs_s.at[dx], cs_r.at[dx], dev(x, z, y, 1 - c)
        )

    def keep(dx, low_column, rows):
        high_column = low_column + rows.shape[1]
        judged[dx, :, low_column:high_column] = rows.astype(BF16)
        xs[c, dx, :, low_column:high_column] = (
            rows * my_gain[:, low_column:high_column]
        ).astype(BF16)
        return jnp.sum(rows * rows, axis=1, keepdims=True)

    places, sums = [], []
    for dx in range(NX):
        s = xg0[:, dx * KEPT:(dx + 1) * KEPT, :].reshape(ALL_SLOTS, WIDE)
        filled = dot(flag_lane, s[:, SIDE:WIDE], NTR)
        rank = dot(filled.astype(BF16), before)
        key = jnp.where(filled > 0.5, rank, -1.0)[0:1]
        place = ones_where(iota((ROWS, ALL_SLOTS), 0).astype(F32) == key)
        rows = dot(place, s)
        places.append(place)
        sums.append(
            keep(dx, 0, rows[:, 0:SIDE]) + keep(dx, 2 * SIDE, rows[:, SIDE:SIDE + TAIL])
        )
        if dx == 1:
            ring_steps(early, 5, 6)
            ring_steps(late, 2, 3)

    ring_steps(early, 6, last - 1)
    ring_steps(late, 3, 4)
    x_wait(1)
    for dx in range(NX):
        s = xg1[:, dx * KEPT:(dx + 1) * KEPT, :].reshape(ALL_SLOTS, SIDE)
        total = sums[dx] + keep(dx, SIDE, dot(places[dx], s))
        share(dx).start()
        table = jnp.where(sub == dx, column_to_row(total), table)
        if dx == 1:
            ring_last_sends(early)
            ring_steps(late, 4, 5)

    sq_in[0] = table

    def squares_out(k):
        return remote(
            sq_in.at[0], sq_in.at[k], sq_s.at[k], sq_r.at[k],
            {"pair": pair, "tensor": ((ten + k) & (NT - 1))},
        )

    @pl.loop(1, NT)
    def _(k):
        squares_out(k).start()

    ring_close(early)
    for dx in range(NX):
        share_in(dx).wait_recv()

    first = xs[0].reshape(NX * ROWS, FEAT)
    second = xs[1].reshape(NX * ROWS, FEAT)
    def products(p):
        w = w32[p].astype(BF16)
        t = dot(first, w[:FEAT]) + dot(second, w[FEAT:])
        return t.astype(BF16).reshape(NX, ROWS, 256)

    def sum_out(n, k):
        t = ((y + k) & (NY - 1))
        src = (part.at[1, t], part.at[1, ((t + NY // 2) & (NY - 1))], part.at[0, t])[n]
        return remote(
            src, part_in.at[n, k], rs_s.at[n, k], rs_r.at[n, k], dev(x, z, t, c)
        )

    part[1] = products(1)
    for k in (2, 1, 3):
        sum_out(0, k).start()
    part[0] = products(0)
    for n in (2, 1):
        for k in (2, 1, 3):
            sum_out(n, k).start()

    ring_steps(late, 5, last - 1)

    @pl.when(off_diagonal)
    def _():
        for p in range(4):
            turned(p).wait_send()

    for h in (0, 1):
        @pl.loop(1, NZ)
        def _(k):
            z_out(h, k).wait_send()

    def ring_left(p):
        @pl.loop(0, last - 1)
        def _(s):
            ring(p, 0, s, s).wait_send()
            ring(p, 1, s, s).wait_send()

        ring(p, 0, last - 1, last - 1).wait_send()

    for p in early:
        ring_left(p)
    for h in (0, 1):
        for k in range(1, NX):
            x_out(h, k).wait_send()
    for dx in range(NX):
        share(dx).wait_send()

    @pl.loop(1, NT)
    def _(k):
        squares_out(k).wait_send()

    @pl.loop(1, NT)
    def _(k):
        squares_out(k).wait_recv()

    total = sq_in[0]
    for k in range(1, NT):
        total = total + sq_in[k]
    far_y = ((y + NY // 2) & (NY - 1))
    width = float(NT * FEAT)

    def row_scale(which):
        row = jnp.sum(jnp.where(sub == which, total, 0.0), axis=0, keepdims=True)
        return lax.rsqrt(row_to_column(row, ROWS) / width + epsilon)

    scale_own, scale_far = row_scale(y), row_scale(far_y)
    def summed(n, mine, scale):
        for k in range(1, NY):
            sum_out(n, k).wait_recv()
        t = mine.astype(F32)
        for k in range(1, NY):
            t = t + part_in[n, k].astype(F32)
        return (t * scale).astype(BF16)

    kv = summed(0, part[1, y], scale_own)
    q_own = summed(2, part[0, y], scale_own)

    queries = jnp.concatenate((q_own[:, 0:HD], q_own[:, HD:2 * HD]), axis=0)
    col = iota((2 * ROWS, ROWS), 1)
    row = iota((2 * ROWS, ROWS), 0)
    row = jnp.where(row >= ROWS, row - ROWS, row)
    resp_q, resp_k = row >> 5, col >> 5
    spot_q, spot_k = row & (LEN - 1), col & (LEN - 1)

    def by_response(resp, values):
        return jnp.where(resp == 0, values[0], jnp.where(resp == 1, values[1], values[2]))

    own_lens = [lens[(y * NZ + z) * RESP + k] for k in range(RESP)]
    far_lens = [lens[(far_y * NZ + z) * RESP + k] for k in range(RESP)]
    partner = by_response(resp_q, [slot_in[0:1, k:k + 1] for k in range(RESP)])
    own_ok = (resp_q == resp_k) & (spot_k <= spot_q) & (spot_k < by_response(resp_k, own_lens))
    far_ok = (partner == resp_k) & (spot_k < by_response(resp_k, far_lens))

    def powers(keys, ok):
        scores = dot(queries, keys, NTR) * score_scale
        scores = soft_cap * jnp.tanh(scores / soft_cap)
        return jnp.exp(jnp.where(ok, scores, negative))

    def weigh(keys_values, ok):
        p = powers(keys_values[:, 0:HD], ok)
        return jnp.sum(p, axis=1, keepdims=True), dot(p.astype(BF16), keys_values[:, HD:2 * HD])

    whole, mixed = weigh(kv, own_ok)
    ring_last_sends(late)
    far_whole, far_mixed = weigh(summed(1, part[1, far_y], scale_far), far_ok)
    mixed = (mixed + far_mixed) / (whole + far_whole)
    row = iota((2 * ROWS, HD), 0)
    row = jnp.where(row >= ROWS, row - ROWS, row)
    present = (row & (LEN - 1)) < by_response(row >> 5, own_lens)
    mixed = jnp.where(present, mixed, 0.0).astype(BF16)
    ctx[y] = jnp.concatenate((mixed[:ROWS], mixed[ROWS:]), axis=1)

    def ctx_out(k):
        return remote(ctx.at[y], ctx.at[y], cx_s.at[k], cx_r.at[k], dev(x, z, ((y + k) & (NY - 1)), c))

    def ctx_in(k):
        f = ((y + NY - k) & (NY - 1))
        return remote(ctx.at[f], ctx.at[f], cx_s.at[k], cx_r.at[k], dev(x, z, f, c))

    for k in (2, 1, 3):
        ctx_out(k).start()
    ring_close(late)

    def out_rows(half):
        return w32[2, pl.ds(pl.multiple_of(half * FEAT, 8), FEAT), :].astype(BF16)

    w_other, w_mine = out_rows(1 - c), out_rows(c)

    def swap(k):
        t = ((y + NY - k) & (NY - 1))
        return remote(
            co_out.at[t], co_in.at[t], co_s.at[k], co_r.at[k], dev(x, z, y, 1 - c)
        )

    def xsum(k):
        t = ((x + k) & (NX - 1))
        return remote(xo_out.at[t], xo_in.at[k], xo_s.at[k], xo_r.at[k], dev(t, z, y, c))

    order = (0, 1, 3, 2)
    for k in order:
        t = ((y + NY - k) & (NY - 1))
        if k > 0:
            ctx_in(k).wait_recv()
        co_out[t] = dot(ctx[t], w_other, NTR).astype(BF16)
        swap(k).start()
        xo_out[t] = dot(ctx[t], w_mine, NTR).astype(BF16)
    for k in order:
        t = ((y + NY - k) & (NY - 1))
        swap(k).wait_recv()
        xo_out[t] = (xo_out[t].astype(F32) + co_in[t].astype(F32)).astype(BF16)

        @pl.when(t != x)
        def _():
            xsum(((t + NX - x) & (NX - 1))).start()

    attended = xo_out[x].astype(F32)
    for k in (1, 3, 2):
        xsum(k).wait_recv()
        attended = attended + xo_in[k].astype(F32)

    squares = column_to_row(jnp.sum(attended * attended, axis=1, keepdims=True))
    fin_in[0] = jnp.where(sub == 0, squares, 0.0)

    def fin_out(k):
        return remote(
            fin_in.at[0], fin_in.at[k], fn_s.at[k], fn_r.at[k],
            {"pair": pair, "tensor": ((ten + k) & (NT - 1))},
        )

    @pl.loop(1, NT)
    def _(k):
        fin_out(k).start()

    ring_left(2)
    for k in range(1, NY):
        for n in range(3):
            sum_out(n, k).wait_send()
        ctx_out(k).wait_send()
        xsum(k).wait_send()
    for k in order:
        swap(k).wait_send()

    residual = judged[x].astype(F32)
    gained = attended * post[...].reshape(1, FEAT)

    @pl.loop(1, NT)
    def _(k):
        fin_out(k).wait_recv()

    total = fin_in[0]
    for k in range(1, NT):
        total = total + fin_in[k]
    scale = lax.rsqrt(row_to_column(total[0:1], ROWS) / width + epsilon)
    out[...] = (residual + gained * scale).astype(BF16)

    @pl.loop(1, NT)
    def _(k):
        fin_out(k).wait_send()


def shards(
    rollout, counts, lengths, partner_slot, pre_gain, post_gain,
    query_weight, key_weight, value_weight, out_weight,
):
    vmem = pl.BlockSpec(memory_space=pltpu.VMEM)
    hbm = pl.BlockSpec(memory_space=pltpu.HBM)
    smem = pl.BlockSpec(memory_space=pltpu.SMEM)
    dma = pltpu.SemaphoreType.DMA
    scratch = [
        pltpu.VMEM((ROWS, FEAT), BF16),
        pltpu.VMEM((WROWS, 256), BF16),
        pltpu.VMEM((WROWS, HD), BF16),
        pltpu.VMEM((WROWS, HD), BF16),
        pltpu.VMEM((WROWS, 256), BF16),
        dma((5,)),
        pltpu.VMEM((ROWS, 128), BF16),
        pltpu.VMEM((2, NZ, SLOTS, SIDE), BF16),
        pltpu.VMEM((2, NZ, SLOTS, SIDE), BF16),
        pltpu.VMEM((3, 2 * WROWS, HD), BF16),
        pltpu.VMEM((NZ, 3, 2 * WROWS, HD), BF16),
        pltpu.VMEM((3, BLOCK, 2 * HD), F32),
        pltpu.VMEM((8, 128), I32),
        pltpu.VMEM((8, 128), I32),
        pltpu.VMEM((NX, ALL_SLOTS, WIDE), BF16),
        pltpu.VMEM((NX, ALL_SLOTS, SIDE), BF16),
        pltpu.VMEM((NC, NX, ROWS, FEAT), BF16),
        pltpu.VMEM((NX, ROWS, FEAT), BF16),
        pltpu.VMEM((NT, 8, 128), F32),
        pltpu.VMEM((NT, 8, 128), F32),
        pltpu.VMEM((2, NX, ROWS, 256), BF16),
        pltpu.VMEM((3, NY, ROWS, 256), BF16),
        pltpu.VMEM((NY, ROWS, 256), BF16),
        pltpu.VMEM((NX, ROWS, FEAT), BF16),
        pltpu.VMEM((NX, ROWS, FEAT), BF16),
        pltpu.VMEM((NX, ROWS, FEAT), BF16),
        pltpu.VMEM((NX, ROWS, FEAT), BF16),
        dma((4,)), dma((4,)),
        dma((2, NZ)), dma((2, NZ)),
        dma((3, 2, NZ // 2)), dma((3, 2, NZ // 2)),
        dma((2, NX)), dma((2, NX)),
        dma((NX,)), dma((NX,)),
        dma((NT,)), dma((NT,)),
        dma((3, NY)), dma((3, NY)),
        dma((NY,)), dma((NY,)),
        dma((NX,)), dma((NX,)),
        dma((NX,)), dma((NX,)),
        dma((NT,)), dma((NT,)),
    ]
    return pl.pallas_call(
        kernel,
        out_shape=jax.ShapeDtypeStruct((ROWS, FEAT), BF16),
        in_specs=[hbm, vmem, smem, vmem, vmem, vmem, hbm, hbm, hbm, hbm],
        out_specs=vmem,
        scratch_shapes=scratch,
        compiler_params=pltpu.CompilerParams(
            collective_id=0, has_side_effects=True, vmem_limit_bytes=62 * 1024 * 1024
        ),
    )(
        rollout, counts, lengths, partner_slot, pre_gain,
        post_gain, query_weight, key_weight, value_weight, out_weight,
    )


def solution(mesh):
    placed = (
        P("pair", "tensor"),
        P("pair", None),
        P(),
        P("pair", None),
        P(),
        P("tensor"),
        P("pair", "tensor"),
        P("pair", "tensor"),
        P("pair", "tensor"),
        P("pair", "tensor"),
    )
    return jax.shard_map(
        shards, mesh=mesh, in_specs=placed, out_specs=P("pair", "tensor"), check_vma=False
    )
```

```python
import jax
import jax.numpy as jnp
from jax import lax
from jax.experimental import pallas as pl
from jax.experimental.pallas import tpu as pltpu
from jax.sharding import PartitionSpec as P

NX, NY, NZ, NC = 4, 4, 16, 2
NT = NY * NC
HD = 128
LEN = 32
RESP = 3
ROWS = RESP * LEN
FEAT = 576
SIDE = 256
TAIL = FEAT - 2 * SIDE
WIDE = SIDE + 128
WROWS = 72
BLOCK = NZ * WROWS
CAP = 3
SLOTS = NX * 4
KEPT = NZ * CAP
ALL_SLOTS = NX * KEPT

score_scale = 144.0 ** (-0.5)
soft_cap = 50.0
epsilon = 1e-06
negative = -1e30

F32 = jnp.float32
BF16 = jnp.bfloat16
I32 = jnp.int32
MESH = pl.DeviceIdType.MESH
NN = (((1,), (0,)), ((), ()))
NTR = (((1,), (1,)), ((), ()))


def dot(a, b, dims=NN):
    return lax.dot_general(a, b, dims, preferred_element_type=F32)


def iota(shape, dim):
    return lax.broadcasted_iota(I32, shape, dim)


def ones_where(cond):
    return jnp.where(cond, 1.0, 0.0).astype(BF16)


def column_to_row(col):
    rows = col.shape[0]
    same = iota((rows, 128), 0) == iota((rows, 128), 1)
    return jnp.sum(jnp.where(same, col, 0.0), axis=0, keepdims=True)


def row_to_column(row, rows):
    same = iota((rows, 128), 0) == iota((rows, 128), 1)
    return jnp.sum(jnp.where(same, row, 0.0), axis=1, keepdims=True)


def kernel(
    roll_h, counts, lens, pslot, gain, post, wq_h, wk_h, wv_h, wo_h, out,
    roll, wq, wk, wv, wo, in_s, low, zsend, zrecv, wsend, wbuf, w32, slot_out, slot_in, xg0, xg1, xs, judged, sq_in, fin_in,
    part, part_in, ycomb, ctx, co_out, co_in, xo_out, xo_in,
    tr_s, tr_r, za_s, za_r, ring_s, ring_r, xg_s, xg_r, cs_s, cs_r, sq_s, sq_r,
    rs_s, rs_r, cx_s, cx_r, co_s, co_r, xo_s, xo_r, fn_s, fn_r,
):
    pair = lax.axis_index("pair")
    ten = lax.axis_index("tensor")
    x, z = pair >> 4, pair & (NZ - 1)
    y, c = ten >> 1, ten & (NC - 1)

    def dev(xx, zz, yy, cc):
        return {"pair": xx * NZ + zz, "tensor": yy * NC + cc}

    def remote(src, dst, send, recv, where):
        return pltpu.make_async_remote_copy(
            src_ref=src, dst_ref=dst, send_sem=send, recv_sem=recv,
            device_id=where, device_id_type=MESH,
        )

    off_diagonal = x != y

    loads = [
        pltpu.make_async_copy(a, b, in_s.at[n])
        for n, (a, b) in enumerate(
            ((roll_h, roll), (wq_h, wq), (wk_h, wk), (wv_h, wv), (wo_h, wo))
        )
    ]
    for load in loads:
        load.start()

    barrier = pltpu.get_barrier_semaphore()

    def greet(where):
        pl.semaphore_signal(barrier, inc=1, device_id=where, device_id_type=MESH)

    @pl.loop(1, NZ)
    def _(k):
        greet(dev(x, ((z + k) & (NZ - 1)), y, c))

    @pl.loop(1, NX)
    def _(k):
        greet(dev(((x + k) & (NX - 1)), z, y, c))

    @pl.loop(1, NT)
    def _(k):
        greet({"pair": pair, "tensor": ((ten + k) & (NT - 1))})

    @pl.when(off_diagonal)
    def _():
        greet(dev(y, z, x, c))

    slots = NZ * SLOTS
    j = iota((slots, NX * NZ), 0)
    dest = ((j >> 2) & (NX - 1)) * NZ + (j >> 4)
    other = iota((slots, NX * NZ), 1)
    sending = counts[...].astype(F32)
    start = jnp.sum(jnp.where(other < dest, sending, 0.0), axis=1, keepdims=True)
    amount = jnp.sum(jnp.where(other == dest, sending, 0.0), axis=1, keepdims=True)
    k_slot = (iota((slots, 1), 0) & 3).astype(F32)
    spare = k_slot == CAP
    row_of = iota((slots, ROWS), 1).astype(F32)

    def picking(cond, k):
        return ones_where(jnp.where(cond & (amount > k), start + k, -1.0) == row_of)

    pick = picking(k_slot < CAP, k_slot)
    pick_tail = [picking(spare, float(k)) for k in range(CAP)]
    spot = iota((slots, 128), 1) - TAIL
    flags = jnp.where(
        spare & (spot >= 0) & (spot < CAP) & (spot.astype(F32) < amount), 1.0, 0.0
    )
    low[...] = jnp.zeros((ROWS, 128), BF16)
    loads[0].wait()
    low[:, 0:TAIL] = roll[:, 2 * SIDE:FEAT]
    low_tail = low[...]
    high_tail = pltpu.roll(low_tail.astype(F32), TAIL, 1).astype(BF16)
    base = dot(pick, roll[:, 0:2 * SIDE])
    tile0 = base[:, 0:128] + dot(pick_tail[0], low_tail) + dot(pick_tail[1], high_tail)
    tile1 = base[:, 128:256] + dot(pick_tail[2], low_tail) + flags
    zsend[0] = jnp.concatenate((tile0, tile1), axis=1).astype(BF16).reshape(NZ, SLOTS, SIDE)
    zsend[1] = base[:, SIDE:].astype(BF16).reshape(NZ, SLOTS, SIDE)
    for h in (0, 1):
        zrecv[h, z] = zsend[h, z]

    for load in loads[1:]:
        load.wait()

    def pack(p, first, second):
        wsend[p] = jnp.concatenate(
            (first.astype(F32), second.astype(F32)), axis=0
        ).astype(BF16)

    pack(0, wq[:, :HD], wq[:, HD:])
    pack(1, wk[...], wv[...])
    pack(2, wo[:, :HD], wo[:, HD:])
    lane = iota((8, 128), 1)
    spread = jnp.zeros((8, 128), I32)
    for k in range(RESP):
        spread = jnp.where(lane == k, pslot[0:1, k:k + 1], spread)
    slot_out[...] = spread

    greeted = NZ - 1 + NX - 1 + NT - 1

    @pl.when(off_diagonal)
    def _():
        pl.semaphore_wait(barrier, greeted + 1)

    @pl.when(jnp.logical_not(off_diagonal))
    def _():
        pl.semaphore_wait(barrier, greeted)

    def z_out(h, k):
        t = ((z + k) & (NZ - 1))
        return remote(
            zsend.at[h, t], zrecv.at[h, z], za_s.at[h, k], za_r.at[h, k], dev(x, t, y, c)
        )

    def z_in(h, k):
        f = ((z + NZ - k) & (NZ - 1))
        return remote(
            zsend.at[h, f], zrecv.at[h, f], za_s.at[h, k], za_r.at[h, k], dev(x, f, y, c)
        )

    def turned(p):
        src, dst = (slot_out, slot_in) if p == 3 else (wsend.at[p], wbuf.at[z, p])
        return remote(src, dst, tr_s.at[p], tr_r.at[p], dev(y, z, x, c))

    @pl.when(off_diagonal)
    def _():
        for p in range(4):
            turned(p).start()

    for h in (0, 1):
        z_out(h, NZ // 2).start()

        @pl.loop(1, NZ // 2)
        def _(k):
            z_out(h, NZ // 2 - k).start()
            z_out(h, NZ // 2 + k).start()

    @pl.when(jnp.logical_not(off_diagonal))
    def _():
        wbuf[z] = wsend[...]
        slot_in[...] = slot_out[...]

    up, down = ((z + 1) & (NZ - 1)), ((z + NZ - 1) & (NZ - 1))

    def ring_block(d, s):
        return ((z + NZ - s) & (NZ - 1)) if d == 1 else ((z + s) & (NZ - 1))

    def ring(p, d, s, distance):
        block = wbuf.at[ring_block(d, distance), p]
        return remote(
            block, block, ring_s.at[p, d, s], ring_r.at[p, d, s],
            dev(x, up if d == 1 else down, y, c),
        )

    def unpack(p, block):
        v = wbuf[block, p].astype(F32)
        at = pl.ds(pl.multiple_of(block * WROWS, 8), WROWS)
        w32[p, at, 0:HD] = v[:WROWS]
        w32[p, at, HD:2 * HD] = v[WROWS:]

    def ring_steps(pieces, low, high):
        @pl.loop(low, high)
        def _(s):
            for p in pieces:
                for d in (0, 1):
                    ring(p, d, s - 1, s).wait_recv()
                    ring(p, d, s, s).start()
            for p in pieces:
                for d in (0, 1):
                    unpack(p, ring_block(d, s))

    last = NZ // 2

    def ring_last_sends(pieces):
        for p in pieces:
            for d in (0, 1):
                ring(p, d, last - 2, last - 1).wait_recv()
            ring(p, 0, last - 1, last - 1).start()
        for p in pieces:
            for d in (0, 1):
                unpack(p, ring_block(d, last - 1))

    def ring_close(pieces):
        for p in pieces:
            ring(p, 0, last - 1, last).wait_recv()
            unpack(p, ring_block(0, last))

    early, late = (0, 1), (2,)
    for p in (0, 1, 2):
        @pl.when(off_diagonal)
        def _():
            turned(p).wait_recv()

        if p in early:
            ring(p, 0, 0, 0).start()
            ring(p, 1, 0, 0).start()
    for p in (0, 1, 2):
        unpack(p, z)

    @pl.when(off_diagonal)
    def _():
        turned(3).wait_recv()

    ring_steps(early, 1, 2)

    def z_wait(h):
        @pl.loop(1, NZ)
        def _(k):
            z_in(h, k).wait_recv()

    held = (xg0, xg1)

    def x_copy(h, k, block, target):
        ref = held[h].at[block]
        return remote(ref, ref, xg_s.at[h, k], xg_r.at[h, k], dev(target, z, y, c))

    def x_out(h, k):
        return x_copy(h, k, x, (x + k) & (NX - 1))

    def x_in(h, k):
        f = (x + NX - k) & (NX - 1)
        return x_copy(h, k, f, f)

    def x_open(h):
        for k in (2, 1, 3):
            x_out(h, k).start()

    def x_wait(h):
        for k in (1, 3, 2):
            x_in(h, k).wait_recv()

    i = iota((ALL_SLOTS, slots), 0)
    q = (i * 171) >> 9
    at = iota((ALL_SLOTS, slots), 1) - (q & (NZ - 1)) * SLOTS - (q >> 4) * 4
    squeeze = ones_where(at == i - 3 * q)
    squeeze_spare = ones_where(at == CAP)
    i = iota((ALL_SLOTS, 128), 0)
    k_kept = i - 3 * ((i * 171) >> 9)
    lane = iota((ALL_SLOTS, 128), 1)

    z_wait(0)
    got = zrecv[0].reshape(slots, SIDE)
    spare_rows = dot(squeeze_spare, got)
    first, second = spare_rows[:, 0:128], spare_rows[:, 128:256]
    tail = jnp.where(
        k_kept == 0, first, jnp.where(k_kept == 1, pltpu.roll(first, TAIL, 1), second)
    )
    flag = jnp.sum(jnp.where(lane == TAIL + k_kept, second, 0.0), axis=1, keepdims=True)
    tail = jnp.where(lane < TAIL, tail, flag)
    xg0[x] = jnp.concatenate((dot(squeeze, got), tail), axis=1).astype(BF16)
    x_open(0)
    ring_steps(early, 2, 3)
    for d in (0, 1):
        ring(2, d, 0, 0).start()
    ring_steps(early, 3, 4)
    z_wait(1)
    xg1[x] = dot(squeeze, zrecv[1].reshape(slots, SIDE)).astype(BF16)
    x_open(1)
    ring_steps(early, 4, 5)
    ring_steps(late, 1, 2)
    x_wait(0)

    before = ones_where(iota((ALL_SLOTS, ALL_SLOTS), 0) < iota((ALL_SLOTS, ALL_SLOTS), 1))
    flag_lane = ones_where(iota((16, 128), 1) == TAIL)
    my_gain = gain[pl.ds(pl.multiple_of(y * NC * FEAT, 128), NC * FEAT)].reshape(1, NC * FEAT)
    my_gain = jnp.where(c == 0, my_gain[:, :FEAT], my_gain[:, FEAT:])
    table = jnp.zeros((8, 128), F32)
    sub = iota((8, 128), 0)

    def share(dx):
        return remote(
            xs.at[c, dx], xs.at[c, dx], cs_s.at[dx], cs_r.at[dx], dev(x, z, y, 1 - c)
        )

    def share_in(dx):
        return remote(
            xs.at[1 - c, dx], xs.at[1 - c, dx], cs_s.at[dx], cs_r.at[dx], dev(x, z, y, 1 - c)
        )

    def keep(dx, low_column, rows):
        high_column = low_column + rows.shape[1]
        judged[dx, :, low_column:high_column] = rows.astype(BF16)
        xs[c, dx, :, low_column:high_column] = (
            rows * my_gain[:, low_column:high_column]
        ).astype(BF16)
        return jnp.sum(rows * rows, axis=1, keepdims=True)

    places, sums = [], []
    for dx in range(NX):
        s = xg0[:, dx * KEPT:(dx + 1) * KEPT, :].reshape(ALL_SLOTS, WIDE)
        filled = dot(flag_lane, s[:, SIDE:WIDE], NTR)
        rank = dot(filled.astype(BF16), before)
        key = jnp.where(filled > 0.5, rank, -1.0)[0:1]
        place = ones_where(iota((ROWS, ALL_SLOTS), 0).astype(F32) == key)
        rows = dot(place, s)
        places.append(place)
        sums.append(
            keep(dx, 0, rows[:, 0:SIDE]) + keep(dx, 2 * SIDE, rows[:, SIDE:SIDE + TAIL])
        )
        if dx == 1:
            ring_steps(early, 5, 6)
            ring_steps(late, 2, 3)

    ring_steps(early, 6, last - 1)
    ring_steps(late, 3, 4)
    x_wait(1)
    for dx in range(NX):
        s = xg1[:, dx * KEPT:(dx + 1) * KEPT, :].reshape(ALL_SLOTS, SIDE)
        total = sums[dx] + keep(dx, SIDE, dot(places[dx], s))
        share(dx).start()
        table = jnp.where(sub == dx, column_to_row(total), table)
        if dx == 1:
            ring_last_sends(early)
            ring_steps(late, 4, 5)

    sq_in[0] = table

    def squares_out(k):
        return remote(
            sq_in.at[0], sq_in.at[k], sq_s.at[k], sq_r.at[k],
            {"pair": pair, "tensor": ((ten + k) & (NT - 1))},
        )

    @pl.loop(1, NT)
    def _(k):
        squares_out(k).start()

    ring_close(early)
    for dx in range(NX):
        share_in(dx).wait_recv()

    first = xs[0].reshape(NX * ROWS, FEAT)
    second = xs[1].reshape(NX * ROWS, FEAT)
    def products(p):
        w = w32[p].astype(BF16)
        t = dot(first, w[:FEAT]) + dot(second, w[FEAT:])
        return t.astype(BF16).reshape(NX, ROWS, 256)

    key_values = products(1)
    part[:, :, 256:512] = key_values
    for dx in range(NX):
        part[dx, :, 512:768] = key_values[(dx + NX // 2) % NX]
    part[:, :, 0:256] = products(0)

    halves = (pl.ds(0, ROWS // 2), pl.ds(ROWS // 2, ROWS // 2))

    def y_near(d):
        return ((y + 1) & (NY - 1)) if d == 0 else ((y + NY - 1) & (NY - 1))

    def ysum(stage, d):
        t = y_near(d)
        src = (
            part.at[(y + NY // 2) & (NY - 1), halves[d]], part.at[t, halves[1 - d]], ycomb.at[d]
        )[stage]
        return remote(
            src, part_in.at[stage, d], rs_s.at[stage, d], rs_r.at[stage, d], dev(x, z, t, c)
        )

    for stage in (0, 1):
        for d in (0, 1):
            ysum(stage, d).start()
    for d in (0, 1):
        ysum(0, d).wait_recv()
        mine = part[y_near(d), halves[d]].astype(F32)
        ycomb[d] = (mine + part_in[0, d].astype(F32)).astype(BF16)
        ysum(2, d).start()

    ring_steps(late, 5, last - 1)

    @pl.when(off_diagonal)
    def _():
        for p in range(4):
            turned(p).wait_send()

    for h in (0, 1):
        @pl.loop(1, NZ)
        def _(k):
            z_out(h, k).wait_send()

    def ring_left(p):
        @pl.loop(0, last - 1)
        def _(s):
            ring(p, 0, s, s).wait_send()
            ring(p, 1, s, s).wait_send()

        ring(p, 0, last - 1, last - 1).wait_send()

    for p in early:
        ring_left(p)
    for h in (0, 1):
        for k in range(1, NX):
            x_out(h, k).wait_send()
    for dx in range(NX):
        share(dx).wait_send()

    @pl.loop(1, NT)
    def _(k):
        squares_out(k).wait_send()

    @pl.loop(1, NT)
    def _(k):
        squares_out(k).wait_recv()

    total = sq_in[0]
    for k in range(1, NT):
        total = total + sq_in[k]
    far_y = ((y + NY // 2) & (NY - 1))
    width = float(NT * FEAT)

    def row_scale(which):
        row = jnp.sum(jnp.where(sub == which, total, 0.0), axis=0, keepdims=True)
        return lax.rsqrt(row_to_column(row, ROWS) / width + epsilon)

    scale_own, scale_far = row_scale(y), row_scale(far_y)
    for stage in (1, 2):
        for d in (0, 1):
            ysum(stage, d).wait_recv()
    both = part[y].astype(F32) + jnp.concatenate(
        (
            part_in[2, 0].astype(F32) + part_in[1, 1].astype(F32),
            part_in[2, 1].astype(F32) + part_in[1, 0].astype(F32),
        ),
        axis=0,
    )
    q_own = (both[:, 0:256] * scale_own).astype(BF16)
    kv = (both[:, 256:512] * scale_own).astype(BF16)
    kv_far = (both[:, 512:768] * scale_far).astype(BF16)

    queries = jnp.concatenate((q_own[:, 0:HD], q_own[:, HD:2 * HD]), axis=0)
    col = iota((2 * ROWS, ROWS), 1)
    row = iota((2 * ROWS, ROWS), 0)
    row = jnp.where(row >= ROWS, row - ROWS, row)
    resp_q, resp_k = row >> 5, col >> 5
    spot_q, spot_k = row & (LEN - 1), col & (LEN - 1)

    def by_response(resp, values):
        return jnp.where(resp == 0, values[0], jnp.where(resp == 1, values[1], values[2]))

    own_lens = [lens[(y * NZ + z) * RESP + k] for k in range(RESP)]
    far_lens = [lens[(far_y * NZ + z) * RESP + k] for k in range(RESP)]
    partner = by_response(resp_q, [slot_in[0:1, k:k + 1] for k in range(RESP)])
    own_ok = (resp_q == resp_k) & (spot_k <= spot_q) & (spot_k < by_response(resp_k, own_lens))
    far_ok = (partner == resp_k) & (spot_k < by_response(resp_k, far_lens))

    def powers(keys, ok):
        scores = dot(queries, keys, NTR) * score_scale
        scores = soft_cap * jnp.tanh(scores / soft_cap)
        return jnp.exp(jnp.where(ok, scores, negative))

    def weigh(keys_values, ok):
        p = powers(keys_values[:, 0:HD], ok)
        return jnp.sum(p, axis=1, keepdims=True), dot(p.astype(BF16), keys_values[:, HD:2 * HD])

    whole, mixed = weigh(kv, own_ok)
    ring_last_sends(late)
    far_whole, far_mixed = weigh(kv_far, far_ok)
    mixed = (mixed + far_mixed) / (whole + far_whole)
    row = iota((2 * ROWS, HD), 0)
    row = jnp.where(row >= ROWS, row - ROWS, row)
    present = (row & (LEN - 1)) < by_response(row >> 5, own_lens)
    mixed = jnp.where(present, mixed, 0.0).astype(BF16)
    ctx[y] = jnp.concatenate((mixed[:ROWS], mixed[ROWS:]), axis=1)

    def ctx_out(k):
        return remote(ctx.at[y], ctx.at[y], cx_s.at[k], cx_r.at[k], dev(x, z, ((y + k) & (NY - 1)), c))

    def ctx_in(k):
        f = ((y + NY - k) & (NY - 1))
        return remote(ctx.at[f], ctx.at[f], cx_s.at[k], cx_r.at[k], dev(x, z, f, c))

    for k in (2, 1, 3):
        ctx_out(k).start()
    ring_close(late)

    def out_rows(half):
        return w32[2, pl.ds(pl.multiple_of(half * FEAT, 8), FEAT), :].astype(BF16)

    w_other, w_mine = out_rows(1 - c), out_rows(c)

    def swap(k):
        t = ((y + NY - k) & (NY - 1))
        return remote(
            co_out.at[t], co_in.at[t], co_s.at[k], co_r.at[k], dev(x, z, y, 1 - c)
        )

    def xsum(k):
        t = ((x + k) & (NX - 1))
        return remote(xo_out.at[t], xo_in.at[k], xo_s.at[k], xo_r.at[k], dev(t, z, y, c))

    order = (0, 1, 3, 2)
    for k in order:
        t = ((y + NY - k) & (NY - 1))
        if k > 0:
            ctx_in(k).wait_recv()
        co_out[t] = dot(ctx[t], w_other, NTR).astype(BF16)
        swap(k).start()
        xo_out[t] = dot(ctx[t], w_mine, NTR).astype(BF16)
    for k in order:
        t = ((y + NY - k) & (NY - 1))
        swap(k).wait_recv()
        xo_out[t] = (xo_out[t].astype(F32) + co_in[t].astype(F32)).astype(BF16)

        @pl.when(t != x)
        def _():
            xsum(((t + NX - x) & (NX - 1))).start()

    attended = xo_out[x].astype(F32)
    for k in (1, 3, 2):
        xsum(k).wait_recv()
        attended = attended + xo_in[k].astype(F32)

    squares = column_to_row(jnp.sum(attended * attended, axis=1, keepdims=True))
    fin_in[0] = jnp.where(sub == 0, squares, 0.0)

    def fin_out(k):
        return remote(
            fin_in.at[0], fin_in.at[k], fn_s.at[k], fn_r.at[k],
            {"pair": pair, "tensor": ((ten + k) & (NT - 1))},
        )

    @pl.loop(1, NT)
    def _(k):
        fin_out(k).start()

    for stage in range(3):
        for d in (0, 1):
            ysum(stage, d).wait_send()
    ring_left(2)
    for k in range(1, NY):
        ctx_out(k).wait_send()
        xsum(k).wait_send()
    for k in order:
        swap(k).wait_send()

    residual = judged[x].astype(F32)
    gained = attended * post[...].reshape(1, FEAT)

    @pl.loop(1, NT)
    def _(k):
        fin_out(k).wait_recv()

    total = fin_in[0]
    for k in range(1, NT):
        total = total + fin_in[k]
    scale = lax.rsqrt(row_to_column(total[0:1], ROWS) / width + epsilon)
    out[...] = (residual + gained * scale).astype(BF16)

    @pl.loop(1, NT)
    def _(k):
        fin_out(k).wait_send()


def shards(
    rollout, counts, lengths, partner_slot, pre_gain, post_gain,
    query_weight, key_weight, value_weight, out_weight,
):
    vmem = pl.BlockSpec(memory_space=pltpu.VMEM)
    hbm = pl.BlockSpec(memory_space=pltpu.HBM)
    smem = pl.BlockSpec(memory_space=pltpu.SMEM)
    dma = pltpu.SemaphoreType.DMA
    scratch = [
        pltpu.VMEM((ROWS, FEAT), BF16),
        pltpu.VMEM((WROWS, 256), BF16),
        pltpu.VMEM((WROWS, HD), BF16),
        pltpu.VMEM((WROWS, HD), BF16),
        pltpu.VMEM((WROWS, 256), BF16),
        dma((5,)),
        pltpu.VMEM((ROWS, 128), BF16),
        pltpu.VMEM((2, NZ, SLOTS, SIDE), BF16),
        pltpu.VMEM((2, NZ, SLOTS, SIDE), BF16),
        pltpu.VMEM((3, 2 * WROWS, HD), BF16),
        pltpu.VMEM((NZ, 3, 2 * WROWS, HD), BF16),
        pltpu.VMEM((3, BLOCK, 2 * HD), F32),
        pltpu.VMEM((8, 128), I32),
        pltpu.VMEM((8, 128), I32),
        pltpu.VMEM((NX, ALL_SLOTS, WIDE), BF16),
        pltpu.VMEM((NX, ALL_SLOTS, SIDE), BF16),
        pltpu.VMEM((NC, NX, ROWS, FEAT), BF16),
        pltpu.VMEM((NX, ROWS, FEAT), BF16),
        pltpu.VMEM((NT, 8, 128), F32),
        pltpu.VMEM((NT, 8, 128), F32),
        pltpu.VMEM((NX, ROWS, 768), BF16),
        pltpu.VMEM((3, 2, ROWS // 2, 768), BF16),
        pltpu.VMEM((2, ROWS // 2, 768), BF16),
        pltpu.VMEM((NY, ROWS, 256), BF16),
        pltpu.VMEM((NX, ROWS, FEAT), BF16),
        pltpu.VMEM((NX, ROWS, FEAT), BF16),
        pltpu.VMEM((NX, ROWS, FEAT), BF16),
        pltpu.VMEM((NX, ROWS, FEAT), BF16),
        dma((4,)), dma((4,)),
        dma((2, NZ)), dma((2, NZ)),
        dma((3, 2, NZ // 2)), dma((3, 2, NZ // 2)),
        dma((2, NX)), dma((2, NX)),
        dma((NX,)), dma((NX,)),
        dma((NT,)), dma((NT,)),
        dma((3, 2)), dma((3, 2)),
        dma((NY,)), dma((NY,)),
        dma((NX,)), dma((NX,)),
        dma((NX,)), dma((NX,)),
        dma((NT,)), dma((NT,)),
    ]
    return pl.pallas_call(
        kernel,
        out_shape=jax.ShapeDtypeStruct((ROWS, FEAT), BF16),
        in_specs=[hbm, vmem, smem, vmem, vmem, vmem, hbm, hbm, hbm, hbm],
        out_specs=vmem,
        scratch_shapes=scratch,
        compiler_params=pltpu.CompilerParams(
            collective_id=0, has_side_effects=True, vmem_limit_bytes=62 * 1024 * 1024
        ),
    )(
        rollout, counts, lengths, partner_slot, pre_gain,
        post_gain, query_weight, key_weight, value_weight, out_weight,
    )


def solution(mesh):
    placed = (
        P("pair", "tensor"),
        P("pair", None),
        P(),
        P("pair", None),
        P(),
        P("tensor"),
        P("pair", "tensor"),
        P("pair", "tensor"),
        P("pair", "tensor"),
        P("pair", "tensor"),
    )
    return jax.shard_map(
        shards, mesh=mesh, in_specs=placed, out_specs=P("pair", "tensor"), check_vma=False
    )
```

```python
import jax
import jax.numpy as jnp
from jax import lax
from jax.experimental import pallas as pl
from jax.experimental.pallas import tpu as pltpu
from jax.sharding import PartitionSpec as P

NX, NY, NZ, NC = 4, 4, 16, 2
NT = NY * NC
HD = 128
LEN = 32
RESP = 3
ROWS = RESP * LEN
FEAT = 576
SIDE = 256
TAIL = FEAT - 2 * SIDE
WIDE = SIDE + 128
WROWS = 72
BLOCK = NZ * WROWS
CAP = 3
SLOTS = NX * 4
KEPT = NZ * CAP
ALL_SLOTS = NX * KEPT

score_scale = 144.0 ** (-0.5)
soft_cap = 50.0
epsilon = 1e-06
negative = -1e30

F32 = jnp.float32
BF16 = jnp.bfloat16
I32 = jnp.int32
MESH = pl.DeviceIdType.MESH
NN = (((1,), (0,)), ((), ()))
NTR = (((1,), (1,)), ((), ()))


def dot(a, b, dims=NN):
    return lax.dot_general(a, b, dims, preferred_element_type=F32)


def iota(shape, dim):
    return lax.broadcasted_iota(I32, shape, dim)


def ones_where(cond):
    return jnp.where(cond, 1.0, 0.0).astype(BF16)


def column_to_row(col):
    rows = col.shape[0]
    same = iota((rows, 128), 0) == iota((rows, 128), 1)
    return jnp.sum(jnp.where(same, col, 0.0), axis=0, keepdims=True)


def row_to_column(row, rows):
    same = iota((rows, 128), 0) == iota((rows, 128), 1)
    return jnp.sum(jnp.where(same, row, 0.0), axis=1, keepdims=True)


def kernel(
    roll_h, counts, lens, pslot, gain, post, wq_h, wk_h, wv_h, wo_h, out,
    roll, wq, wk, wv, wo, in_s, low, zsend, zrecv, wsend, wbuf, w32, slot_out, slot_in, xg0, xg1, xs, judged, sq_in, fin_in,
    part, part_in, ctx, co_out, co_in, xo_out, xo_in,
    tr_s, tr_r, za_s, za_r, ring_s, ring_r, xg_s, xg_r, cs_s, cs_r, sq_s, sq_r,
    rs_s, rs_r, cx_s, cx_r, co_s, co_r, xo_s, xo_r, fn_s, fn_r,
):
    pair = lax.axis_index("pair")
    ten = lax.axis_index("tensor")
    x, z = pair >> 4, pair & (NZ - 1)
    y, c = ten >> 1, ten & (NC - 1)

    def dev(xx, zz, yy, cc):
        return {"pair": xx * NZ + zz, "tensor": yy * NC + cc}

    def remote(src, dst, send, recv, where):
        return pltpu.make_async_remote_copy(
            src_ref=src, dst_ref=dst, send_sem=send, recv_sem=recv,
            device_id=where, device_id_type=MESH,
        )

    off_diagonal = x != y

    loads = [
        pltpu.make_async_copy(a, b, in_s.at[n])
        for n, (a, b) in enumerate(
            ((roll_h, roll), (wq_h, wq), (wk_h, wk), (wv_h, wv), (wo_h, wo))
        )
    ]
    for load in loads:
        load.start()

    barrier = pltpu.get_barrier_semaphore()

    def greet(where):
        pl.semaphore_signal(barrier, inc=1, device_id=where, device_id_type=MESH)

    @pl.loop(1, NZ)
    def _(k):
        greet(dev(x, ((z + k) & (NZ - 1)), y, c))

    @pl.loop(1, NX)
    def _(k):
        greet(dev(((x + k) & (NX - 1)), z, y, c))

    @pl.loop(1, NT)
    def _(k):
        greet({"pair": pair, "tensor": ((ten + k) & (NT - 1))})

    @pl.when(off_diagonal)
    def _():
        greet(dev(y, z, x, c))

    slots = NZ * SLOTS
    j = iota((slots, NX * NZ), 0)
    dest = ((j >> 2) & (NX - 1)) * NZ + (j >> 4)
    other = iota((slots, NX * NZ), 1)
    sending = counts[...].astype(F32)
    start = jnp.sum(jnp.where(other < dest, sending, 0.0), axis=1, keepdims=True)
    amount = jnp.sum(jnp.where(other == dest, sending, 0.0), axis=1, keepdims=True)
    k_slot = (iota((slots, 1), 0) & 3).astype(F32)
    spare = k_slot == CAP
    row_of = iota((slots, ROWS), 1).astype(F32)

    def picking(cond, k):
        return ones_where(jnp.where(cond & (amount > k), start + k, -1.0) == row_of)

    pick = picking(k_slot < CAP, k_slot)
    pick_tail = [picking(spare, float(k)) for k in range(CAP)]
    spot = iota((slots, 128), 1) - TAIL
    flags = jnp.where(
        spare & (spot >= 0) & (spot < CAP) & (spot.astype(F32) < amount), 1.0, 0.0
    )
    low[...] = jnp.zeros((ROWS, 128), BF16)
    loads[0].wait()
    low[:, 0:TAIL] = roll[:, 2 * SIDE:FEAT]
    low_tail = low[...]
    high_tail = pltpu.roll(low_tail.astype(F32), TAIL, 1).astype(BF16)
    base = dot(pick, roll[:, 0:2 * SIDE])
    tile0 = base[:, 0:128] + dot(pick_tail[0], low_tail) + dot(pick_tail[1], high_tail)
    tile1 = base[:, 128:256] + dot(pick_tail[2], low_tail) + flags
    zsend[0] = jnp.concatenate((tile0, tile1), axis=1).astype(BF16).reshape(NZ, SLOTS, SIDE)
    zsend[1] = base[:, SIDE:].astype(BF16).reshape(NZ, SLOTS, SIDE)
    for h in (0, 1):
        zrecv[h, z] = zsend[h, z]

    for load in loads[1:]:
        load.wait()

    def pack(p, first, second):
        wsend[p] = jnp.concatenate(
            (first.astype(F32), second.astype(F32)), axis=0
        ).astype(BF16)

    pack(0, wq[:, :HD], wq[:, HD:])
    pack(1, wk[...], wv[...])
    pack(2, wo[:, :HD], wo[:, HD:])
    lane = iota((8, 128), 1)
    spread = jnp.zeros((8, 128), I32)
    for k in range(RESP):
        spread = jnp.where(lane == k, pslot[0:1, k:k + 1], spread)
    slot_out[...] = spread

    greeted = NZ - 1 + NX - 1 + NT - 1

    @pl.when(off_diagonal)
    def _():
        pl.semaphore_wait(barrier, greeted + 1)

    @pl.when(jnp.logical_not(off_diagonal))
    def _():
        pl.semaphore_wait(barrier, greeted)

    def z_out(h, k):
        t = ((z + k) & (NZ - 1))
        return remote(
            zsend.at[h, t], zrecv.at[h, z], za_s.at[h, k], za_r.at[h, k], dev(x, t, y, c)
        )

    def z_in(h, k):
        f = ((z + NZ - k) & (NZ - 1))
        return remote(
            zsend.at[h, f], zrecv.at[h, f], za_s.at[h, k], za_r.at[h, k], dev(x, f, y, c)
        )

    def turned(p):
        src, dst = (slot_out, slot_in) if p == 3 else (wsend.at[p], wbuf.at[z, p])
        return remote(src, dst, tr_s.at[p], tr_r.at[p], dev(y, z, x, c))

    @pl.when(off_diagonal)
    def _():
        for p in range(4):
            turned(p).start()

    for h in (0, 1):
        z_out(h, NZ // 2).start()

        @pl.loop(1, NZ // 2)
        def _(k):
            z_out(h, NZ // 2 - k).start()
            z_out(h, NZ // 2 + k).start()

    @pl.when(jnp.logical_not(off_diagonal))
    def _():
        wbuf[z] = wsend[...]
        slot_in[...] = slot_out[...]

    up, down = ((z + 1) & (NZ - 1)), ((z + NZ - 1) & (NZ - 1))

    def ring_block(d, s):
        return ((z + NZ - s) & (NZ - 1)) if d == 1 else ((z + s) & (NZ - 1))

    def ring(p, d, s, distance):
        block = wbuf.at[ring_block(d, distance), p]
        return remote(
            block, block, ring_s.at[p, d, s], ring_r.at[p, d, s],
            dev(x, up if d == 1 else down, y, c),
        )

    def unpack(p, block):
        v = wbuf[block, p].astype(F32)
        at = pl.ds(pl.multiple_of(block * WROWS, 8), WROWS)
        w32[p, at, 0:HD] = v[:WROWS]
        w32[p, at, HD:2 * HD] = v[WROWS:]

    def ring_steps(pieces, low, high):
        @pl.loop(low, high)
        def _(s):
            for p in pieces:
                for d in (0, 1):
                    ring(p, d, s - 1, s).wait_recv()
                    ring(p, d, s, s).start()
            for p in pieces:
                for d in (0, 1):
                    unpack(p, ring_block(d, s))

    last = NZ // 2

    def ring_last_sends(pieces):
        for p in pieces:
            for d in (0, 1):
                ring(p, d, last - 2, last - 1).wait_recv()
            ring(p, 0, last - 1, last - 1).start()
        for p in pieces:
            for d in (0, 1):
                unpack(p, ring_block(d, last - 1))

    def ring_close(pieces):
        for p in pieces:
            ring(p, 0, last - 1, last).wait_recv()
            unpack(p, ring_block(0, last))

    early, late = (0, 1), (2,)
    for p in (0, 1, 2):
        @pl.when(off_diagonal)
        def _():
            turned(p).wait_recv()

        if p in early:
            ring(p, 0, 0, 0).start()
            ring(p, 1, 0, 0).start()
    for p in (0, 1, 2):
        unpack(p, z)

    @pl.when(off_diagonal)
    def _():
        turned(3).wait_recv()

    ring_steps(early, 1, 2)

    def z_wait(h):
        @pl.loop(1, NZ)
        def _(k):
            z_in(h, k).wait_recv()

    held = (xg0, xg1)

    def x_copy(h, k, block, target):
        ref = held[h].at[block]
        return remote(ref, ref, xg_s.at[h, k], xg_r.at[h, k], dev(target, z, y, c))

    def x_out(h, k):
        return x_copy(h, k, x, (x + k) & (NX - 1))

    def x_in(h, k):
        f = (x + NX - k) & (NX - 1)
        return x_copy(h, k, f, f)

    def x_open(h):
        for k in (2, 1, 3):
            x_out(h, k).start()

    def x_wait(h):
        for k in (1, 3, 2):
            x_in(h, k).wait_recv()

    i = iota((ALL_SLOTS, slots), 0)
    q = (i * 171) >> 9
    at = iota((ALL_SLOTS, slots), 1) - (q & (NZ - 1)) * SLOTS - (q >> 4) * 4
    squeeze = ones_where(at == i - 3 * q)
    squeeze_spare = ones_where(at == CAP)
    i = iota((ALL_SLOTS, 128), 0)
    k_kept = i - 3 * ((i * 171) >> 9)
    lane = iota((ALL_SLOTS, 128), 1)

    z_wait(0)
    got = zrecv[0].reshape(slots, SIDE)
    spare_rows = dot(squeeze_spare, got)
    first, second = spare_rows[:, 0:128], spare_rows[:, 128:256]
    tail = jnp.where(
        k_kept == 0, first, jnp.where(k_kept == 1, pltpu.roll(first, TAIL, 1), second)
    )
    flag = jnp.sum(jnp.where(lane == TAIL + k_kept, second, 0.0), axis=1, keepdims=True)
    tail = jnp.where(lane < TAIL, tail, flag)
    xg0[x] = jnp.concatenate((dot(squeeze, got), tail), axis=1).astype(BF16)
    x_open(0)
    ring_steps(early, 2, 3)
    ring_steps(early, 3, 4)
    z_wait(1)
    xg1[x] = dot(squeeze, zrecv[1].reshape(slots, SIDE)).astype(BF16)
    x_open(1)
    ring_steps(early, 4, 5)
    for d in (0, 1):
        ring(2, d, 0, 0).start()
    x_wait(0)

    before = ones_where(iota((ALL_SLOTS, ALL_SLOTS), 0) < iota((ALL_SLOTS, ALL_SLOTS), 1))
    flag_lane = ones_where(iota((16, 128), 1) == TAIL)
    my_gain = gain[pl.ds(pl.multiple_of(y * NC * FEAT, 128), NC * FEAT)].reshape(1, NC * FEAT)
    my_gain = jnp.where(c == 0, my_gain[:, :FEAT], my_gain[:, FEAT:])
    table = jnp.zeros((8, 128), F32)
    sub = iota((8, 128), 0)

    def share(dx):
        return remote(
            xs.at[c, dx], xs.at[c, dx], cs_s.at[dx], cs_r.at[dx], dev(x, z, y, 1 - c)
        )

    def share_in(dx):
        return remote(
            xs.at[1 - c, dx], xs.at[1 - c, dx], cs_s.at[dx], cs_r.at[dx], dev(x, z, y, 1 - c)
        )

    def keep(dx, low_column, rows):
        high_column = low_column + rows.shape[1]
        judged[dx, :, low_column:high_column] = rows.astype(BF16)
        xs[c, dx, :, low_column:high_column] = (
            rows * my_gain[:, low_column:high_column]
        ).astype(BF16)
        return jnp.sum(rows * rows, axis=1, keepdims=True)

    places, sums = [], []
    for dx in range(NX):
        s = xg0[:, dx * KEPT:(dx + 1) * KEPT, :].reshape(ALL_SLOTS, WIDE)
        filled = dot(flag_lane, s[:, SIDE:WIDE], NTR)
        rank = dot(filled.astype(BF16), before)
        key = jnp.where(filled > 0.5, rank, -1.0)[0:1]
        place = ones_where(iota((ROWS, ALL_SLOTS), 0).astype(F32) == key)
        rows = dot(place, s)
        places.append(place)
        sums.append(
            keep(dx, 0, rows[:, 0:SIDE]) + keep(dx, 2 * SIDE, rows[:, SIDE:SIDE + TAIL])
        )
        if dx == 1:
            ring_steps(early, 5, 6)
            ring_steps(late, 1, 2)

    ring_steps(early, 6, last - 1)
    ring_steps(late, 2, 3)
    x_wait(1)
    for dx in range(NX):
        s = xg1[:, dx * KEPT:(dx + 1) * KEPT, :].reshape(ALL_SLOTS, SIDE)
        total = sums[dx] + keep(dx, SIDE, dot(places[dx], s))
        share(dx).start()
        table = jnp.where(sub == dx, column_to_row(total), table)
        if dx == 1:
            ring_last_sends(early)
            ring_steps(late, 3, 4)

    sq_in[0] = table

    def squares_out(k):
        return remote(
            sq_in.at[0], sq_in.at[k], sq_s.at[k], sq_r.at[k],
            {"pair": pair, "tensor": ((ten + k) & (NT - 1))},
        )

    @pl.loop(1, NT)
    def _(k):
        squares_out(k).start()

    ring_close(early)
    for dx in range(NX):
        share_in(dx).wait_recv()

    first = xs[0].reshape(NX * ROWS, FEAT)
    second = xs[1].reshape(NX * ROWS, FEAT)
    def products(p):
        w = w32[p].astype(BF16)
        t = dot(first, w[:FEAT]) + dot(second, w[FEAT:])
        return t.astype(BF16).reshape(NX, ROWS, 256)

    def sum_out(n, k):
        t = ((y + k) & (NY - 1))
        src = (part.at[1, t], part.at[1, ((t + NY // 2) & (NY - 1))], part.at[0, t])[n]
        return remote(
            src, part_in.at[n, k], rs_s.at[n, k], rs_r.at[n, k], dev(x, z, t, c)
        )

    part[1] = products(1)
    for k in (2, 1, 3):
        sum_out(0, k).start()
    part[0] = products(0)
    for n in (2, 1):
        for k in (2, 1, 3):
            sum_out(n, k).start()

    ring_steps(late, 4, last - 1)

    @pl.when(off_diagonal)
    def _():
        for p in range(4):
            turned(p).wait_send()

    for h in (0, 1):
        @pl.loop(1, NZ)
        def _(k):
            z_out(h, k).wait_send()

    def ring_left(p):
        @pl.loop(0, last - 1)
        def _(s):
            ring(p, 0, s, s).wait_send()
            ring(p, 1, s, s).wait_send()

        ring(p, 0, last - 1, last - 1).wait_send()

    for p in early:
        ring_left(p)
    for h in (0, 1):
        for k in range(1, NX):
            x_out(h, k).wait_send()
    for dx in range(NX):
        share(dx).wait_send()

    @pl.loop(1, NT)
    def _(k):
        squares_out(k).wait_send()

    @pl.loop(1, NT)
    def _(k):
        squares_out(k).wait_recv()

    total = sq_in[0]
    for k in range(1, NT):
        total = total + sq_in[k]
    far_y = ((y + NY // 2) & (NY - 1))
    width = float(NT * FEAT)

    def row_scale(which):
        row = jnp.sum(jnp.where(sub == which, total, 0.0), axis=0, keepdims=True)
        return lax.rsqrt(row_to_column(row, ROWS) / width + epsilon)

    scale_own, scale_far = row_scale(y), row_scale(far_y)
    def summed(n, mine, scale):
        for k in range(1, NY):
            sum_out(n, k).wait_recv()
        t = mine.astype(F32)
        for k in range(1, NY):
            t = t + part_in[n, k].astype(F32)
        return (t * scale).astype(BF16)

    kv = summed(0, part[1, y], scale_own)
    q_own = summed(2, part[0, y], scale_own)

    queries = jnp.concatenate((q_own[:, 0:HD], q_own[:, HD:2 * HD]), axis=0)
    col = iota((2 * ROWS, ROWS), 1)
    row = iota((2 * ROWS, ROWS), 0)
    row = jnp.where(row >= ROWS, row - ROWS, row)
    resp_q, resp_k = row >> 5, col >> 5
    spot_q, spot_k = row & (LEN - 1), col & (LEN - 1)

    def by_response(resp, values):
        return jnp.where(resp == 0, values[0], jnp.where(resp == 1, values[1], values[2]))

    own_lens = [lens[(y * NZ + z) * RESP + k] for k in range(RESP)]
    far_lens = [lens[(far_y * NZ + z) * RESP + k] for k in range(RESP)]
    partner = by_response(resp_q, [slot_in[0:1, k:k + 1] for k in range(RESP)])
    own_ok = (resp_q == resp_k) & (spot_k <= spot_q) & (spot_k < by_response(resp_k, own_lens))
    far_ok = (partner == resp_k) & (spot_k < by_response(resp_k, far_lens))

    def powers(keys, ok):
        scores = dot(queries, keys, NTR) * score_scale
        scores = soft_cap * jnp.tanh(scores / soft_cap)
        return jnp.exp(jnp.where(ok, scores, negative))

    def weigh(keys_values, ok):
        p = powers(keys_values[:, 0:HD], ok)
        return jnp.sum(p, axis=1, keepdims=True), dot(p.astype(BF16), keys_values[:, HD:2 * HD])

    whole, mixed = weigh(kv, own_ok)
    ring_last_sends(late)
    far_whole, far_mixed = weigh(summed(1, part[1, far_y], scale_far), far_ok)
    mixed = (mixed + far_mixed) / (whole + far_whole)
    row = iota((2 * ROWS, HD), 0)
    row = jnp.where(row >= ROWS, row - ROWS, row)
    present = (row & (LEN - 1)) < by_response(row >> 5, own_lens)
    mixed = jnp.where(present, mixed, 0.0).astype(BF16)
    ctx[y] = jnp.concatenate((mixed[:ROWS], mixed[ROWS:]), axis=1)

    def ctx_out(k):
        return remote(ctx.at[y], ctx.at[y], cx_s.at[k], cx_r.at[k], dev(x, z, ((y + k) & (NY - 1)), c))

    def ctx_in(k):
        f = ((y + NY - k) & (NY - 1))
        return remote(ctx.at[f], ctx.at[f], cx_s.at[k], cx_r.at[k], dev(x, z, f, c))

    for k in (2, 1, 3):
        ctx_out(k).start()
    ring_close(late)

    def out_rows(half):
        return w32[2, pl.ds(pl.multiple_of(half * FEAT, 8), FEAT), :].astype(BF16)

    w_other, w_mine = out_rows(1 - c), out_rows(c)

    def swap(k):
        t = ((y + NY - k) & (NY - 1))
        return remote(
            co_out.at[t], co_in.at[t], co_s.at[k], co_r.at[k], dev(x, z, y, 1 - c)
        )

    def xsum(k):
        t = ((x + k) & (NX - 1))
        return remote(xo_out.at[t], xo_in.at[k], xo_s.at[k], xo_r.at[k], dev(t, z, y, c))

    order = (0, 1, 3, 2)
    for k in order:
        t = ((y + NY - k) & (NY - 1))
        if k > 0:
            ctx_in(k).wait_recv()
        co_out[t] = dot(ctx[t], w_other, NTR).astype(BF16)
        swap(k).start()
        xo_out[t] = dot(ctx[t], w_mine, NTR).astype(BF16)
    for k in order:
        t = ((y + NY - k) & (NY - 1))
        swap(k).wait_recv()
        xo_out[t] = (xo_out[t].astype(F32) + co_in[t].astype(F32)).astype(BF16)

        @pl.when(t != x)
        def _():
            xsum(((t + NX - x) & (NX - 1))).start()

    attended = xo_out[x].astype(F32)
    for k in (1, 3, 2):
        xsum(k).wait_recv()
        attended = attended + xo_in[k].astype(F32)

    squares = column_to_row(jnp.sum(attended * attended, axis=1, keepdims=True))
    fin_in[0] = jnp.where(sub == 0, squares, 0.0)

    def fin_out(k):
        return remote(
            fin_in.at[0], fin_in.at[k], fn_s.at[k], fn_r.at[k],
            {"pair": pair, "tensor": ((ten + k) & (NT - 1))},
        )

    @pl.loop(1, NT)
    def _(k):
        fin_out(k).start()

    ring_left(2)
    for k in range(1, NY):
        for n in range(3):
            sum_out(n, k).wait_send()
        ctx_out(k).wait_send()
        xsum(k).wait_send()
    for k in order:
        swap(k).wait_send()

    residual = judged[x].astype(F32)
    gained = attended * post[...].reshape(1, FEAT)

    @pl.loop(1, NT)
    def _(k):
        fin_out(k).wait_recv()

    total = fin_in[0]
    for k in range(1, NT):
        total = total + fin_in[k]
    scale = lax.rsqrt(row_to_column(total[0:1], ROWS) / width + epsilon)
    out[...] = (residual + gained * scale).astype(BF16)

    @pl.loop(1, NT)
    def _(k):
        fin_out(k).wait_send()


def shards(
    rollout, counts, lengths, partner_slot, pre_gain, post_gain,
    query_weight, key_weight, value_weight, out_weight,
):
    vmem = pl.BlockSpec(memory_space=pltpu.VMEM)
    hbm = pl.BlockSpec(memory_space=pltpu.HBM)
    smem = pl.BlockSpec(memory_space=pltpu.SMEM)
    dma = pltpu.SemaphoreType.DMA
    scratch = [
        pltpu.VMEM((ROWS, FEAT), BF16),
        pltpu.VMEM((WROWS, 256), BF16),
        pltpu.VMEM((WROWS, HD), BF16),
        pltpu.VMEM((WROWS, HD), BF16),
        pltpu.VMEM((WROWS, 256), BF16),
        dma((5,)),
        pltpu.VMEM((ROWS, 128), BF16),
        pltpu.VMEM((2, NZ, SLOTS, SIDE), BF16),
        pltpu.VMEM((2, NZ, SLOTS, SIDE), BF16),
        pltpu.VMEM((3, 2 * WROWS, HD), BF16),
        pltpu.VMEM((NZ, 3, 2 * WROWS, HD), BF16),
        pltpu.VMEM((3, BLOCK, 2 * HD), F32),
        pltpu.VMEM((8, 128), I32),
        pltpu.VMEM((8, 128), I32),
        pltpu.VMEM((NX, ALL_SLOTS, WIDE), BF16),
        pltpu.VMEM((NX, ALL_SLOTS, SIDE), BF16),
        pltpu.VMEM((NC, NX, ROWS, FEAT), BF16),
        pltpu.VMEM((NX, ROWS, FEAT), BF16),
        pltpu.VMEM((NT, 8, 128), F32),
        pltpu.VMEM((NT, 8, 128), F32),
        pltpu.VMEM((2, NX, ROWS, 256), BF16),
        pltpu.VMEM((3, NY, ROWS, 256), BF16),
        pltpu.VMEM((NY, ROWS, 256), BF16),
        pltpu.VMEM((NX, ROWS, FEAT), BF16),
        pltpu.VMEM((NX, ROWS, FEAT), BF16),
        pltpu.VMEM((NX, ROWS, FEAT), BF16),
        pltpu.VMEM((NX, ROWS, FEAT), BF16),
        dma((4,)), dma((4,)),
        dma((2, NZ)), dma((2, NZ)),
        dma((3, 2, NZ // 2)), dma((3, 2, NZ // 2)),
        dma((2, NX)), dma((2, NX)),
        dma((NX,)), dma((NX,)),
        dma((NT,)), dma((NT,)),
        dma((3, NY)), dma((3, NY)),
        dma((NY,)), dma((NY,)),
        dma((NX,)), dma((NX,)),
        dma((NX,)), dma((NX,)),
        dma((NT,)), dma((NT,)),
    ]
    return pl.pallas_call(
        kernel,
        out_shape=jax.ShapeDtypeStruct((ROWS, FEAT), BF16),
        in_specs=[hbm, vmem, smem, vmem, vmem, vmem, hbm, hbm, hbm, hbm],
        out_specs=vmem,
        scratch_shapes=scratch,
        compiler_params=pltpu.CompilerParams(
            collective_id=0, has_side_effects=True, vmem_limit_bytes=62 * 1024 * 1024
        ),
    )(
        rollout, counts, lengths, partner_slot, pre_gain,
        post_gain, query_weight, key_weight, value_weight, out_weight,
    )


def solution(mesh):
    placed = (
        P("pair", "tensor"),
        P("pair", None),
        P(),
        P("pair", None),
        P(),
        P("tensor"),
        P("pair", "tensor"),
        P("pair", "tensor"),
        P("pair", "tensor"),
        P("pair", "tensor"),
    )
    return jax.shard_map(
        shards, mesh=mesh, in_specs=placed, out_specs=P("pair", "tensor"), check_vma=False
    )
```

```python
import jax
import jax.numpy as jnp
from jax import lax
from jax.experimental import pallas as pl
from jax.experimental.pallas import tpu as pltpu
from jax.sharding import PartitionSpec as P

NX, NY, NZ, NC = 4, 4, 16, 2
NT = NY * NC
HD = 128
LEN = 32
RESP = 3
ROWS = RESP * LEN
FEAT = 576
SIDE = 256
TAIL = FEAT - 2 * SIDE
WIDE = SIDE + 128
WROWS = 72
BLOCK = NZ * WROWS
CAP = 3
SLOTS = NX * 4
KEPT = NZ * CAP
ALL_SLOTS = NX * KEPT

score_scale = 144.0 ** (-0.5)
soft_cap = 50.0
epsilon = 1e-06
negative = -1e30

F32 = jnp.float32
BF16 = jnp.bfloat16
I32 = jnp.int32
MESH = pl.DeviceIdType.MESH
NN = (((1,), (0,)), ((), ()))
NTR = (((1,), (1,)), ((), ()))


def dot(a, b, dims=NN):
    return lax.dot_general(a, b, dims, preferred_element_type=F32)


def iota(shape, dim):
    return lax.broadcasted_iota(I32, shape, dim)


def ones_where(cond):
    return jnp.where(cond, 1.0, 0.0).astype(BF16)


def column_to_row(col):
    rows = col.shape[0]
    same = iota((rows, 128), 0) == iota((rows, 128), 1)
    return jnp.sum(jnp.where(same, col, 0.0), axis=0, keepdims=True)


def row_to_column(row, rows):
    same = iota((rows, 128), 0) == iota((rows, 128), 1)
    return jnp.sum(jnp.where(same, row, 0.0), axis=1, keepdims=True)


def kernel(
    roll_h, counts, lens, pslot, gain, post, wq_h, wk_h, wv_h, wo_h, out,
    roll, wq, wk, wv, wo, in_s, low, zsend, zrecv, wsend, wbuf, w32, slot_out, slot_in, xg0, xg1, xs, judged, sq_in, fin_in,
    part, part_in, ctx, co_out, co_in, xo_out, xo_in,
    tr_s, tr_r, za_s, za_r, ring_s, ring_r, xg_s, xg_r, cs_s, cs_r, sq_s, sq_r,
    rs_s, rs_r, cx_s, cx_r, co_s, co_r, xo_s, xo_r, fn_s, fn_r,
):
    pair = lax.axis_index("pair")
    ten = lax.axis_index("tensor")
    x, z = pair >> 4, pair & (NZ - 1)
    y, c = ten >> 1, ten & (NC - 1)

    def dev(xx, zz, yy, cc):
        return {"pair": xx * NZ + zz, "tensor": yy * NC + cc}

    def remote(src, dst, send, recv, where):
        return pltpu.make_async_remote_copy(
            src_ref=src, dst_ref=dst, send_sem=send, recv_sem=recv,
            device_id=where, device_id_type=MESH,
        )

    off_diagonal = x != y

    loads = [
        pltpu.make_async_copy(a, b, in_s.at[n])
        for n, (a, b) in enumerate(
            ((roll_h, roll), (wq_h, wq), (wk_h, wk), (wv_h, wv), (wo_h, wo))
        )
    ]
    for load in loads:
        load.start()

    barrier = pltpu.get_barrier_semaphore()

    def greet(where):
        pl.semaphore_signal(barrier, inc=1, device_id=where, device_id_type=MESH)

    @pl.loop(1, NZ)
    def _(k):
        greet(dev(x, ((z + k) & (NZ - 1)), y, c))

    @pl.loop(1, NX)
    def _(k):
        greet(dev(((x + k) & (NX - 1)), z, y, c))

    @pl.loop(1, NT)
    def _(k):
        greet({"pair": pair, "tensor": ((ten + k) & (NT - 1))})

    @pl.when(off_diagonal)
    def _():
        greet(dev(y, z, x, c))

    slots = NZ * SLOTS
    j = iota((slots, NX * NZ), 0)
    dest = ((j >> 2) & (NX - 1)) * NZ + (j >> 4)
    other = iota((slots, NX * NZ), 1)
    sending = counts[...].astype(F32)
    start = jnp.sum(jnp.where(other < dest, sending, 0.0), axis=1, keepdims=True)
    amount = jnp.sum(jnp.where(other == dest, sending, 0.0), axis=1, keepdims=True)
    k_slot = (iota((slots, 1), 0) & 3).astype(F32)
    spare = k_slot == CAP
    row_of = iota((slots, ROWS), 1).astype(F32)

    def picking(cond, k):
        return ones_where(jnp.where(cond & (amount > k), start + k, -1.0) == row_of)

    pick = picking(k_slot < CAP, k_slot)
    pick_tail = [picking(spare, float(k)) for k in range(CAP)]
    spot = iota((slots, 128), 1) - TAIL
    flags = jnp.where(
        spare & (spot >= 0) & (spot < CAP) & (spot.astype(F32) < amount), 1.0, 0.0
    )
    low[...] = jnp.zeros((ROWS, 128), BF16)
    loads[0].wait()
    low[:, 0:TAIL] = roll[:, 2 * SIDE:FEAT]
    low_tail = low[...]
    high_tail = pltpu.roll(low_tail.astype(F32), TAIL, 1).astype(BF16)
    base = dot(pick, roll[:, 0:2 * SIDE])
    tile0 = base[:, 0:128] + dot(pick_tail[0], low_tail) + dot(pick_tail[1], high_tail)
    tile1 = base[:, 128:256] + dot(pick_tail[2], low_tail) + flags
    zsend[0] = jnp.concatenate((tile0, tile1), axis=1).astype(BF16).reshape(NZ, SLOTS, SIDE)
    zsend[1] = base[:, SIDE:].astype(BF16).reshape(NZ, SLOTS, SIDE)
    for h in (0, 1):
        zrecv[h, z] = zsend[h, z]

    for load in loads[1:]:
        load.wait()

    def pack(p, first, second):
        wsend[p] = jnp.concatenate(
            (first.astype(F32), second.astype(F32)), axis=0
        ).astype(BF16)

    pack(0, wq[:, :HD], wq[:, HD:])
    pack(1, wk[...], wv[...])
    pack(2, wo[:, :HD], wo[:, HD:])
    lane = iota((8, 128), 1)
    spread = jnp.zeros((8, 128), I32)
    for k in range(RESP):
        spread = jnp.where(lane == k, pslot[0:1, k:k + 1], spread)
    slot_out[...] = spread

    greeted = NZ - 1 + NX - 1 + NT - 1

    @pl.when(off_diagonal)
    def _():
        pl.semaphore_wait(barrier, greeted + 1)

    @pl.when(jnp.logical_not(off_diagonal))
    def _():
        pl.semaphore_wait(barrier, greeted)

    def z_out(h, k):
        t = ((z + k) & (NZ - 1))
        return remote(
            zsend.at[h, t], zrecv.at[h, z], za_s.at[h, k], za_r.at[h, k], dev(x, t, y, c)
        )

    def z_in(h, k):
        f = ((z + NZ - k) & (NZ - 1))
        return remote(
            zsend.at[h, f], zrecv.at[h, f], za_s.at[h, k], za_r.at[h, k], dev(x, f, y, c)
        )

    def turned(p):
        src, dst = (slot_out, slot_in) if p == 3 else (wsend.at[p], wbuf.at[z, p])
        return remote(src, dst, tr_s.at[p], tr_r.at[p], dev(y, z, x, c))

    @pl.when(off_diagonal)
    def _():
        for p in range(4):
            turned(p).start()

    for h in (0, 1):
        z_out(h, NZ // 2).start()

        @pl.loop(1, NZ // 2)
        def _(k):
            z_out(h, NZ // 2 - k).start()
            z_out(h, NZ // 2 + k).start()

    @pl.when(jnp.logical_not(off_diagonal))
    def _():
        wbuf[z] = wsend[...]
        slot_in[...] = slot_out[...]

    up, down = ((z + 1) & (NZ - 1)), ((z + NZ - 1) & (NZ - 1))

    def ring_block(d, s):
        return ((z + NZ - s) & (NZ - 1)) if d == 1 else ((z + s) & (NZ - 1))

    def ring(p, d, s, distance):
        block = wbuf.at[ring_block(d, distance), p]
        return remote(
            block, block, ring_s.at[p, d, s], ring_r.at[p, d, s],
            dev(x, up if d == 1 else down, y, c),
        )

    def unpack(p, block):
        v = wbuf[block, p].astype(F32)
        at = pl.ds(pl.multiple_of(block * WROWS, 8), WROWS)
        w32[p, at, 0:HD] = v[:WROWS]
        w32[p, at, HD:2 * HD] = v[WROWS:]

    def ring_steps(pieces, low, high):
        @pl.loop(low, high)
        def _(s):
            for p in pieces:
                for d in (0, 1):
                    ring(p, d, s - 1, s).wait_recv()
                    ring(p, d, s, s).start()
            for p in pieces:
                for d in (0, 1):
                    unpack(p, ring_block(d, s))

    last = NZ // 2

    def ring_last_sends(pieces):
        for p in pieces:
            for d in (0, 1):
                ring(p, d, last - 2, last - 1).wait_recv()
            ring(p, 0, last - 1, last - 1).start()
        for p in pieces:
            for d in (0, 1):
                unpack(p, ring_block(d, last - 1))

    def ring_close(pieces):
        for p in pieces:
            ring(p, 0, last - 1, last).wait_recv()
            unpack(p, ring_block(0, last))

    early, late = (0, 1), (2,)
    for p in (0, 1, 2):
        @pl.when(off_diagonal)
        def _():
            turned(p).wait_recv()

        if p in early:
            ring(p, 0, 0, 0).start()
            ring(p, 1, 0, 0).start()
    for p in (0, 1, 2):
        unpack(p, z)

    @pl.when(off_diagonal)
    def _():
        turned(3).wait_recv()

    ring_steps(early, 1, 2)
    for d in (0, 1):
        ring(2, d, 0, 0).start()

    def z_wait(h):
        @pl.loop(1, NZ)
        def _(k):
            z_in(h, k).wait_recv()

    held = (xg0, xg1)

    def x_copy(h, k, block, target):
        ref = held[h].at[block]
        return remote(ref, ref, xg_s.at[h, k], xg_r.at[h, k], dev(target, z, y, c))

    def x_out(h, k):
        return x_copy(h, k, x, (x + k) & (NX - 1))

    def x_in(h, k):
        f = (x + NX - k) & (NX - 1)
        return x_copy(h, k, f, f)

    def x_open(h):
        for k in (2, 1, 3):
            x_out(h, k).start()

    def x_wait(h):
        for k in (1, 3, 2):
            x_in(h, k).wait_recv()

    i = iota((ALL_SLOTS, slots), 0)
    q = (i * 171) >> 9
    at = iota((ALL_SLOTS, slots), 1) - (q & (NZ - 1)) * SLOTS - (q >> 4) * 4
    squeeze = ones_where(at == i - 3 * q)
    squeeze_spare = ones_where(at == CAP)
    i = iota((ALL_SLOTS, 128), 0)
    k_kept = i - 3 * ((i * 171) >> 9)
    lane = iota((ALL_SLOTS, 128), 1)

    z_wait(0)
    got = zrecv[0].reshape(slots, SIDE)
    spare_rows = dot(squeeze_spare, got)
    first, second = spare_rows[:, 0:128], spare_rows[:, 128:256]
    tail = jnp.where(
        k_kept == 0, first, jnp.where(k_kept == 1, pltpu.roll(first, TAIL, 1), second)
    )
    flag = jnp.sum(jnp.where(lane == TAIL + k_kept, second, 0.0), axis=1, keepdims=True)
    tail = jnp.where(lane < TAIL, tail, flag)
    xg0[x] = jnp.concatenate((dot(squeeze, got), tail), axis=1).astype(BF16)
    x_open(0)
    ring_steps(early, 2, 3)
    ring_steps(early, 3, 4)
    ring_steps(late, 1, 2)
    z_wait(1)
    xg1[x] = dot(squeeze, zrecv[1].reshape(slots, SIDE)).astype(BF16)
    x_open(1)
    ring_steps(early, 4, 5)
    ring_steps(late, 2, 3)
    x_wait(0)

    before = ones_where(iota((ALL_SLOTS, ALL_SLOTS), 0) < iota((ALL_SLOTS, ALL_SLOTS), 1))
    flag_lane = ones_where(iota((16, 128), 1) == TAIL)
    my_gain = gain[pl.ds(pl.multiple_of(y * NC * FEAT, 128), NC * FEAT)].reshape(1, NC * FEAT)
    my_gain = jnp.where(c == 0, my_gain[:, :FEAT], my_gain[:, FEAT:])
    table = jnp.zeros((8, 128), F32)
    sub = iota((8, 128), 0)

    def share(dx):
        return remote(
            xs.at[c, dx], xs.at[c, dx], cs_s.at[dx], cs_r.at[dx], dev(x, z, y, 1 - c)
        )

    def share_in(dx):
        return remote(
            xs.at[1 - c, dx], xs.at[1 - c, dx], cs_s.at[dx], cs_r.at[dx], dev(x, z, y, 1 - c)
        )

    def keep(dx, low_column, rows):
        high_column = low_column + rows.shape[1]
        judged[dx, :, low_column:high_column] = rows.astype(BF16)
        xs[c, dx, :, low_column:high_column] = (
            rows * my_gain[:, low_column:high_column]
        ).astype(BF16)
        return jnp.sum(rows * rows, axis=1, keepdims=True)

    places, sums = [], []
    for dx in range(NX):
        s = xg0[:, dx * KEPT:(dx + 1) * KEPT, :].reshape(ALL_SLOTS, WIDE)
        filled = dot(flag_lane, s[:, SIDE:WIDE], NTR)
        rank = dot(filled.astype(BF16), before)
        key = jnp.where(filled > 0.5, rank, -1.0)[0:1]
        place = ones_where(iota((ROWS, ALL_SLOTS), 0).astype(F32) == key)
        rows = dot(place, s)
        places.append(place)
        sums.append(
            keep(dx, 0, rows[:, 0:SIDE]) + keep(dx, 2 * SIDE, rows[:, SIDE:SIDE + TAIL])
        )
        if dx == 1:
            ring_steps(early, 5, 6)
            ring_steps(late, 3, 4)

    ring_steps(early, 6, last - 1)
    ring_steps(late, 4, 5)
    x_wait(1)
    for dx in range(NX):
        s = xg1[:, dx * KEPT:(dx + 1) * KEPT, :].reshape(ALL_SLOTS, SIDE)
        total = sums[dx] + keep(dx, SIDE, dot(places[dx], s))
        share(dx).start()
        table = jnp.where(sub == dx, column_to_row(total), table)
        if dx == 1:
            ring_last_sends(early)
            ring_steps(late, 5, 6)

    sq_in[0] = table

    def squares_out(k):
        return remote(
            sq_in.at[0], sq_in.at[k], sq_s.at[k], sq_r.at[k],
            {"pair": pair, "tensor": ((ten + k) & (NT - 1))},
        )

    @pl.loop(1, NT)
    def _(k):
        squares_out(k).start()

    ring_close(early)
    for dx in range(NX):
        share_in(dx).wait_recv()

    first = xs[0].reshape(NX * ROWS, FEAT)
    second = xs[1].reshape(NX * ROWS, FEAT)
    def products(p):
        w = w32[p].astype(BF16)
        t = dot(first, w[:FEAT]) + dot(second, w[FEAT:])
        return t.astype(BF16).reshape(NX, ROWS, 256)

    def sum_out(n, k):
        t = ((y + k) & (NY - 1))
        src = (part.at[1, t], part.at[1, ((t + NY // 2) & (NY - 1))], part.at[0, t])[n]
        return remote(
            src, part_in.at[n, k], rs_s.at[n, k], rs_r.at[n, k], dev(x, z, t, c)
        )

    part[1] = products(1)
    for k in (2, 1, 3):
        sum_out(0, k).start()
    part[0] = products(0)
    for n in (2, 1):
        for k in (2, 1, 3):
            sum_out(n, k).start()

    ring_steps(late, 6, last - 1)

    @pl.when(off_diagonal)
    def _():
        for p in range(4):
            turned(p).wait_send()

    for h in (0, 1):
        @pl.loop(1, NZ)
        def _(k):
            z_out(h, k).wait_send()

    def ring_left(p):
        @pl.loop(0, last - 1)
        def _(s):
            ring(p, 0, s, s).wait_send()
            ring(p, 1, s, s).wait_send()

        ring(p, 0, last - 1, last - 1).wait_send()

    for p in early:
        ring_left(p)
    for h in (0, 1):
        for k in range(1, NX):
            x_out(h, k).wait_send()
    for dx in range(NX):
        share(dx).wait_send()

    @pl.loop(1, NT)
    def _(k):
        squares_out(k).wait_send()

    @pl.loop(1, NT)
    def _(k):
        squares_out(k).wait_recv()

    total = sq_in[0]
    for k in range(1, NT):
        total = total + sq_in[k]
    far_y = ((y + NY // 2) & (NY - 1))
    width = float(NT * FEAT)

    def row_scale(which):
        row = jnp.sum(jnp.where(sub == which, total, 0.0), axis=0, keepdims=True)
        return lax.rsqrt(row_to_column(row, ROWS) / width + epsilon)

    scale_own, scale_far = row_scale(y), row_scale(far_y)
    def summed(n, mine, scale):
        for k in range(1, NY):
            sum_out(n, k).wait_recv()
        t = mine.astype(F32)
        for k in range(1, NY):
            t = t + part_in[n, k].astype(F32)
        return (t * scale).astype(BF16)

    kv = summed(0, part[1, y], scale_own)
    q_own = summed(2, part[0, y], scale_own)

    queries = jnp.concatenate((q_own[:, 0:HD], q_own[:, HD:2 * HD]), axis=0)
    col = iota((2 * ROWS, ROWS), 1)
    row = iota((2 * ROWS, ROWS), 0)
    row = jnp.where(row >= ROWS, row - ROWS, row)
    resp_q, resp_k = row >> 5, col >> 5
    spot_q, spot_k = row & (LEN - 1), col & (LEN - 1)

    def by_response(resp, values):
        return jnp.where(resp == 0, values[0], jnp.where(resp == 1, values[1], values[2]))

    own_lens = [lens[(y * NZ + z) * RESP + k] for k in range(RESP)]
    far_lens = [lens[(far_y * NZ + z) * RESP + k] for k in range(RESP)]
    partner = by_response(resp_q, [slot_in[0:1, k:k + 1] for k in range(RESP)])
    own_ok = (resp_q == resp_k) & (spot_k <= spot_q) & (spot_k < by_response(resp_k, own_lens))
    far_ok = (partner == resp_k) & (spot_k < by_response(resp_k, far_lens))

    def powers(keys, ok):
        scores = dot(queries, keys, NTR) * score_scale
        scores = soft_cap * jnp.tanh(scores / soft_cap)
        return jnp.exp(jnp.where(ok, scores, negative))

    def weigh(keys_values, ok):
        p = powers(keys_values[:, 0:HD], ok)
        return jnp.sum(p, axis=1, keepdims=True), dot(p.astype(BF16), keys_values[:, HD:2 * HD])

    whole, mixed = weigh(kv, own_ok)
    ring_last_sends(late)
    far_whole, far_mixed = weigh(summed(1, part[1, far_y], scale_far), far_ok)
    mixed = (mixed + far_mixed) / (whole + far_whole)
    row = iota((2 * ROWS, HD), 0)
    row = jnp.where(row >= ROWS, row - ROWS, row)
    present = (row & (LEN - 1)) < by_response(row >> 5, own_lens)
    mixed = jnp.where(present, mixed, 0.0).astype(BF16)
    ctx[y] = jnp.concatenate((mixed[:ROWS], mixed[ROWS:]), axis=1)

    def ctx_out(k):
        return remote(ctx.at[y], ctx.at[y], cx_s.at[k], cx_r.at[k], dev(x, z, ((y + k) & (NY - 1)), c))

    def ctx_in(k):
        f = ((y + NY - k) & (NY - 1))
        return remote(ctx.at[f], ctx.at[f], cx_s.at[k], cx_r.at[k], dev(x, z, f, c))

    for k in (2, 1, 3):
        ctx_out(k).start()
    ring_close(late)

    def out_rows(half):
        return w32[2, pl.ds(pl.multiple_of(half * FEAT, 8), FEAT), :].astype(BF16)

    w_other, w_mine = out_rows(1 - c), out_rows(c)

    def swap(k):
        t = ((y + NY - k) & (NY - 1))
        return remote(
            co_out.at[t], co_in.at[t], co_s.at[k], co_r.at[k], dev(x, z, y, 1 - c)
        )

    def xsum(k):
        t = ((x + k) & (NX - 1))
        return remote(xo_out.at[t], xo_in.at[k], xo_s.at[k], xo_r.at[k], dev(t, z, y, c))

    order = (0, 1, 3, 2)
    for k in order:
        t = ((y + NY - k) & (NY - 1))
        if k > 0:
            ctx_in(k).wait_recv()
        co_out[t] = dot(ctx[t], w_other, NTR).astype(BF16)
        swap(k).start()
        xo_out[t] = dot(ctx[t], w_mine, NTR).astype(BF16)
    for k in order:
        t = ((y + NY - k) & (NY - 1))
        swap(k).wait_recv()
        xo_out[t] = (xo_out[t].astype(F32) + co_in[t].astype(F32)).astype(BF16)

        @pl.when(t != x)
        def _():
            xsum(((t + NX - x) & (NX - 1))).start()

    attended = xo_out[x].astype(F32)
    for k in (1, 3, 2):
        xsum(k).wait_recv()
        attended = attended + xo_in[k].astype(F32)

    squares = column_to_row(jnp.sum(attended * attended, axis=1, keepdims=True))
    fin_in[0] = jnp.where(sub == 0, squares, 0.0)

    def fin_out(k):
        return remote(
            fin_in.at[0], fin_in.at[k], fn_s.at[k], fn_r.at[k],
            {"pair": pair, "tensor": ((ten + k) & (NT - 1))},
        )

    @pl.loop(1, NT)
    def _(k):
        fin_out(k).start()

    ring_left(2)
    for k in range(1, NY):
        for n in range(3):
            sum_out(n, k).wait_send()
        ctx_out(k).wait_send()
        xsum(k).wait_send()
    for k in order:
        swap(k).wait_send()

    residual = judged[x].astype(F32)
    gained = attended * post[...].reshape(1, FEAT)

    @pl.loop(1, NT)
    def _(k):
        fin_out(k).wait_recv()

    total = fin_in[0]
    for k in range(1, NT):
        total = total + fin_in[k]
    scale = lax.rsqrt(row_to_column(total[0:1], ROWS) / width + epsilon)
    out[...] = (residual + gained * scale).astype(BF16)

    @pl.loop(1, NT)
    def _(k):
        fin_out(k).wait_send()


def shards(
    rollout, counts, lengths, partner_slot, pre_gain, post_gain,
    query_weight, key_weight, value_weight, out_weight,
):
    vmem = pl.BlockSpec(memory_space=pltpu.VMEM)
    hbm = pl.BlockSpec(memory_space=pltpu.HBM)
    smem = pl.BlockSpec(memory_space=pltpu.SMEM)
    dma = pltpu.SemaphoreType.DMA
    scratch = [
        pltpu.VMEM((ROWS, FEAT), BF16),
        pltpu.VMEM((WROWS, 256), BF16),
        pltpu.VMEM((WROWS, HD), BF16),
        pltpu.VMEM((WROWS, HD), BF16),
        pltpu.VMEM((WROWS, 256), BF16),
        dma((5,)),
        pltpu.VMEM((ROWS, 128), BF16),
        pltpu.VMEM((2, NZ, SLOTS, SIDE), BF16),
        pltpu.VMEM((2, NZ, SLOTS, SIDE), BF16),
        pltpu.VMEM((3, 2 * WROWS, HD), BF16),
        pltpu.VMEM((NZ, 3, 2 * WROWS, HD), BF16),
        pltpu.VMEM((3, BLOCK, 2 * HD), F32),
        pltpu.VMEM((8, 128), I32),
        pltpu.VMEM((8, 128), I32),
        pltpu.VMEM((NX, ALL_SLOTS, WIDE), BF16),
        pltpu.VMEM((NX, ALL_SLOTS, SIDE), BF16),
        pltpu.VMEM((NC, NX, ROWS, FEAT), BF16),
        pltpu.VMEM((NX, ROWS, FEAT), BF16),
        pltpu.VMEM((NT, 8, 128), F32),
        pltpu.VMEM((NT, 8, 128), F32),
        pltpu.VMEM((2, NX, ROWS, 256), BF16),
        pltpu.VMEM((3, NY, ROWS, 256), BF16),
        pltpu.VMEM((NY, ROWS, 256), BF16),
        pltpu.VMEM((NX, ROWS, FEAT), BF16),
        pltpu.VMEM((NX, ROWS, FEAT), BF16),
        pltpu.VMEM((NX, ROWS, FEAT), BF16),
        pltpu.VMEM((NX, ROWS, FEAT), BF16),
        dma((4,)), dma((4,)),
        dma((2, NZ)), dma((2, NZ)),
        dma((3, 2, NZ // 2)), dma((3, 2, NZ // 2)),
        dma((2, NX)), dma((2, NX)),
        dma((NX,)), dma((NX,)),
        dma((NT,)), dma((NT,)),
        dma((3, NY)), dma((3, NY)),
        dma((NY,)), dma((NY,)),
        dma((NX,)), dma((NX,)),
        dma((NX,)), dma((NX,)),
        dma((NT,)), dma((NT,)),
    ]
    return pl.pallas_call(
        kernel,
        out_shape=jax.ShapeDtypeStruct((ROWS, FEAT), BF16),
        in_specs=[hbm, vmem, smem, vmem, vmem, vmem, hbm, hbm, hbm, hbm],
        out_specs=vmem,
        scratch_shapes=scratch,
        compiler_params=pltpu.CompilerParams(
            collective_id=0, has_side_effects=True, vmem_limit_bytes=62 * 1024 * 1024
        ),
    )(
        rollout, counts, lengths, partner_slot, pre_gain,
        post_gain, query_weight, key_weight, value_weight, out_weight,
    )


def solution(mesh):
    placed = (
        P("pair", "tensor"),
        P("pair", None),
        P(),
        P("pair", None),
        P(),
        P("tensor"),
        P("pair", "tensor"),
        P("pair", "tensor"),
        P("pair", "tensor"),
        P("pair", "tensor"),
    )
    return jax.shard_map(
        shards, mesh=mesh, in_specs=placed, out_specs=P("pair", "tensor"), check_vma=False
    )
```
